128 devices in a mesh: wide: 16 (over z, y_lo, core), narrow: 8 (over x, y_hi).
Axes of the slice: x: 4, y: 4 (y_hi: 2, y_lo: 2; y = y_hi * 2 + y_lo), z: 4, core: 2. Of those that a mesh axis runs over, the one named last changes fastest.
Arguments:
- inputs: bfloat16 [2, 16, 1024, 768], P(None, 'wide', 'narrow'), may hold values from -9 to 9
- lengths: int32 [2, 16], P(None, 'wide'), may hold values from 102 to 1024, as said below
- norm_params: bfloat16 [2, 4, 768], P(None, None, ('wide', 'narrow')), may hold values from -2 to 2.203125, as said below
- attn_in: bfloat16 [2, 768, 2304], P(None, ('wide', 'narrow')), may hold values from -0.21875 to 0.21875
- attn_out: bfloat16 [2, 768, 768], P(None, ('wide', 'narrow')), may hold values from -1.25 to 1.25
- mlp_in: bfloat16 [2, 768, 3072], P(None, 'narrow', 'wide'), may hold values from -0.21875 to 0.21875
- mlp_out: bfloat16 [2, 3072, 768], P(None, 'wide', 'narrow'), may hold values from -0.21875 to 0.21875
- cotangent: bfloat16 [2, 16, 1024, 768], P(None, 'wide', 'narrow'), may hold values from -6 to 6
Outputs:
- outputs: float32 [2, 16, 1024, 768], P(None, 'wide', 'narrow')
- grad_inputs: float32 [2, 16, 1024, 768], P(None, 'wide', 'narrow')
- grad_norm_params: float32 [2, 4, 768], P(None, None, ('wide', 'narrow'))
- grad_attn_in: float32 [2, 768, 2304], P(None, ('wide', 'narrow'))
- grad_attn_out: float32 [2, 768, 768], P(None, ('wide', 'narrow'))
- grad_mlp_in: float32 [2, 768, 3072], P(None, 'narrow', 'wide')
- grad_mlp_out: float32 [2, 3072, 768], P(None, 'wide', 'narrow')
The draws below stay inside these ranges and needn't reach their ends.
Inputs may be any that keep to these rules, and one draw needn't show every extreme that they name: `lengths`: among the 2 clips that share an index of wide, one has 1024 patches; one clip has 102. `norm_params`: rows 0 and 2 of each layer are gains, rows 1 and 3 biases.
All inputs are finite; a program needn't handle non-finite values.
Results may differ from the reference program's by a relative error of at most 0.02.
Values may be sent and summed in bfloat16 or wider, within the bound.
No kernel may reach another device: no remote copies, remote signals or barrier semaphores. Data moves between devices by JAX's collectives and lax.ppermute only.
A program may use at most 256 MiB of HBM per device.

```python
import jax
import jax.numpy as jnp
from jax import lax

D = 768
HEADS = 12
HEAD_DIM = 64
FF = 3072
LAYERS = 2
MICRO = 2
SEQ = 1024
CLIPS_DEV = 1
CLIPS = 16


def draw_lengths(key, part):
    key = jax.random.fold_in(key, 11)
    key_lengths, key_pick = jax.random.split(key)
    drawn = jax.random.randint(key_lengths, (MICRO, CLIPS), SEQ // 10, SEQ + 1)
    groups = CLIPS // CLIPS_DEV
    members = MICRO * CLIPS_DEV
    table = jnp.transpose(drawn.reshape(MICRO, groups, CLIPS_DEV), (1, 0, 2)).reshape(groups, members)
    chosen = jax.random.randint(key_pick, (groups, 1), 0, members)
    member_slot = jnp.arange(members)[None, :]
    table = jnp.where(member_slot == chosen, SEQ, table)
    short_slot = (chosen[0, 0] + 1) % members
    first_group = jnp.arange(groups)[:, None] == 0
    table = jnp.where(first_group & (member_slot == short_slot), SEQ // 10, table)
    table = jnp.transpose(table.reshape(groups, MICRO, CLIPS_DEV), (1, 0, 2)).reshape(MICRO, CLIPS)
    return table.astype(jnp.int32)


def draw_norm_params(key, part):
    key = jax.random.fold_in(key, 23)
    key_gain, key_offset = jax.random.split(key)
    table_shape = (LAYERS, 4, D)
    gains = jnp.exp(jax.random.uniform(key_gain, table_shape, jnp.float32, -0.69, 0.69))
    offsets = jnp.clip(0.5 * jax.random.normal(key_offset, table_shape, jnp.float32), -2.0, 2.0)
    is_gain = (jnp.arange(4) % 2 == 0)[None, :, None]
    return jnp.where(is_gain, gains, offsets).astype(jnp.bfloat16)


def steps_of(own_key, shape, pieces, smallest, top_value):
    def one(dim, blocks):
        steps = jax.random.uniform(jax.random.fold_in(jax.random.fold_in(own_key, 6), dim), (blocks,), jnp.float32, smallest / len(pieces), top_value / len(pieces))
        return jnp.repeat(jnp.exp(steps), shape[dim] // blocks).reshape((-1,) + (1,) * (len(shape) - dim - 1))

    loudness = one(*pieces[0])
    for cut in pieces[1:]:
        loudness = loudness * one(*cut)
    return loudness


def gaussian(key, extent, deviation, most, pieces=(), dtype=jnp.bfloat16):
    array = jax.random.normal(key, extent, jnp.float32) * deviation
    if len(pieces) > 0:
        array = steps_of(key, extent, pieces, -0.22, 0.18) * array
    return jnp.clip(array, min=-most, max=most).astype(dtype)


def setup_inputs(seed: int = 0) -> dict:
    streams_of = jax.random.split(jax.random.key(seed), 9)
    return {
        "inputs": gaussian(streams_of[0], (MICRO, CLIPS, SEQ, D), 1.5, 9.0, ((1, 16), (2, 8))),
        "lengths": draw_lengths(jax.random.fold_in(streams_of[8], 71), 0),
        "norm_params": draw_norm_params(jax.random.fold_in(streams_of[8], 71), 0),
        "attn_in": gaussian(streams_of[3], (LAYERS, D, 3 * D), D ** -0.5, 0.21875, ((1, 128),)),
        "attn_out": gaussian(streams_of[4], (LAYERS, D, D), (D // 32) ** -0.5, 1.25, ((1, 128),)),
        "mlp_in": gaussian(streams_of[5], (LAYERS, D, FF), D ** -0.5, 0.21875, ((1, 8), (2, 16))),
        "mlp_out": gaussian(streams_of[6], (LAYERS, FF, D), (FF // 4) ** -0.5, 0.21875, ((1, 16), (2, 8))),
        "cotangent": gaussian(streams_of[7], (MICRO, CLIPS, SEQ, D), 1.0, 6.0, ((1, 16), (2, 8))),
    }


@jax.custom_vjp
def low(v):
    return lax.optimization_barrier(v.astype(jnp.bfloat16)).astype(jnp.float32)

@jax.custom_vjp
def low_back(v):
    return v

def low_keep(v):
    return (low(v), None)

def low_pass(kept, grad):
    return (grad,)

def back_keep(v):
    return (v, None)

def back_low(kept, grad):
    return (low(grad),)
low.defvjp(low_keep, low_pass)
low_back.defvjp(back_keep, back_low)
EPS = 1e-06
ROOT_HALF = 0.7071067811865476
HIGH = lax.Precision.HIGHEST

def norm_rows(values, gain_row, offset_row):
    average = lax.optimization_barrier(jnp.mean(values, -1, keepdims=True))
    centred = values - average
    spread = lax.optimization_barrier(jnp.mean(centred * centred, -1, keepdims=True))
    return centred * lax.rsqrt(spread + EPS) * gain_row + offset_row

def gelu_exact(values):
    return 0.5 * values * (1.0 + jax.scipy.special.erf(values * ROOT_HALF))

def attend_clip(query_rows, key_rows, value_rows, length):
    key_valid = jnp.arange(SEQ) < length
    query_heads = query_rows.reshape(SEQ, HEADS, HEAD_DIM)
    key_heads = key_rows.reshape(SEQ, HEADS, HEAD_DIM)
    value_heads = value_rows.reshape(SEQ, HEADS, HEAD_DIM)
    scores = jnp.einsum('qhe,khe->hqk', query_heads, key_heads, precision=HIGH) * HEAD_DIM ** (-0.5)
    scores = low_back(scores)
    scores = jnp.where(key_valid[None, None, :], scores, -1e+30)
    row_peak = lax.optimization_barrier(jnp.max(scores, -1, keepdims=True))
    expont = jnp.exp(scores - row_peak)
    attn_probs = low(expont / lax.optimization_barrier(jnp.sum(expont, -1, keepdims=True)))
    mixture = jnp.einsum('hqk,khe->qhe', attn_probs, value_heads, precision=HIGH)
    return mixture.reshape(SEQ, HEADS * HEAD_DIM)

def clip_forward(clip_rows, length, weights):
    norm_table, qkv_weight, proj_weight, first_weight, second_weight = weights
    hidden = clip_rows
    for layer_index in range(LAYERS):
        normed_one = low(norm_rows(hidden, norm_table[layer_index, 0], norm_table[layer_index, 1]))
        projected = jnp.dot(normed_one, qkv_weight[layer_index], precision=HIGH)
        query_rows = low(low_back(projected[:, :D]))
        key_rows = low(low_back(projected[:, D:2 * D]))
        value_rows = low(low_back(projected[:, 2 * D:]))
        attended = low(low_back(attend_clip(query_rows, key_rows, value_rows, length)))
        hidden = hidden + low_back(jnp.dot(attended, proj_weight[layer_index], precision=HIGH))
        normed_two = low(norm_rows(hidden, norm_table[layer_index, 2], norm_table[layer_index, 3]))
        before_act = low_back(jnp.dot(normed_two, first_weight[layer_index], precision=HIGH))
        activated = low(gelu_exact(before_act))
        hidden = hidden + low_back(jnp.dot(activated, second_weight[layer_index], precision=HIGH))
    return hidden

def reference(inputs, lengths, norm_params, attn_in, attn_out, mlp_in, mlp_out, cotangent):
    weights = (norm_params.astype(jnp.float32), attn_in.astype(jnp.float32), attn_out.astype(jnp.float32), mlp_in.astype(jnp.float32), mlp_out.astype(jnp.float32))
    clip_rows = inputs.astype(jnp.float32).reshape(MICRO * CLIPS, SEQ, D)
    clip_lengths = lengths.reshape(MICRO * CLIPS)
    clip_step = jax.checkpoint(clip_forward)

    def forward_all(rows_all, weight_set):
        return lax.map(lambda clip_pair: clip_step(clip_pair[0], clip_pair[1], weight_set), (rows_all, clip_lengths))
    results, pullback = jax.vjp(forward_all, clip_rows, weights)
    grad_rows, grad_weights = pullback(cotangent.astype(jnp.float32).reshape(MICRO * CLIPS, SEQ, D))
    out_shape = (MICRO, CLIPS, SEQ, D)
    return (results.reshape(out_shape), grad_rows.reshape(out_shape), grad_weights[0], grad_weights[1], grad_weights[2], grad_weights[3], grad_weights[4])
```

```python
import functools

import jax
import jax.numpy as jnp
from jax import lax
from jax.experimental import pallas as pl
from jax.experimental.pallas import tpu as pltpu
from jax.sharding import PartitionSpec as P

D = 768
FF = 3072
HEAD_DIM = 64
GROUP = 192
TOKENS = 256
EPS = 1e-06
ROOT_HALF = 0.7071067811865476
INV_ROOT_TWO_PI = 0.3989422804014327
ROW_A = 3200
BF = jnp.bfloat16
F32 = jnp.float32
AXES = ("wide", "narrow")
VMEM_LIMIT = 56 * 1024 * 1024


def index_of(z, y, c, x):
    return ((z * 2 + y % 2) * 2 + c) * 8 + x * 2 + y // 2


def fetch(value, z=0, y=0, c=0, x=0):
    pairs = []
    for tz in range(4):
        for ty in range(4):
            for tc in range(2):
                for tx in range(4):
                    source = index_of((tz + z) % 4, (ty + y) % 4, (tc + c) % 2, (tx + x) % 4)
                    pairs.append((source, index_of(tz, ty, tc, tx)))
    return lax.ppermute(value, AXES, pairs)


def gather_four(value, axis):
    return [value] + [fetch(value, **{axis: k}) for k in (1, 2, 3)]


def reduce_four(blocks, axis):
    total = blocks[0].astype(F32)
    for k in (1, 2, 3):
        total = total + fetch(blocks[k], **{axis: 4 - k}).astype(F32)
    return total


def exchange_four(pieces):
    return [pieces[0]] + [fetch(pieces[4 - k], x=k) for k in (1, 2, 3)]


def dot(left, right, over_left=1, over_right=0):
    return lax.dot_general(
        left, right, (((over_left,), (over_right,)), ((), ())), preferred_element_type=F32
    )


def dot_two(left, right, over_left=1, over_right=0):
    high = left.astype(BF)
    low = (left - high.astype(F32)).astype(BF)
    return dot(high, right, over_left, over_right) + dot(low, right, over_left, over_right)


def normed(values):
    average = jnp.mean(values, -1, keepdims=True)
    centred = values - average
    spread = jnp.mean(centred * centred, -1, keepdims=True)
    scale = lax.rsqrt(spread + EPS)
    return centred * scale, scale


def norm_back(grad, values, gain_row):
    z, scale = normed(values)
    dz = grad * gain_row
    out = (
        dz - jnp.mean(dz, -1, keepdims=True) - z * jnp.mean(dz * z, -1, keepdims=True)
    ) * scale
    gain_grad = jnp.sum(grad * z, 0, keepdims=True)
    offset_grad = jnp.sum(grad, 0, keepdims=True)
    return out, gain_grad, offset_grad


def two_rows(first, second):
    return jnp.concatenate([first, second, jnp.zeros((6, D), F32)], 0)


def group_start(x, k, base=0):
    return pl.multiple_of(base + lax.rem(x + k, 4) * GROUP, GROUP)


def start_copies(pairs, sems):
    copies = [
        pltpu.make_async_copy(source, target, sems.at[i])
        for i, (source, target) in enumerate(pairs)
    ]
    for copy in copies:
        copy.start()
    return copies


def wait_copies(copies):
    for copy in copies:
        copy.wait()


def qkv_kernel(layer, place_ref, h_ref, pa_ref, *refs):
    blocks, refs = refs[:8], refs[8:]
    a1p_ref, gains_ref, out_refs = refs[0], refs[1], refs[2:6]
    win, table, turned, sems = refs[6:]
    rows = [pl.ds(96 * i, 96) for i in range(8)]
    norm_copies = start_copies(
        [(b.at[layer, :, pl.ds(FF, 128)], table.at[r]) for b, r in zip(blocks, rows)],
        sems.at[pl.ds(0, 8)],
    )
    win_copies = start_copies(
        [(b.at[layer, :, pl.ds(0, 3 * D)], win.at[r]) for b, r in zip(blocks, rows)],
        sems.at[pl.ds(8, 8)],
    )
    z, _ = normed(h_ref[...])
    wait_copies(norm_copies)
    gains = dot(table[...], pa_ref[...], 0, 1)[0:8]
    gains_ref[...] = gains
    a1 = (z * gains[0:1] + gains[1:2]).astype(BF)
    a1p = dot(a1, pa_ref[...]).astype(BF)
    a1p_ref[...] = a1p
    wait_copies(win_copies)
    for c in range(3):
        part = dot(a1p, win[:, c * D : (c + 1) * D])
        if c == 0:
            part = part * HEAD_DIM ** (-0.5)
        turned[c * D : (c + 1) * D, :] = part.astype(BF).T
    x = place_ref[0]
    for k in range(4):
        for c in range(3):
            out_refs[k][c * GROUP : (c + 1) * GROUP, :] = turned[
                pl.ds(group_start(x, k, c * D), GROUP), :
            ]


def key_bias(place_ref, bias):
    x, yh, length = place_ref[0], place_ref[1], place_ref[2]
    for k in range(4):
        for half in range(2):
            start = lax.rem(x + k, 4) * 256 + lax.rem(yh + half, 2) * 128
            slot = start + lax.broadcasted_iota(jnp.int32, (128, TOKENS), 0)
            bias[pl.ds(k * 256 + half * 128, 128), :] = jnp.where(slot < length, 0.0, -1e30)


def side_by_side(refs, start):
    return jnp.concatenate([r[start : start + HEAD_DIM, :] for r in refs], 1)


def attend_kernel(place_ref, t0, t1, t2, t3, u0, u1, u2, u3, sums_ref, bias):
    t_refs, u_refs = (t0, t1, t2, t3), (u0, u1, u2, u3)
    key_bias(place_ref, bias)
    for j in range(3):
        keys = side_by_side(t_refs, GROUP + j * HEAD_DIM).T
        values_t = side_by_side(t_refs, 2 * GROUP + j * HEAD_DIM)
        for b in range(4):
            query_t = t_refs[b][j * HEAD_DIM : (j + 1) * HEAD_DIM, :]
            scores = dot(keys, query_t) + bias[...]
            peak = jnp.max(scores, 0, keepdims=True)
            expont = jnp.exp(scores - peak)
            total = jnp.sum(expont, 0, keepdims=True)
            mixed = dot(values_t, expont.astype(BF)) / total
            u_refs[b][j * HEAD_DIM : (j + 1) * HEAD_DIM, :] = mixed.astype(BF)
            sums_ref[j : j + 1, b * TOKENS : (b + 1) * TOKENS] = peak + jnp.log(total)


def attend_back_kernel(place_ref, *refs):
    t_refs, g_refs, u_refs = refs[0:4], refs[4:8], refs[8:12]
    sums_ref = refs[12]
    out_refs = refs[13:17]
    bias = refs[17]
    key_bias(place_ref, bias)
    for j in range(3):
        keys_t = side_by_side(t_refs, GROUP + j * HEAD_DIM)
        keys = keys_t.T
        values = side_by_side(t_refs, 2 * GROUP + j * HEAD_DIM).T
        grad_keys = jnp.zeros((4 * TOKENS, HEAD_DIM), F32)
        grad_values = jnp.zeros((4 * TOKENS, HEAD_DIM), F32)
        rows = slice(j * HEAD_DIM, (j + 1) * HEAD_DIM)
        for b in range(4):
            query_t = t_refs[b][rows, :]
            grad_t = g_refs[b][rows, :]
            scores = dot(keys, query_t) + bias[...]
            probs = jnp.exp(scores - sums_ref[j : j + 1, b * TOKENS : (b + 1) * TOKENS])
            grad_probs = dot(values, grad_t)
            delta = jnp.sum(
                grad_t.astype(F32) * u_refs[b][rows, :].astype(F32), 0, keepdims=True
            )
            grad_scores = (probs * (grad_probs - delta)).astype(BF)
            grad_values = grad_values + dot(probs.astype(BF), grad_t, 1, 1)
            grad_keys = grad_keys + dot(grad_scores, query_t, 1, 1)
            grad_query = dot(keys_t, grad_scores) * HEAD_DIM ** (-0.5)
            out_refs[b][rows, :] = grad_query.astype(BF)
        grad_keys = grad_keys.astype(BF).T
        grad_values = grad_values.astype(BF).T
        for b in range(4):
            columns = slice(b * TOKENS, (b + 1) * TOKENS)
            start = GROUP + j * HEAD_DIM
            out_refs[b][start : start + HEAD_DIM, :] = grad_keys[:, columns]
            start = 2 * GROUP + j * HEAD_DIM
            out_refs[b][start : start + HEAD_DIM, :] = grad_values[:, columns]


def mlp_copies(layer, a_blocks, b_blocks, c_blocks, wout, w1, w2, sems):
    out_copies = start_copies(
        [
            (b.at[layer, :, pl.ds(3 * D, D)], wout.at[pl.ds(96 * i, 96)])
            for i, b in enumerate(a_blocks)
        ],
        sems.at[pl.ds(0, 8)],
    )
    first_copies = start_copies(
        [
            (b.at[layer], w1.at[i // 4, pl.ds(192 * (i % 4), 192)])
            for i, b in enumerate(b_blocks)
        ],
        sems.at[pl.ds(8, 8)],
    )
    second_copies = start_copies(
        [
            (b.at[layer], w2.at[i // 4, pl.ds(384 * (i % 4), 384)])
            for i, b in enumerate(c_blocks)
        ],
        sems.at[pl.ds(16, 8)],
    )
    return out_copies, first_copies, second_copies


def mlp_kernel(layer, place_ref, h_ref, *refs):
    u_refs, refs = refs[:4], refs[4:]
    po_ref, p2_ref, gains_ref = refs[:3]
    a_blocks, b_blocks, c_blocks = refs[3:11], refs[11:19], refs[19:27]
    h1_ref, next_ref, a2_ref, op_ref, act_ref, slope_ref = refs[27:33]
    turned, wout, w1, w2, sems = refs[33:]
    out_copies, first_copies, second_copies = mlp_copies(
        layer, a_blocks, b_blocks, c_blocks, wout, w1, w2, sems
    )
    x = place_ref[0]
    for k in range(4):
        turned[pl.ds(group_start(x, k), GROUP), :] = u_refs[k][...]
    op = dot(turned[...], po_ref[...], 0, 0).astype(BF)
    op_ref[...] = op
    wait_copies(out_copies)
    h1 = h_ref[...] + dot_two(dot(op, wout[...]), p2_ref[...])
    h1_ref[...] = h1
    z, _ = normed(h1)
    a2 = (z * gains_ref[2:3] + gains_ref[3:4]).astype(BF)
    a2_ref[...] = a2
    wait_copies(first_copies)
    total = h1
    for half in range(2):
        pre = dot(a2, w1[half])
        below = 0.5 * (1.0 + lax.erf(pre * ROOT_HALF))
        act = (pre * below).astype(BF)
        slope = below + pre * (jnp.exp(-0.5 * pre * pre) * INV_ROOT_TWO_PI)
        columns = slice(half * 1536, (half + 1) * 1536)
        act_ref[:, columns] = act
        slope_ref[:, columns] = slope.astype(BF)
        if half == 0:
            wait_copies(second_copies)
        total = total + dot(act, w2[half])
    next_ref[...] = total


def mlp_back_kernel(layer, place_ref, g_ref, slope_ref, h1_ref, gains_ref, p2_ref, po_ref, *refs):
    a_blocks, b_blocks, c_blocks = refs[0:8], refs[8:16], refs[16:24]
    dpre_ref, g1_ref, g1b_ref, norm_ref = refs[24:28]
    out_refs = refs[28:32]
    turned, wout, w1, w2, sems = refs[32:]
    out_copies, first_copies, second_copies = mlp_copies(
        layer, a_blocks, b_blocks, c_blocks, wout, w1, w2, sems
    )
    grad = g_ref[...]
    grad_low = grad.astype(BF)
    wait_copies(second_copies)
    grad_a2 = jnp.zeros((TOKENS, D), F32)
    for half in range(2):
        columns = slice(half * 1536, (half + 1) * 1536)
        grad_act = dot(grad_low, w2[half], 1, 1)
        dpre = (grad_act * slope_ref[:, columns].astype(F32)).astype(BF)
        dpre_ref[:, columns] = dpre
        if half == 0:
            wait_copies(first_copies)
        grad_a2 = grad_a2 + dot(dpre, w1[half], 1, 1)
    dv, gain_grad, offset_grad = norm_back(grad_a2, h1_ref[...], gains_ref[2:3])
    norm_ref[...] = two_rows(gain_grad, offset_grad)
    g1 = grad + dv
    g1_ref[...] = g1
    g1b = dot(g1.astype(BF), p2_ref[...], 1, 1).astype(BF)
    g1b_ref[...] = g1b
    wait_copies(out_copies)
    grad_op = dot(g1b, wout[...], 1, 1).astype(BF)
    turned[...] = dot(po_ref[...], grad_op, 1, 1).astype(BF)
    x = place_ref[0]
    for k in range(4):
        out_refs[k][...] = turned[pl.ds(group_start(x, k), GROUP), :]


def mlp_grad_kernel(g_ref, act_ref, a2_ref, dpre_ref, first_keep, first_send, second_keep, second_send):
    grad_low = g_ref[...].astype(BF)
    a2 = a2_ref[...]
    for half, (first, second) in enumerate(((first_keep, second_keep), (first_send, second_send))):
        for part in range(2):
            start = half * 1536 + part * 768
            columns = slice(start, start + 768)
            inner = slice(part * 768, part * 768 + 768)
            first[:, inner] = dot(a2, dpre_ref[:, columns], 0, 0).astype(BF)
            second[inner, :] = dot(act_ref[:, columns], grad_low, 0, 0).astype(BF)


def qkv_back_kernel(layer, place_ref, d0, d1, d2, d3, h_ref, g1_ref, gains_ref, pa_ref, *refs):
    blocks, refs = refs[:8], refs[8:]
    next_ref, dqkv_ref, norm_ref, win, sems = refs
    win_copies = start_copies(
        [
            (b.at[layer, :, pl.ds(0, 3 * D)], win.at[pl.ds(96 * i, 96)])
            for i, b in enumerate(blocks)
        ],
        sems,
    )
    x = place_ref[0]
    for k, piece in enumerate((d0, d1, d2, d3)):
        for c in range(3):
            dqkv_ref[pl.ds(group_start(x, k, c * D), GROUP), :] = piece[
                c * GROUP : (c + 1) * GROUP, :
            ]
    wait_copies(win_copies)
    turned = dot(win[...], dqkv_ref[...])
    grad_a1 = dot_two(turned, pa_ref[...], 0, 1)
    dv, gain_grad, offset_grad = norm_back(grad_a1, h_ref[...], gains_ref[0:1])
    norm_ref[...] = two_rows(gain_grad, offset_grad)
    next_ref[...] = g1_ref[...] + dv


def attn_grad_kernel(a1p_ref, dqkv_ref, op_ref, g1b_ref, norm1_ref, norm2_ref, pa_ref, keep_ref, send_ref):
    norms = jnp.concatenate(
        [norm1_ref[0:2], norm2_ref[0:2], jnp.zeros((124, D), F32)], 0
    )
    norms = dot_two(norms, pa_ref[...]).T
    for half, out in enumerate((keep_ref, send_ref)):
        rows = slice(half * 384, half * 384 + 384)
        for c in range(3):
            out[:, c * D : (c + 1) * D] = dot(
                a1p_ref[:, rows], dqkv_ref[c * D : (c + 1) * D, :], 0, 1
            ).astype(BF)
        out[:, 3 * D : 4 * D] = dot(op_ref[:, rows], g1b_ref[...], 0, 0).astype(BF)
        out[:, 4 * D :] = norms[rows].astype(BF)


def shaped(*shape, dtype=BF):
    return jax.ShapeDtypeStruct(shape, dtype)


def run_kernel(kernel, inputs, outs, scratch=(), flops=0, any_count=0, scalars=True):
    specs = []
    for i in range(len(inputs)):
        if scalars and i == 0:
            specs.append(pl.BlockSpec(memory_space=pltpu.SMEM))
        elif i >= len(inputs) - any_count:
            specs.append(pl.BlockSpec(memory_space=pl.ANY))
        else:
            specs.append(pl.BlockSpec(memory_space=pltpu.VMEM))
    moved = sum(v.size * v.dtype.itemsize for v in inputs) + sum(
        v.size * v.dtype.itemsize for v in outs
    )
    return pl.pallas_call(
        kernel,
        out_shape=tuple(outs),
        in_specs=specs,
        out_specs=tuple(pl.BlockSpec(memory_space=pltpu.VMEM) for _ in outs),
        scratch_shapes=list(scratch),
        compiler_params=pltpu.CompilerParams(vmem_limit_bytes=VMEM_LIMIT),
        cost_estimate=pl.CostEstimate(flops=flops, bytes_accessed=moved, transcendentals=0),
    )(*inputs)


MLP_SCRATCH = (
    pltpu.VMEM((D, TOKENS), BF),
    pltpu.VMEM((D, D), BF),
    pltpu.VMEM((2, D, 1536), BF),
    pltpu.VMEM((2, 1536, D), BF),
    pltpu.SemaphoreType.DMA((24,)),
)
UNIT = 2 * TOKENS * D * D
ATTEND = 2 * 3 * 1024 * 1024 * HEAD_DIM * 4


def by_y(quads, low):
    one = jnp.where(low == 0, quads[1], quads[3])
    three = jnp.where(low == 0, quads[3], quads[1])
    return jnp.stack([jnp.stack([quads[0], one]), jnp.stack([quads[2], three])])


def from_y(table, low):
    one = jnp.where(low == 0, table[0, 1], table[1, 1])
    three = jnp.where(low == 0, table[1, 1], table[0, 1])
    return [table[0, 0], one, table[1, 0], three]


def weights_everywhere(norm_params, attn_in, attn_out, mlp_in, mlp_out, low):
    norm_part = jnp.pad(jnp.swapaxes(norm_params, 1, 2), ((0, 0), (0, 0), (0, 124)))
    a = jnp.concatenate([attn_in, attn_out, norm_part], -1).reshape(300, 128)
    b = mlp_in.reshape(288, 128)
    c = mlp_out.reshape(288, 128)
    a, b, c = (
        jnp.stack(gather_four(a, "z")),
        jnp.stack(gather_four(b, "y")),
        jnp.stack(gather_four(c, "x")),
    )
    a, b, c = gather_four(a, "x"), gather_four(b, "z"), gather_four(c, "y")
    a = jnp.stack(a).reshape(4, 4, 2, 6, ROW_A)
    a = a.transpose(2, 1, 0, 3, 4).reshape(2, 96, ROW_A)
    b = jnp.stack(b).reshape(4, 4, 2, 96, 192)
    b = by_y([b[:, k] for k in range(4)], low)
    b = b.transpose(3, 0, 4, 2, 1, 5).reshape(2, 192, 1536)
    c = by_y([v.reshape(4, 2, 192, 96) for v in c], low)
    c = c.transpose(3, 1, 4, 2, 0, 5).reshape(2, 384, 768)
    a, b, c = gather_four(a, "y"), gather_four(b, "x"), gather_four(c, "z")
    return tuple(part + [fetch(v, c=1) for v in part] for part in (a, b, c))


def gradients_home(keeps, sends, low):
    halves = [
        [
            (k.astype(F32) + fetch(s, c=1).astype(F32)).astype(BF)
            for k, s in zip(keep, send)
        ]
        for keep, send in zip(keeps, sends)
    ]

    def parts(which, rows):
        return [
            jnp.stack([halves[l][which][k * rows : (k + 1) * rows] for l in range(2)])
            for k in range(4)
        ]

    a, b, c = (
        reduce_four(parts(0, 96), "y").astype(BF),
        reduce_four(parts(1, 192), "x").astype(BF),
        reduce_four(parts(2, 384), "z").astype(BF),
    )
    a = a.reshape(2, 4, 4, 6, ROW_A).transpose(2, 1, 0, 3, 4).reshape(4, 4, 300, 128)
    b = b.reshape(2, 2, 96, 4, 2, 192).transpose(1, 4, 3, 0, 2, 5)
    b = jnp.stack(from_y(b, low)).transpose(1, 0, 2, 3, 4).reshape(4, 4, 288, 128)
    c = c.reshape(2, 2, 192, 4, 2, 96).transpose(4, 1, 3, 0, 2, 5)
    c = jnp.stack(from_y(c, low)).reshape(4, 4, 288, 128)
    a, b, c = (
        reduce_four([a[k] for k in range(4)], "x").astype(BF),
        reduce_four([b[k] for k in range(4)], "z").astype(BF),
        reduce_four([c[k] for k in range(4)], "y").astype(BF),
    )
    a, b, c = (
        reduce_four([a[k] for k in range(4)], "z"),
        reduce_four([b[k] for k in range(4)], "y"),
        reduce_four([c[k] for k in range(4)], "x"),
    )
    a = a.reshape(2, 6, ROW_A)
    return (
        jnp.swapaxes(a[:, :, 4 * D : 4 * D + 4], 1, 2),
        a[:, :, : 3 * D],
        a[:, :, 3 * D : 4 * D],
        b.reshape(2, 96, 192),
        c.reshape(2, 192, 96),
    )


def body(inputs, lengths, norm_params, attn_in, attn_out, mlp_in, mlp_out, cotangent):
    wide = lax.axis_index("wide")
    narrow = lax.axis_index("narrow")
    core, low, z = wide % 2, (wide // 2) % 2, wide // 4
    x, high = narrow // 2, narrow % 2
    y = high * 2 + low

    a_blocks, b_blocks, c_blocks = weights_everywhere(
        norm_params, attn_in, attn_out, mlp_in, mlp_out, low
    )

    slot = jnp.arange(D, dtype=jnp.int32)
    own_order = ((x + slot // 192) % 4) * 192 + ((high + (slot // 96) % 2) % 2) * 96 + slot % 96
    row_core = (core + slot // 384) % 2
    row_y = (y + (slot // 96) % 4) % 4
    row_z = (z + (slot // 24) % 4) % 4
    row_x = (x + (slot // 6) % 4) % 4
    row_order = 6 * index_of(row_z, row_y, row_core, row_x) + slot % 6
    pa = (own_order[:, None] == row_order[None, :]).astype(BF)
    po = (slot[:, None] == row_order[None, :]).astype(BF)
    p2 = (slot[:, None] == own_order[None, :]).astype(BF)

    both = jnp.stack([inputs, cotangent])[:, :, 0]
    mine = lax.dynamic_index_in_dim(both, high, 1, keepdims=False)
    other = lax.dynamic_index_in_dim(both, 1 - high, 1, keepdims=False)
    rows = jnp.concatenate([mine, fetch(other, y=2)], 1)
    rows = jnp.einsum("ntd,dr->ntr", rows, p2, preferred_element_type=F32)
    hidden, grad = rows[0], rows[1]
    length = lax.dynamic_index_in_dim(lengths[:, 0], high, 0, keepdims=False)
    place = jnp.stack([x, high, length, z]).astype(jnp.int32)

    records = []
    for layer in range(2):
        a1p, gains, *pieces = run_kernel(
            functools.partial(qkv_kernel, layer),
            [place, hidden, pa] + a_blocks,
            [shaped(TOKENS, D), shaped(8, D, dtype=F32)] + [shaped(576, TOKENS)] * 4,
            (
                pltpu.VMEM((D, 3 * D), BF),
                pltpu.VMEM((D, 128), BF),
                pltpu.VMEM((3 * D, TOKENS), BF),
                pltpu.SemaphoreType.DMA((16,)),
            ),
            flops=4 * UNIT,
            any_count=8,
        )
        turned = exchange_four(pieces)
        *mixed, sums = run_kernel(
            attend_kernel,
            [place] + turned,
            [shaped(GROUP, TOKENS)] * 4 + [shaped(3, 1024, dtype=F32)],
            (pltpu.VMEM((1024, TOKENS), F32),),
            flops=ATTEND,
        )
        back = exchange_four(mixed)
        h1, following, a2, op, act, slope = run_kernel(
            functools.partial(mlp_kernel, layer),
            [place, hidden] + back + [po, p2, gains] + a_blocks + b_blocks + c_blocks,
            [
                shaped(TOKENS, D, dtype=F32),
                shaped(TOKENS, D, dtype=F32),
                shaped(TOKENS, D),
                shaped(TOKENS, D),
                shaped(TOKENS, FF),
                shaped(TOKENS, FF),
            ],
            MLP_SCRATCH,
            flops=11 * UNIT,
            any_count=24,
        )
        records.append((hidden, a1p, gains, turned, mixed, sums, h1, a2, op, act, slope))
        hidden = following

    def leave(values):
        values = jnp.dot(
            values, p2.astype(F32).T, precision=lax.Precision.HIGHEST, preferred_element_type=F32
        )
        own = values[:128]
        came = fetch(values[128:], y=2)
        return jnp.stack(
            [jnp.where(high == 0, own, came), jnp.where(high == 0, came, own)]
        )[:, None]

    outputs = leave(hidden)

    keeps, sends = [None, None], [None, None]
    for layer in (1, 0):
        hidden, a1p, gains, turned, mixed, sums, h1, a2, op, act, slope = records[layer]
        dpre, g1, g1b, norm2, *pieces = run_kernel(
            functools.partial(mlp_back_kernel, layer),
            [place, grad, slope, h1, gains, p2, po] + a_blocks + b_blocks + c_blocks,
            [
                shaped(TOKENS, FF),
                shaped(TOKENS, D, dtype=F32),
                shaped(TOKENS, D),
                shaped(8, D, dtype=F32),
            ]
            + [shaped(GROUP, TOKENS)] * 4,
            MLP_SCRATCH,
            flops=11 * UNIT,
            any_count=24,
        )
        grad_mixed = exchange_four(pieces)
        first_keep, first_send, second_keep, second_send = run_kernel(
            mlp_grad_kernel,
            [grad, act, a2, dpre],
            [shaped(D, 1536), shaped(D, 1536), shaped(1536, D), shaped(1536, D)],
            flops=8 * UNIT,
            scalars=False,
        )
        pieces = run_kernel(
            attend_back_kernel,
            [place] + turned + grad_mixed + mixed + [sums],
            [shaped(576, TOKENS)] * 4,
            (pltpu.VMEM((1024, TOKENS), F32),),
            flops=3 * ATTEND,
        )
        grad_pieces = exchange_four(pieces)
        grad, dqkv, norm1 = run_kernel(
            functools.partial(qkv_back_kernel, layer),
            [place] + grad_pieces + [hidden, g1, gains, pa] + a_blocks,
            [shaped(TOKENS, D, dtype=F32), shaped(3 * D, TOKENS), shaped(8, D, dtype=F32)],
            (pltpu.VMEM((D, 3 * D), BF), pltpu.SemaphoreType.DMA((8,))),
            flops=5 * UNIT,
            any_count=8,
        )
        attn_keep, attn_send = run_kernel(
            attn_grad_kernel,
            [a1p, dqkv, op, g1b, norm1, norm2, pa],
            [shaped(384, ROW_A)] * 2,
            flops=4 * UNIT,
            scalars=False,
        )
        keeps[layer] = (attn_keep, first_keep, second_keep)
        sends[layer] = (attn_send, first_send, second_send)
    grad_inputs = leave(grad)
    return (outputs, grad_inputs) + gradients_home(keeps, sends, low)


def solution(mesh):
    in_specs = (
        P(None, "wide", "narrow", None),
        P(None, "wide"),
        P(None, None, ("wide", "narrow")),
        P(None, ("wide", "narrow"), None),
        P(None, ("wide", "narrow"), None),
        P(None, "narrow", "wide"),
        P(None, "wide", "narrow"),
        P(None, "wide", "narrow", None),
    )
    out_specs = (
        P(None, "wide", "narrow", None),
        P(None, "wide", "narrow", None),
        P(None, None, ("wide", "narrow")),
        P(None, ("wide", "narrow"), None),
        P(None, ("wide", "narrow"), None),
        P(None, "narrow", "wide"),
        P(None, "wide", "narrow"),
    )
    return jax.shard_map(body, mesh=mesh, in_specs=in_specs, out_specs=out_specs, check_vma=False)
```

```python
import functools

import jax
import jax.numpy as jnp
from jax import lax
from jax.experimental import pallas as pl
from jax.experimental.pallas import tpu as pltpu
from jax.sharding import PartitionSpec as P

D = 768
FF = 3072
HEAD_DIM = 64
GROUP = 192
TOKENS = 256
EPS = 1e-06
ROOT_HALF = 0.7071067811865476
INV_ROOT_TWO_PI = 0.3989422804014327
ROW_A = 3200
BF = jnp.bfloat16
F32 = jnp.float32
AXES = ("wide", "narrow")
VMEM_LIMIT = 56 * 1024 * 1024


def index_of(z, y, c, x):
    return ((z * 2 + y % 2) * 2 + c) * 8 + x * 2 + y // 2


def everywhere():
    for z in range(4):
        for y in range(4):
            for c in range(2):
                for x in range(4):
                    yield {"z": z, "y": y, "c": c, "x": x}


def fetch(value, axis, step):
    pairs = []
    for here in everywhere():
        there = dict(here)
        there[axis] = (here[axis] + step) % (2 if axis == "c" else 4)
        pairs.append((index_of(**there), index_of(**here)))
    return lax.ppermute(value, AXES, pairs)


def swap(value, axis, side):
    pairs = []
    for here in everywhere():
        step = side if (here[axis] + here["c"]) % 2 == 0 else -side
        there = dict(here)
        there[axis] = (here[axis] + step) % 4
        pairs.append((index_of(**here), index_of(**there)))
    return lax.ppermute(value, AXES, pairs)


def exchange_four(pieces):
    return [pieces[0]] + [fetch(pieces[4 - k], "x", k) for k in (1, 2, 3)]


def dot(left, right, over_left=1, over_right=0):
    return lax.dot_general(
        left, right, (((over_left,), (over_right,)), ((), ())), preferred_element_type=F32
    )


def dot_two(left, right, over_left=1, over_right=0):
    high = left.astype(BF)
    low = (left - high.astype(F32)).astype(BF)
    return dot(high, right, over_left, over_right) + dot(low, right, over_left, over_right)


def normed(values):
    average = jnp.mean(values, -1, keepdims=True)
    centred = values - average
    spread = jnp.mean(centred * centred, -1, keepdims=True)
    scale = lax.rsqrt(spread + EPS)
    return centred * scale, scale


def norm_back(grad, values, gain_row):
    z, scale = normed(values)
    dz = grad * gain_row
    out = (
        dz - jnp.mean(dz, -1, keepdims=True) - z * jnp.mean(dz * z, -1, keepdims=True)
    ) * scale
    gain_grad = jnp.sum(grad * z, 0, keepdims=True)
    offset_grad = jnp.sum(grad, 0, keepdims=True)
    return out, gain_grad, offset_grad


def two_rows(first, second):
    return jnp.concatenate([first, second, jnp.zeros((6, D), F32)], 0)


def group_start(x, k, base=0):
    return pl.multiple_of(base + lax.rem(x + k, 4) * GROUP, GROUP)


def start_copies(pairs, sems):
    copies = [
        pltpu.make_async_copy(source, target, sems.at[i])
        for i, (source, target) in enumerate(pairs)
    ]
    for copy in copies:
        copy.start()
    return copies


def wait_copies(copies):
    for copy in copies:
        copy.wait()


X, HIGH, LENGTH, NEAR_X, NEAR_Y, NEAR_Z, LOW = range(7)


def weight_blocks(refs, near):
    pair, far, core_pair, core_far = refs
    return [
        (pair, 0, 0, 0),
        (pair, 1, 0, near),
        (far, 0, 0, 3 - near),
        (far, 1, 0, 3),
        (core_pair, 0, 1, 0),
        (core_pair, 1, 1, 3 - near),
        (core_far, 0, 1, near),
        (core_far, 1, 1, 3),
    ]


def at_rows(core, spot, rows):
    return pl.ds(pl.multiple_of((core * 4 + spot) * rows, rows), rows)


def qkv_kernel(place_ref, h_ref, pa_ref, *refs):
    blocks = weight_blocks(refs[:4], place_ref[NEAR_Y])
    a1p_keep, a1p_send, gains_ref = refs[4:7]
    out_refs = refs[7:11]
    win, table, turned, sems = refs[11:]
    norm_copies = start_copies(
        [
            (r.at[i, :, pl.ds(FF, 128)], table.at[at_rows(core, spot, 96)])
            for r, i, core, spot in blocks
        ],
        sems.at[pl.ds(0, 8)],
    )
    win_copies = start_copies(
        [
            (r.at[i, :, pl.ds(0, 3 * D)], win.at[at_rows(core, spot, 96)])
            for r, i, core, spot in blocks
        ],
        sems.at[pl.ds(8, 8)],
    )
    z, _ = normed(h_ref[...])
    wait_copies(norm_copies)
    gains = dot(table[...], pa_ref[...], 0, 1)[0:8]
    gains_ref[...] = gains
    a1 = (z * gains[0:1] + gains[1:2]).astype(BF)
    a1p = dot(a1, pa_ref[...]).astype(BF)
    a1p_keep[...] = a1p[:, :384]
    a1p_send[...] = a1p[:, 384:]
    wait_copies(win_copies)
    for c in range(3):
        part = dot(a1p, win[:, c * D : (c + 1) * D])
        if c == 0:
            part = part * HEAD_DIM ** (-0.5)
        turned[c * D : (c + 1) * D, :] = part.astype(BF).T
    x = place_ref[X]
    for k in range(4):
        for c in range(3):
            out_refs[k][c * GROUP : (c + 1) * GROUP, :] = turned[
                pl.ds(group_start(x, k, c * D), GROUP), :
            ]


def key_bias(place_ref, bias):
    x, yh, length = place_ref[0], place_ref[1], place_ref[2]
    for k in range(4):
        for half in range(2):
            start = lax.rem(x + k, 4) * 256 + lax.rem(yh + half, 2) * 128
            slot = start + lax.broadcasted_iota(jnp.int32, (128, TOKENS), 0)
            bias[pl.ds(k * 256 + half * 128, 128), :] = jnp.where(slot < length, 0.0, -1e30)


def side_by_side(refs, start):
    return jnp.concatenate([r[start : start + HEAD_DIM, :] for r in refs], 1)


def attend_kernel(place_ref, t0, t1, t2, t3, u0, u1, u2, u3, sums_ref, bias):
    t_refs, u_refs = (t0, t1, t2, t3), (u0, u1, u2, u3)
    key_bias(place_ref, bias)
    for j in range(3):
        keys = side_by_side(t_refs, GROUP + j * HEAD_DIM).T
        values_t = side_by_side(t_refs, 2 * GROUP + j * HEAD_DIM)
        for b in range(4):
            query_t = t_refs[b][j * HEAD_DIM : (j + 1) * HEAD_DIM, :]
            scores = dot(keys, query_t) + bias[...]
            peak = jnp.max(scores, 0, keepdims=True)
            expont = jnp.exp(scores - peak)
            total = jnp.sum(expont, 0, keepdims=True)
            mixed = dot(values_t, expont.astype(BF)) / total
            u_refs[b][j * HEAD_DIM : (j + 1) * HEAD_DIM, :] = mixed.astype(BF)
            sums_ref[j : j + 1, b * TOKENS : (b + 1) * TOKENS] = peak + jnp.log(total)


def attend_back_kernel(place_ref, *refs):
    t_refs, g_refs, u_refs = refs[0:4], refs[4:8], refs[8:12]
    sums_ref = refs[12]
    out_refs = refs[13:17]
    bias = refs[17]
    key_bias(place_ref, bias)
    for j in range(3):
        keys_t = side_by_side(t_refs, GROUP + j * HEAD_DIM)
        keys = keys_t.T
        values = side_by_side(t_refs, 2 * GROUP + j * HEAD_DIM).T
        grad_keys = jnp.zeros((4 * TOKENS, HEAD_DIM), F32)
        grad_values = jnp.zeros((4 * TOKENS, HEAD_DIM), F32)
        rows = slice(j * HEAD_DIM, (j + 1) * HEAD_DIM)
        for b in range(4):
            query_t = t_refs[b][rows, :]
            grad_t = g_refs[b][rows, :]
            scores = dot(keys, query_t) + bias[...]
            probs = jnp.exp(scores - sums_ref[j : j + 1, b * TOKENS : (b + 1) * TOKENS])
            grad_probs = dot(values, grad_t)
            delta = jnp.sum(
                grad_t.astype(F32) * u_refs[b][rows, :].astype(F32), 0, keepdims=True
            )
            grad_scores = (probs * (grad_probs - delta)).astype(BF)
            grad_values = grad_values + dot(probs.astype(BF), grad_t, 1, 1)
            grad_keys = grad_keys + dot(grad_scores, query_t, 1, 1)
            grad_query = dot(keys_t, grad_scores) * HEAD_DIM ** (-0.5)
            out_refs[b][rows, :] = grad_query.astype(BF)
        grad_keys = grad_keys.astype(BF).T
        grad_values = grad_values.astype(BF).T
        for b in range(4):
            columns = slice(b * TOKENS, (b + 1) * TOKENS)
            start = GROUP + j * HEAD_DIM
            out_refs[b][start : start + HEAD_DIM, :] = grad_keys[:, columns]
            start = 2 * GROUP + j * HEAD_DIM
            out_refs[b][start : start + HEAD_DIM, :] = grad_values[:, columns]


def mlp_copies(place_ref, refs, wout, w1, w2, sems):
    out_copies = start_copies(
        [
            (r.at[i, :, pl.ds(3 * D, D)], wout.at[at_rows(core, spot, 96)])
            for r, i, core, spot in weight_blocks(refs[0:4], place_ref[NEAR_Y])
        ],
        sems.at[pl.ds(0, 8)],
    )
    first_copies = start_copies(
        [
            (r.at[i], w1.at[core, at_rows(0, spot, 192)])
            for r, i, core, spot in weight_blocks(refs[4:8], place_ref[NEAR_X])
        ],
        sems.at[pl.ds(8, 8)],
    )
    second_copies = start_copies(
        [
            (r.at[i], w2.at[:, at_rows(core, spot, 384)])
            for r, i, core, spot in weight_blocks(refs[8:12], place_ref[NEAR_Z])
        ],
        sems.at[pl.ds(16, 8)],
    )
    return out_copies, first_copies, second_copies


def mlp_kernel(place_ref, h_ref, u0, u1, u2, u3, a1p_send, po_ref, p2_ref, gains_ref, *refs):
    h1_ref, next_ref, slope_ref, send_ref, op_keep, act_keep = refs[12:18]
    turned, wout, w1, w2, sems = refs[18:]
    out_copies, first_copies, second_copies = mlp_copies(
        place_ref, refs[:12], wout, w1, w2, sems
    )
    send_ref[:, 0:384] = a1p_send[...]
    x = place_ref[X]
    for k, piece in enumerate((u0, u1, u2, u3)):
        turned[pl.ds(group_start(x, k), GROUP), :] = piece[...]
    op = dot(turned[...], po_ref[...], 0, 0).astype(BF)
    op_keep[...] = op[:, :384]
    send_ref[:, 384:768] = op[:, 384:]
    wait_copies(out_copies)
    h1 = h_ref[...] + dot_two(dot(op, wout[...]), p2_ref[...])
    h1_ref[...] = h1
    z, _ = normed(h1)
    a2 = (z * gains_ref[2:3] + gains_ref[3:4]).astype(BF)
    send_ref[:, 768:1536] = a2
    wait_copies(first_copies)
    total = h1
    for half in range(2):
        pre = dot(a2, w1[half])
        below = 0.5 * (1.0 + lax.erf(pre * ROOT_HALF))
        act = (pre * below).astype(BF)
        slope = below + pre * (jnp.exp(-0.5 * pre * pre) * INV_ROOT_TWO_PI)
        columns = slice(half * 1536, (half + 1) * 1536)
        if half == 0:
            act_keep[...] = act
            wait_copies(second_copies)
        else:
            send_ref[:, 1536:] = act
        slope_ref[:, columns] = slope.astype(BF)
        total = total + dot(act, w2[:, columns], 1, 1)
    next_ref[...] = total


def mlp_back_kernel(place_ref, g_ref, slope_ref, h1_ref, gains_ref, p2_ref, po_ref, *refs):
    g1_ref, send_ref, dpre_keep, norm_ref = refs[12:16]
    out_refs = refs[16:20]
    turned, wout, w1, w2, sems = refs[20:]
    out_copies, first_copies, second_copies = mlp_copies(
        place_ref, refs[:12], wout, w1, w2, sems
    )
    grad = g_ref[...]
    grad_low = grad.astype(BF)
    send_ref[:, 1536:2304] = grad_low
    wait_copies(second_copies)
    grad_a2 = jnp.zeros((TOKENS, D), F32)
    for half in range(2):
        columns = slice(half * 1536, (half + 1) * 1536)
        grad_act = dot(grad_low, w2[:, columns])
        dpre = (grad_act * slope_ref[:, columns].astype(F32)).astype(BF)
        if half == 0:
            dpre_keep[...] = dpre
            wait_copies(first_copies)
        else:
            send_ref[:, 0:1536] = dpre
        grad_a2 = grad_a2 + dot(dpre, w1[half], 1, 1)
    dv, gain_grad, offset_grad = norm_back(grad_a2, h1_ref[...], gains_ref[2:3])
    norm_ref[...] = two_rows(gain_grad, offset_grad)
    g1 = grad + dv
    g1_ref[...] = g1
    g1b = dot(g1.astype(BF), p2_ref[...], 1, 1).astype(BF)
    send_ref[:, 2304:] = g1b
    wait_copies(out_copies)
    grad_op = dot(g1b, wout[...], 1, 1).astype(BF)
    turned[...] = dot(po_ref[...], grad_op, 1, 1).astype(BF)
    x = place_ref[X]
    for k in range(4):
        out_refs[k][...] = turned[pl.ds(group_start(x, k), GROUP), :]


def both_cores(first_ref, second_ref):
    return jnp.concatenate([first_ref[...], second_ref[...]], 0)


def store_blocks(near, mine, send, columns, blocks):
    mine[0, :, columns] = blocks[0]
    send[1, :, columns] = blocks[3]

    @pl.when(near == 1)
    def _():
        mine[1, :, columns] = blocks[1]
        send[0, :, columns] = blocks[2]

    @pl.when(near == 2)
    def _():
        mine[1, :, columns] = blocks[2]
        send[0, :, columns] = blocks[1]


def mlp_grad_kernel(
    place_ref, a2_0, a2_1, act_0, act_1, dpre_0, dpre_1, gb_0, gb_1,
    first_mine, first_send, second_mine, second_send,
):
    a2 = both_cores(a2_0, a2_1)
    grad_low = both_cores(gb_0, gb_1)
    dpre = both_cores(dpre_0, dpre_1)
    for part in range(2):
        columns = slice(part * 768, part * 768 + 768)
        value = dot(a2, dpre[:, columns], 0, 0).astype(BF)
        blocks = [value[192 * k : 192 * k + 192] for k in range(4)]
        store_blocks(place_ref[NEAR_X], first_mine, first_send, columns, blocks)
    act = both_cores(act_0, act_1)
    blocks = [
        dot(grad_low, act[:, 384 * k : 384 * k + 384], 0, 0).astype(BF) for k in range(4)
    ]
    store_blocks(place_ref[NEAR_Z], second_mine, second_send, slice(0, 384), blocks)


def qkv_back_kernel(
    place_ref, d0, d1, d2, d3, h_ref, g1_ref, gains_ref, pa_ref, norm2_ref, *refs
):
    blocks = weight_blocks(refs[:4], place_ref[NEAR_Y])
    next_ref, dqkv_ref, norm_ref, win, sems = refs[4:]
    win_copies = start_copies(
        [
            (r.at[i, :, pl.ds(0, 3 * D)], win.at[at_rows(core, spot, 96)])
            for r, i, core, spot in blocks
        ],
        sems,
    )
    x = place_ref[X]
    for k, piece in enumerate((d0, d1, d2, d3)):
        for c in range(3):
            dqkv_ref[pl.ds(group_start(x, k, c * D), GROUP), :] = piece[
                c * GROUP : (c + 1) * GROUP, :
            ]
    wait_copies(win_copies)
    turned = dot(win[...], dqkv_ref[...])
    grad_a1 = dot_two(turned, pa_ref[...], 0, 1)
    dv, gain_grad, offset_grad = norm_back(grad_a1, h_ref[...], gains_ref[0:1])
    norm_ref[...] = jnp.concatenate(
        [gain_grad, offset_grad, norm2_ref[0:2], jnp.zeros((4, D), F32)], 0
    )
    next_ref[...] = g1_ref[...] + dv


def attn_grad_kernel(
    place_ref, a1p_0, a1p_1, op_0, op_1, g1b_0, g1b_1, dqkv_0, dqkv_1, norm_0, norm_1, pa_ref,
    mine, send,
):
    near = place_ref[NEAR_Y]
    norms = norm_0[...] + norm_1[...]
    norms = dot_two(norms, pa_ref[:, 0:384])
    norms = jnp.concatenate([norms, jnp.zeros((120, 384), F32)], 0).T.astype(BF)
    a1p = both_cores(a1p_0, a1p_1)
    for c in range(5):
        columns = slice(c * D, min((c + 1) * D, ROW_A))
        if c < 3:
            dqkv = jnp.concatenate(
                [dqkv_0[c * D : (c + 1) * D, :], dqkv_1[c * D : (c + 1) * D, :]], 1
            )
            value = dot(a1p, dqkv, 0, 1).astype(BF)
        elif c == 3:
            value = dot(both_cores(op_0, op_1), both_cores(g1b_0, g1b_1), 0, 0).astype(BF)
        else:
            value = norms
        blocks = [value[96 * k : 96 * k + 96] for k in range(4)]
        store_blocks(near, mine, send, columns, blocks)


def join_kernel(*refs):
    count = (len(refs) - 1) // 3
    pairs = []
    for own, came, out in zip(refs[:count], refs[count : 2 * count], refs[2 * count : -1]):
        pairs += [(own, out.at[0]), (came, out.at[1])]
    wait_copies(start_copies(pairs, refs[-1]))


def order_kernel(spots, place_ref, *refs):
    count = len(spots)
    pairs = []
    for spot, pair, far, out in zip(
        spots, refs[:count], refs[count : 2 * count], refs[2 * count : -1]
    ):
        near = place_ref[spot]
        pairs += [
            (pair.at[0], out.at[0]),
            (pair.at[1], out.at[near]),
            (far.at[0], out.at[3 - near]),
            (far.at[1], out.at[3]),
        ]
    wait_copies(start_copies(pairs, refs[-1]))


def layer_blocks_kernel(layer, place_ref, b_ref, c_ref, first_ref, second_ref):
    middle = 1 + place_ref[LOW]
    part = slice(layer * 192, layer * 192 + 192)
    for high in range(2):
        one, two = (0, middle) if high == 0 else (3, 3 - middle)
        for k in range(4):
            both = [b_ref[k, one][:, part], b_ref[k, two][:, part]]
            first_ref[high * 96 : high * 96 + 96, k * 384 : k * 384 + 384] = jnp.concatenate(
                both, 1
            )
            both = [c_ref[one, k][:, part], c_ref[two, k][:, part]]
            start = (2 * k + high) * 96
            second_ref[start : start + 96, :] = jnp.concatenate(both, 1)


def both_layers_kernel(place_ref, *refs):
    b0, b0_came, c0, c0_came, b1, b1_came, c1, c1_came = refs[:8]
    b_mine, b_send, c_mine, c_send = refs[8:]
    middle = 1 + place_ref[LOW]
    near_z, near_x = place_ref[NEAR_Z], place_ref[NEAR_X]

    def put(mine, send, near, spot, index, value):
        if isinstance(spot, int) and spot == 0:
            mine[0, index] = value
        elif isinstance(spot, int) and spot == 3:
            send[1, index] = value
        else:

            @pl.when(near == spot)
            def _():
                mine[1, index] = value

            @pl.when(near != spot)
            def _():
                send[0, index] = value

    for high in range(2):
        for k in range(4):
            rows, columns = slice(high * 96, high * 96 + 96), slice(k * 384, k * 384 + 384)
            b_parts = [
                total_of(b0[rows, columns], b0_came[rows, columns]),
                total_of(b1[rows, columns], b1_came[rows, columns]),
            ]
            rows = slice((2 * k + high) * 96, (2 * k + high) * 96 + 96)
            c_parts = [
                total_of(c0[rows, :], c0_came[rows, :]),
                total_of(c1[rows, :], c1_came[rows, :]),
            ]
            for part in range(2):
                if part == 0:
                    spot = 0 if high == 0 else 3
                else:
                    spot = middle if high == 0 else 3 - middle
                columns = slice(part * 192, part * 192 + 192)
                value = jnp.concatenate([v[:, columns] for v in b_parts], 1)
                put(b_mine, b_send, near_z, k, spot, value)
                value = jnp.concatenate([v[:, columns] for v in c_parts], 1)
                put(c_mine, c_send, near_x, k, spot, value)


def split_kernel(spots, place_ref, *refs):
    count = len(spots)
    for n, spot in enumerate(spots):
        near = place_ref[spot]
        value, mine, send = refs[n], refs[count + 2 * n], refs[count + 2 * n + 1]
        mine[0] = value[0]
        mine[1] = value[near]
        send[0] = value[3 - near]
        send[1] = value[3]


def total_of(first, second):
    return (first.astype(F32) + second.astype(F32)).astype(BF)


def halve_kernel(*refs):
    count = len(refs) // 4
    for n in range(count):
        mine, came = refs[n], refs[count + n]
        keep, send = refs[2 * count + 2 * n], refs[2 * count + 2 * n + 1]
        keep[...] = total_of(mine[0], came[0])
        send[...] = total_of(mine[1], came[1])


def total_kernel(keep, came, *out_refs):
    for k, out in enumerate(out_refs):
        out[...] = total_of(keep[k], came[k])


def total_split_kernel(spots, place_ref, *refs):
    count = len(spots)
    for n, spot in enumerate(spots):
        near = place_ref[spot]
        keep, came = refs[n], refs[count + n]
        mine, send = refs[2 * count + 2 * n], refs[2 * count + 2 * n + 1]
        mine[0] = total_of(keep[0], came[0])
        mine[1] = total_of(keep[near], came[near])
        send[0] = total_of(keep[3 - near], came[3 - near])
        send[1] = total_of(keep[3], came[3])


def nothing_kernel(*refs):
    pass


def after(values, done):
    anywhere = pl.BlockSpec(memory_space=pl.ANY)
    return pl.pallas_call(
        nothing_kernel,
        out_shape=tuple(jax.ShapeDtypeStruct(v.shape, v.dtype) for v in values),
        in_specs=[anywhere] * (len(values) + len(done)),
        out_specs=tuple(anywhere for _ in values),
        input_output_aliases={i: i for i in range(len(values))},
    )(*values, *done)


def shaped(*shape, dtype=BF):
    return jax.ShapeDtypeStruct(shape, dtype)


def like(value, *lead):
    return jax.ShapeDtypeStruct(tuple(lead) + tuple(value.shape), value.dtype)


def run_kernel(
    kernel, inputs, outs, scratch=(), flops=0, any_count=0, scalars=True, lying=False, done=()
):
    specs, arrays, moved = [], [], 0
    anywhere = pl.BlockSpec(memory_space=pl.ANY)
    for i, value in enumerate(inputs):
        if isinstance(value, tuple):
            value, width, index = value
            specs.append(pl.BlockSpec((value.shape[0], width), lambda _, n=index: (0, n)))
            moved += value.shape[0] * width * value.dtype.itemsize
        elif scalars and i == 0:
            specs.append(pl.BlockSpec(memory_space=pltpu.SMEM))
        else:
            lies = lying or i >= len(inputs) - any_count
            specs.append(anywhere if lies else pl.BlockSpec(memory_space=pltpu.VMEM))
            moved += value.size * value.dtype.itemsize
        arrays.append(value)
    moved += sum(v.size * v.dtype.itemsize for v in outs)
    count, extra = len(inputs), len(done)

    def whole(*refs):
        kernel(*refs[:count], *refs[count + extra :])

    return pl.pallas_call(
        whole,
        grid=(1,),
        out_shape=tuple(outs),
        in_specs=specs + [anywhere] * extra,
        out_specs=tuple(
            pl.BlockSpec(memory_space=pltpu.VMEM) for _ in outs
        ),
        scratch_shapes=list(scratch),
        compiler_params=pltpu.CompilerParams(vmem_limit_bytes=VMEM_LIMIT),
        cost_estimate=pl.CostEstimate(flops=flops, bytes_accessed=moved, transcendentals=0),
    )(*arrays, *done)


MLP_SCRATCH = (
    pltpu.VMEM((D, TOKENS), BF),
    pltpu.VMEM((D, D), BF),
    pltpu.VMEM((2, D, 1536), BF),
    pltpu.VMEM((D, FF), BF),
    pltpu.SemaphoreType.DMA((24,)),
)
UNIT = 2 * TOKENS * D * D
ATTEND = 2 * 3 * 1024 * 1024 * HEAD_DIM * 4


NEAR = {"x": NEAR_X, "y": NEAR_Y, "z": NEAR_Z}


def swaps(values, axes, side):
    return [swap(v, axis, side) for v, axis in zip(values, axes)]


def join(values, came, done=()):
    return list(
        run_kernel(
            join_kernel,
            values + came,
            [like(v, 2) for v in values],
            (pltpu.SemaphoreType.DMA((2 * len(values),)),),
            scalars=False,
            lying=True,
            done=done,
        )
    )


def gather_round(place, values, axes, done=()):
    pairs = join(values, swaps(values, axes, 1))
    far = swaps(pairs, axes, -1)
    return list(
        run_kernel(
            functools.partial(order_kernel, [NEAR[axis] for axis in axes]),
            [place] + pairs + far,
            [like(v, 4) for v in values],
            (pltpu.SemaphoreType.DMA((4 * len(values),)),),
            lying=True,
            done=done,
        )
    )


def padded(value):
    return jnp.pad(value.reshape(300, 128), ((0, 4), (0, 0)))


def weights_around(place, norm_params, attn_in, attn_out, mlp_in, mlp_out, done):
    norm_part = jnp.pad(jnp.swapaxes(norm_params, 1, 2), ((0, 0), (0, 0), (0, 124)))
    a = padded(jnp.concatenate([attn_in, attn_out, norm_part], -1))
    b = mlp_in.transpose(1, 0, 2).reshape(96, 384)
    c = mlp_out.transpose(2, 0, 1).reshape(96, 384)
    values = gather_round(place, [a, b, c], "zyx")
    a, b, c = gather_round(place, values, "xzy", done)
    a = a[:, :, :300].reshape(4, 4, 2, 6, ROW_A)
    layers = []
    for layer in range(2):
        al = a[:, :, layer].transpose(1, 0, 2, 3).reshape(96, ROW_A)
        bl, cl = run_kernel(
            functools.partial(layer_blocks_kernel, layer),
            [place, b, c],
            [shaped(192, 1536), shaped(768, 384)],
        )
        layers.append([al, bl, cl])
    return layers


LAST = "yxz"


def with_core(value):
    return fetch(value, "c", 1)


def halved(mine, came, done=()):
    outs = [like(v[0]) for v in mine for _ in range(2)]
    out = run_kernel(halve_kernel, list(mine) + list(came), outs, scalars=False, done=done)
    return list(out[0::2]), list(out[1::2])


def turn_rings(place, keep, came, later, done=()):
    halves = [like(v[0], 2) for v in keep for _ in range(2)]
    out = run_kernel(
        functools.partial(total_split_kernel, [NEAR[axis] for axis in later]),
        [place] + keep + came,
        halves,
        done=done,
    )
    return list(out[0::2]), list(out[1::2])


def total(keep, came):
    return (keep.astype(F32) + came.astype(F32)).astype(BF)


def gradients_home(place, a_layers, b_layers, c_layers, behind):
    b_mine, b_send, c_mine, c_send = run_kernel(
        both_layers_kernel,
        [place] + b_layers[0] + c_layers[0] + b_layers[1] + c_layers[1],
        [shaped(2, 4, 96, 384)] * 4,
    )
    mine, send = [b_mine, c_mine], [b_send, c_send]
    keep, send = halved(mine, swaps(send, "zx", -1), done=behind)
    came = swaps(send, "zx", 1)

    parts = [v.reshape(4, 4, 6, ROW_A).transpose(1, 0, 2, 3) for v in a_layers]
    a = jnp.stack(parts, 2).reshape(4, 4, 300, 128)
    a = jnp.pad(a, ((0, 0), (0, 0), (0, 4), (0, 0)))
    a_mine, a_send = run_kernel(
        functools.partial(split_kernel, [NEAR_X]), [place, a], [like(a[0], 2)] * 2
    )
    a_came = swap(a_send, "x", -1)
    mine, send = turn_rings(place, keep, came, "yy", done=[a_mine])
    came = swaps(send, "yy", -1)
    (a_keep,), (a_send,) = halved([a_mine], [a_came], done=[mine[0]])
    a_came = swap(a_send, "x", 1)
    keep, send = halved(mine, came, done=[a_keep])
    came = swaps(send, "yy", 1)
    parts = run_kernel(
        total_kernel, [a_keep, a_came], [like(a_keep[0])] * 4, scalars=False, done=[keep[0]]
    )
    b, c = [k.astype(F32) + v.astype(F32) for k, v in zip(keep, came)]
    a = parts[0].astype(F32)
    for part, step in zip(parts[1:], (-1, 1, 2)):
        a = a + fetch(part, "z", step).astype(F32)
    a = a[:300].reshape(2, 6, ROW_A)
    return (
        jnp.swapaxes(a[:, :, 4 * D : 4 * D + 4], 1, 2),
        a[:, :, : 3 * D],
        a[:, :, 3 * D : 4 * D],
        b.reshape(96, 2, 192).transpose(1, 0, 2),
        c.reshape(96, 2, 192).transpose(1, 2, 0),
    )


def body(inputs, lengths, norm_params, attn_in, attn_out, mlp_in, mlp_out, cotangent):
    wide = lax.axis_index("wide")
    narrow = lax.axis_index("narrow")
    core, low, z = wide % 2, (wide // 2) % 2, wide // 4
    x, high = narrow // 2, narrow % 2
    y = high * 2 + low
    length = lax.dynamic_index_in_dim(lengths[:, 0], high, 0, keepdims=False)
    near = [1 + (v + core) % 2 for v in (x, y, z)]
    place = jnp.stack([x, high, length] + near + [low]).astype(jnp.int32)

    def weights_of(pairs, far):
        return [[p, f, with_core(p), with_core(f)] for p, f in zip(pairs, far)]

    def behind(values, done):
        return list(after(values, done))

    slot = jnp.arange(D, dtype=jnp.int32)
    step = jnp.array([0, 1, 3, 2], jnp.int32)
    own_order = ((x + step[slot // 192]) % 4) * 192 + ((high + (slot // 96) % 2) % 2) * 96 + slot % 96
    row_core = (core + slot // 384) % 2
    row_y = (y + step[(slot // 96) % 4]) % 4
    row_z = (z + step[(slot // 24) % 4]) % 4
    row_x = (x + step[(slot // 6) % 4]) % 4
    row_order = 6 * index_of(row_z, row_y, row_core, row_x) + slot % 6
    pa = (own_order[:, None] == row_order[None, :]).astype(BF)
    po = (slot[:, None] == row_order[None, :]).astype(BF)
    p2 = (slot[:, None] == own_order[None, :]).astype(BF)

    def mine_and_other(values):
        mine = lax.dynamic_index_in_dim(values[:, 0], high, 0, keepdims=False)
        return mine, lax.dynamic_index_in_dim(values[:, 0], 1 - high, 0, keepdims=False)

    def in_own_order(mine, came):
        return dot(jnp.concatenate([mine, came], 0), p2)

    mine, other = mine_and_other(inputs)
    other = fetch(other, "y", 2)
    hidden = in_own_order(mine, other)
    around = weights_around(
        place, norm_params, attn_in, attn_out, mlp_in, mlp_out, [other]
    )
    grad_mine, grad_other = mine_and_other(cotangent)
    weights = [None, None]
    pairs = join(around[0], swaps(around[0], LAST, 1), [pa, po, p2, hidden])
    far = behind(swaps(pairs, LAST, -1), [])
    weights[0] = weights_of(pairs[:1] + behind(pairs[1:], far[:1]), far)
    records = []
    for layer in range(2):
        a_weights = weights[layer][0]
        a1p_keep, a1p_send, gains, *pieces = run_kernel(
            qkv_kernel,
            [place, hidden, pa] + a_weights,
            [shaped(TOKENS, 384), shaped(TOKENS, 384), shaped(8, D, dtype=F32)]
            + [shaped(576, TOKENS)] * 4,
            (
                pltpu.VMEM((D, 3 * D), BF),
                pltpu.VMEM((D, 128), BF),
                pltpu.VMEM((3 * D, TOKENS), BF),
                pltpu.SemaphoreType.DMA((16,)),
            ),
            flops=4 * UNIT,
            any_count=4,
            done=[weights[layer][n][1] for n in (1, 2)],
        )
        cores = [v for part in weights[layer][1:] for v in part[2:]]
        pieces = behind(pieces, [cores[0], cores[2]])
        turned = exchange_four(pieces)
        if layer == 0:
            held = list(after(around[1], turned[1:]))
            first = swaps(held, LAST, 1)
        else:
            (grad_other,) = after([grad_other], turned[1:])
            grad_other = fetch(grad_other, "y", 2)
        *mixed, sums = run_kernel(
            attend_kernel,
            [place] + turned,
            [shaped(GROUP, TOKENS)] * 4 + [shaped(3, 1024, dtype=F32)],
            (pltpu.VMEM((1024, TOKENS), F32),),
            flops=ATTEND,
            done=cores,
        )
        if layer == 0:
            mixed = list(after(mixed, first))
        back = exchange_four(mixed)
        if layer == 0:
            pairs = list(after(join(held, first), back[1:]))
            far = behind(swaps(pairs, LAST, -1), [])
        h1, following, slope, forward_send, op_keep, act_keep = run_kernel(
            mlp_kernel,
            [place, hidden] + back + [a1p_send, po, p2, gains] + sum(weights[layer], []),
            [
                shaped(TOKENS, D, dtype=F32),
                shaped(TOKENS, D, dtype=F32),
                shaped(TOKENS, FF),
                shaped(TOKENS, FF),
                shaped(TOKENS, 384),
                shaped(TOKENS, 1536),
            ],
            MLP_SCRATCH,
            flops=11 * UNIT,
            any_count=12,
        )
        records.append(
            (hidden, a1p_keep, gains, turned, mixed, sums, h1, slope, forward_send, op_keep, act_keep)
        )
        if layer == 0:
            far = behind(far, [following])
            weights[1] = weights_of(pairs[:2] + behind(pairs[2:], [following]), far)
        hidden = following

    def leave(values, ahead=()):
        values = jnp.dot(
            values, p2.astype(F32).T, precision=lax.Precision.HIGHEST, preferred_element_type=F32
        )
        far = values[128:]
        if ahead:
            (far,) = after([far], list(ahead))
        else:
            far = far.astype(BF)
        return values[:128], fetch(far, "y", 2)

    def arrange(own, came):
        return jnp.stack(
            [jnp.where(high == 0, own, came), jnp.where(high == 0, came, own)]
        )[:, None]

    def back_to_qkv(layer, grad, done):
        hidden, a1p_keep, gains, turned, mixed, sums, h1, slope = records[layer][:8]
        return run_kernel(
            mlp_back_kernel,
            [place, grad, slope, h1, gains, p2, po] + sum(weights[layer], []),
            [
                shaped(TOKENS, D, dtype=F32),
                shaped(TOKENS, FF),
                shaped(TOKENS, 1536),
                shaped(8, D, dtype=F32),
            ]
            + [shaped(GROUP, TOKENS)] * 4,
            MLP_SCRATCH,
            flops=11 * UNIT,
            any_count=12,
            done=done,
        )

    def mlp_gradients(forward, back, act_keep, dpre_keep):
        return run_kernel(
            mlp_grad_kernel,
            [
                place,
                (forward[0], 768, 1),
                (forward[1], 768, 1),
                act_keep,
                (forward[1], 1536, 1),
                dpre_keep,
                (back[1], 1536, 0),
                (back[0], 768, 2),
                (back[1], 768, 2),
            ],
            [shaped(2, 192, 1536)] * 2 + [shaped(2, 768, 384)] * 2,
            flops=8 * UNIT,
        )

    def attend_back(layer, grad_mixed, done):
        turned, mixed, sums = records[layer][3:6]
        return run_kernel(
            attend_back_kernel,
            [place] + turned + grad_mixed + mixed + [sums],
            [shaped(576, TOKENS)] * 4,
            (pltpu.VMEM((1024, TOKENS), F32),),
            flops=3 * ATTEND,
            done=done,
        )

    def qkv_back(layer, grad_pieces, g1, norm2, done):
        hidden, gains = records[layer][0], records[layer][2]
        return run_kernel(
            qkv_back_kernel,
            [place] + grad_pieces + [hidden, g1, gains, pa, norm2] + weights[layer][0],
            [shaped(TOKENS, D, dtype=F32), shaped(3 * D, TOKENS), shaped(8, D, dtype=F32)],
            (pltpu.VMEM((D, 3 * D), BF), pltpu.SemaphoreType.DMA((8,))),
            flops=5 * UNIT,
            any_count=4,
            done=done,
        )

    def attn_gradients(forward, back, a1p_keep, op_keep, dqkv, norms, done=()):
        return run_kernel(
            attn_grad_kernel,
            [
                place,
                a1p_keep,
                (forward[1], 384, 0),
                op_keep,
                (forward[1], 384, 1),
                (back[0], 768, 3),
                (back[1], 768, 3),
                dqkv[0],
                dqkv[1],
                norms[0],
                norms[1],
                pa,
            ],
            [shaped(2, 96, ROW_A)] * 2,
            flops=4 * UNIT,
            done=done,
        )

    grad = in_own_order(grad_mine, grad_other)

    forward_send, op_keep, act_keep = records[1][8:]
    a1p_keep = records[1][1]
    forward = forward_send, with_core(forward_send)
    g1, back_send, dpre_keep, norm2, *pieces = back_to_qkv(1, grad, [])
    grad_mixed = exchange_four(pieces)
    back = back_send, with_core(back_send)
    b1_mine, b1_send, c1_mine, c1_send = mlp_gradients(forward, back, act_keep, dpre_keep)
    b1_send, c1_send = after([b1_send, c1_send], grad_mixed[1:])
    b1_came, c1_came = swap(b1_send, "x", -1), swap(c1_send, "z", -1)
    outputs = leave(hidden, grad_mixed[1:])
    pieces = attend_back(1, grad_mixed, [b1_mine])
    pieces = after(pieces, [outputs[1], b1_came, c1_came])
    grad_pieces = exchange_four(pieces)
    (b1_keep, c1_keep), (b1_send, c1_send) = halved([b1_mine, c1_mine], [b1_came, c1_came])
    b1_send, c1_send = after([b1_send, c1_send], grad_pieces[1:])
    b1_came, c1_came = swap(b1_send, "x", 1), swap(c1_send, "z", 1)
    grad, dqkv, norms = qkv_back(1, grad_pieces, g1, norm2, [b1_keep])
    dqkv, norms = (dqkv, with_core(dqkv)), (norms, with_core(norms))

    forward_send0, op_keep0, act_keep0 = records[0][8:]
    a1p_keep0 = records[0][1]
    forward0 = forward_send0, with_core(forward_send0)
    g1, back_send0, dpre_keep0, norm2, *pieces = back_to_qkv(0, grad, [b1_came, c1_came])
    pieces = after(pieces, [dqkv[1], norms[1]])
    grad_mixed = exchange_four(pieces)
    back0 = back_send0, with_core(back_send0)
    b0_mine, b0_send, c0_mine, c0_send = mlp_gradients(forward0, back0, act_keep0, dpre_keep0)
    b0_send, c0_send = after([b0_send, c0_send], grad_mixed[1:])
    b0_came, c0_came = swap(b0_send, "x", -1), swap(c0_send, "z", -1)
    pieces = attend_back(0, grad_mixed, [b0_mine])
    pieces = after(pieces, [b0_came, c0_came])
    (op_keep,) = after([op_keep], pieces[:1])
    grad_pieces = exchange_four(pieces)
    a1_mine, a1_send = attn_gradients(forward, back, a1p_keep, op_keep, dqkv, norms)
    (a1_send,) = after([a1_send], grad_pieces[1:])
    a1_came = swap(a1_send, "y", -1)
    grad, dqkv, norms = qkv_back(0, grad_pieces, g1, norm2, [a1_mine])
    dqkv, norms = (dqkv, with_core(dqkv)), (norms, with_core(norms))
    (b0_keep, c0_keep, a1_keep), (b0_send, c0_send, a1_send) = halved(
        [b0_mine, c0_mine, a1_mine], [b0_came, c0_came, a1_came], [grad]
    )
    b0_came, c0_came = swap(b0_send, "x", 1), swap(c0_send, "z", 1)
    a1_came = swap(a1_send, "y", 1)
    grad_own, grad_far = leave(grad)
    a0_mine, a0_send = attn_gradients(
        forward0, back0, a1p_keep0, op_keep0, dqkv, norms, [b0_keep]
    )
    (a0_send,) = after([a0_send], [b0_came, c0_came, a1_came, grad_far])
    a0_came = swap(a0_send, "y", -1)
    (a0_keep,), (a0_send,) = halved([a0_mine], [a0_came])
    a0_came = swap(a0_send, "y", 1)
    weight_grads = gradients_home(
        place,
        [total(a0_keep, a0_came), total(a1_keep, a1_came)],
        [[b0_keep, b0_came], [b1_keep, b1_came]],
        [[c0_keep, c0_came], [c1_keep, c1_came]],
        [a0_keep],
    )
    grad_inputs = grad_own, grad_far.astype(F32)
    return (arrange(*outputs), arrange(*grad_inputs)) + weight_grads


def solution(mesh):
    in_specs = (
        P(None, "wide", "narrow", None),
        P(None, "wide"),
        P(None, None, ("wide", "narrow")),
        P(None, ("wide", "narrow"), None),
        P(None, ("wide", "narrow"), None),
        P(None, "narrow", "wide"),
        P(None, "wide", "narrow"),
        P(None, "wide", "narrow", None),
    )
    out_specs = (
        P(None, "wide", "narrow", None),
        P(None, "wide", "narrow", None),
        P(None, None, ("wide", "narrow")),
        P(None, ("wide", "narrow"), None),
        P(None, ("wide", "narrow"), None),
        P(None, "narrow", "wide"),
        P(None, "wide", "narrow"),
    )
    return jax.shard_map(body, mesh=mesh, in_specs=in_specs, out_specs=out_specs, check_vma=False)
```

```python
import functools

import jax
import jax.numpy as jnp
from jax import lax
from jax.experimental import pallas as pl
from jax.experimental.pallas import tpu as pltpu
from jax.sharding import PartitionSpec as P

D = 768
FF = 3072
HEAD_DIM = 64
GROUP = 192
TOKENS = 256
SPAN = 1024
SPAN_BACK = 512
EPS = 1e-06
ROOT_HALF = 0.7071067811865476
INV_ROOT_TWO_PI = 0.3989422804014327
ROW_A = 3200
BF = jnp.bfloat16
F32 = jnp.float32
AXES = ("wide", "narrow")
VMEM_LIMIT = 56 * 1024 * 1024


def index_of(z, y, c, x):
    return ((z * 2 + y % 2) * 2 + c) * 8 + x * 2 + y // 2


def everywhere():
    for z in range(4):
        for y in range(4):
            for c in range(2):
                for x in range(4):
                    yield {"z": z, "y": y, "c": c, "x": x}


def fetch(value, axis, step):
    pairs = []
    for here in everywhere():
        there = dict(here)
        there[axis] = (here[axis] + step) % (2 if axis == "c" else 4)
        pairs.append((index_of(**there), index_of(**here)))
    return lax.ppermute(value, AXES, pairs)


def swap(value, axis, side):
    pairs = []
    for here in everywhere():
        step = side if (here[axis] + here["c"]) % 2 == 0 else -side
        there = dict(here)
        there[axis] = (here[axis] + step) % 4
        pairs.append((index_of(**here), index_of(**there)))
    return lax.ppermute(value, AXES, pairs)


def exchange_four(pieces):
    return [pieces[0]] + [fetch(pieces[4 - k], "x", k) for k in (1, 2, 3)]


def dot(left, right, over_left=1, over_right=0):
    return lax.dot_general(
        left, right, (((over_left,), (over_right,)), ((), ())), preferred_element_type=F32
    )


def dot_two(left, right, over_left=1, over_right=0):
    high = left.astype(BF)
    low = (left - high.astype(F32)).astype(BF)
    return dot(high, right, over_left, over_right) + dot(low, right, over_left, over_right)


def normed(values):
    average = jnp.mean(values, -1, keepdims=True)
    centred = values - average
    spread = jnp.mean(centred * centred, -1, keepdims=True)
    scale = lax.rsqrt(spread + EPS)
    return centred * scale, scale


def norm_back(grad, values, gain_row):
    z, scale = normed(values)
    dz = grad * gain_row
    out = (
        dz - jnp.mean(dz, -1, keepdims=True) - z * jnp.mean(dz * z, -1, keepdims=True)
    ) * scale
    gain_grad = jnp.sum(grad * z, 0, keepdims=True)
    offset_grad = jnp.sum(grad, 0, keepdims=True)
    return out, gain_grad, offset_grad


def two_rows(first, second):
    return jnp.concatenate([first, second, jnp.zeros((6, D), F32)], 0)


def group_start(x, k, base=0):
    return pl.multiple_of(base + lax.rem(x + k, 4) * GROUP, GROUP)


def start_copies(pairs, sems):
    copies = [
        pltpu.make_async_copy(source, target, sems.at[i])
        for i, (source, target) in enumerate(pairs)
    ]
    for copy in copies:
        copy.start()
    return copies


def wait_copies(copies):
    for copy in copies:
        copy.wait()


X, HIGH, LENGTH, NEAR_X, NEAR_Y, NEAR_Z, LOW = range(7)


def weight_blocks(refs, near):
    pair, far, core_pair, core_far = refs
    return [
        (pair, 0, 0, 0),
        (pair, 1, 0, near),
        (far, 0, 0, 3 - near),
        (far, 1, 0, 3),
        (core_pair, 0, 1, 0),
        (core_pair, 1, 1, 3 - near),
        (core_far, 0, 1, near),
        (core_far, 1, 1, 3),
    ]


def at_rows(core, spot, rows):
    return pl.ds(pl.multiple_of((core * 4 + spot) * rows, rows), rows)


def qkv_kernel(place_ref, h_ref, pa_ref, *refs):
    blocks = weight_blocks(refs[:4], place_ref[NEAR_Y])
    a1p_keep, a1p_send, gains_ref = refs[4:7]
    out_refs = refs[7:11]
    win, table, turned, sems = refs[11:]
    norm_copies = start_copies(
        [
            (r.at[i, :, pl.ds(FF, 128)], table.at[at_rows(core, spot, 96)])
            for r, i, core, spot in blocks
        ],
        sems.at[pl.ds(0, 8)],
    )
    win_copies = start_copies(
        [
            (r.at[i, :, pl.ds(0, 3 * D)], win.at[at_rows(core, spot, 96)])
            for r, i, core, spot in blocks
        ],
        sems.at[pl.ds(8, 8)],
    )
    z, _ = normed(h_ref[...])
    wait_copies(norm_copies)
    gains = dot(table[...], pa_ref[...], 0, 1)[0:8]
    gains_ref[...] = gains
    a1 = (z * gains[0:1] + gains[1:2]).astype(BF)
    a1p = dot(a1, pa_ref[...]).astype(BF)
    a1p_keep[...] = a1p[:, :384]
    a1p_send[...] = a1p[:, 384:]
    wait_copies(win_copies)
    for c in range(3):
        part = dot(a1p, win[:, c * D : (c + 1) * D])
        if c == 0:
            part = part * HEAD_DIM ** (-0.5)
        turned[c * D : (c + 1) * D, :] = part.astype(BF).T
    x = place_ref[X]
    for k in range(4):
        for c in range(3):
            out_refs[k][c * GROUP : (c + 1) * GROUP, :] = turned[
                pl.ds(group_start(x, k, c * D), GROUP), :
            ]


def mask_row(place_ref):
    x, yh, length = place_ref[X], place_ref[HIGH], place_ref[LENGTH]
    rows = []
    for k in range(4):
        for half in range(2):
            start = lax.rem(x + k, 4) * 256 + lax.rem(yh + half, 2) * 128
            slot = start + lax.broadcasted_iota(jnp.int32, (1, 128), 1)
            rows.append(jnp.where(slot < length, 0.0, -1e30))
    return jnp.concatenate(rows, 1)


def side_by_side(refs, start):
    return jnp.concatenate([r[start : start + HEAD_DIM, :] for r in refs], 1)


def with_rows(block, rows):
    count, width = len(rows), block.shape[1]
    tail = jnp.concatenate(rows + [jnp.zeros((16 - count, width), F32)], 0).astype(BF)
    return jnp.concatenate([block, tail], 0)


def in_three(row):
    high = row.astype(BF).astype(F32)
    middle = (row - high).astype(BF).astype(F32)
    return [high, middle, row - high - middle]


def attend_kernel(place_ref, t0, t1, t2, t3, u0, u1, u2, u3, sums_ref):
    t_refs, u_refs = (t0, t1, t2, t3), (u0, u1, u2, u3)
    mask = mask_row(place_ref)
    count = SPAN // TOKENS
    ones = jnp.ones((1, SPAN), F32)
    for j in range(3):
        keys = with_rows(side_by_side(t_refs, GROUP + j * HEAD_DIM), [mask]).T
        values_t = side_by_side(t_refs, 2 * GROUP + j * HEAD_DIM)
        rows = slice(j * HEAD_DIM, (j + 1) * HEAD_DIM)
        for b in range(0, 4, count):
            query_t = side_by_side(t_refs[b : b + count], j * HEAD_DIM)
            scores = dot(keys, with_rows(query_t, [ones]))
            peak = jnp.max(scores, 0, keepdims=True)
            expont = jnp.exp(scores - peak)
            total = jnp.sum(expont, 0, keepdims=True)
            mixed = (dot(values_t, expont.astype(BF)) / total).astype(BF)
            for n in range(count):
                u_refs[b + n][rows, :] = mixed[:, n * TOKENS : (n + 1) * TOKENS]
            sums_ref[j : j + 1, b * TOKENS : (b + count) * TOKENS] = peak + jnp.log(total)


def attend_back_kernel(place_ref, *refs):
    t_refs, g_refs, u_refs = refs[0:4], refs[4:8], refs[8:12]
    sums_ref = refs[12]
    out_refs = refs[13:17]
    mask = mask_row(place_ref)
    count = SPAN_BACK // TOKENS
    ones = jnp.ones((1, SPAN_BACK), F32)
    one_row = jnp.ones((1, 4 * TOKENS), F32)
    for j in range(3):
        keys_t = side_by_side(t_refs, GROUP + j * HEAD_DIM)
        keys = with_rows(keys_t, [mask] + [one_row] * 3).T
        values = with_rows(side_by_side(t_refs, 2 * GROUP + j * HEAD_DIM), [one_row] * 3).T
        grad_keys = jnp.zeros((4 * TOKENS, HEAD_DIM), F32)
        grad_values = jnp.zeros((4 * TOKENS, HEAD_DIM), F32)
        rows = slice(j * HEAD_DIM, (j + 1) * HEAD_DIM)
        for b in range(0, 4, count):
            query_t = side_by_side(t_refs[b : b + count], j * HEAD_DIM)
            grad_t = side_by_side(g_refs[b : b + count], j * HEAD_DIM)
            mixed_t = side_by_side(u_refs[b : b + count], j * HEAD_DIM)
            sums = sums_ref[j : j + 1, b * TOKENS : (b + count) * TOKENS]
            delta = jnp.sum(grad_t.astype(F32) * mixed_t.astype(F32), 0, keepdims=True)
            probs = jnp.exp(dot(keys, with_rows(query_t, [ones] + in_three(-sums))))
            grad_probs = dot(values, with_rows(grad_t, in_three(-delta)))
            grad_scores = (probs * grad_probs).astype(BF)
            grad_values = grad_values + dot(probs.astype(BF), grad_t, 1, 1)
            grad_keys = grad_keys + dot(grad_scores, query_t, 1, 1)
            grad_query = (dot(keys_t, grad_scores) * HEAD_DIM ** (-0.5)).astype(BF)
            for n in range(count):
                out_refs[b + n][rows, :] = grad_query[:, n * TOKENS : (n + 1) * TOKENS]
        grad_keys = grad_keys.astype(BF).T
        grad_values = grad_values.astype(BF).T
        for b in range(4):
            columns = slice(b * TOKENS, (b + 1) * TOKENS)
            start = GROUP + j * HEAD_DIM
            out_refs[b][start : start + HEAD_DIM, :] = grad_keys[:, columns]
            start = 2 * GROUP + j * HEAD_DIM
            out_refs[b][start : start + HEAD_DIM, :] = grad_values[:, columns]


def mlp_copies(place_ref, refs, wout, w1, w2, sems):
    out_copies = start_copies(
        [
            (r.at[i, :, pl.ds(3 * D, D)], wout.at[at_rows(core, spot, 96)])
            for r, i, core, spot in weight_blocks(refs[0:4], place_ref[NEAR_Y])
        ],
        sems.at[pl.ds(0, 8)],
    )
    first_copies = start_copies(
        [
            (ref.at[k], w1.at[core, pl.ds(192 * k, 192)])
            for core, ref in enumerate(refs[4:6])
            for k in range(4)
        ],
        sems.at[pl.ds(8, 8)],
    )
    second_copies = start_copies(
        [
            (ref.at[k], w2.at[:, pl.ds((core * 4 + k) * 384, 384)])
            for core, ref in enumerate(refs[6:8])
            for k in range(4)
        ],
        sems.at[pl.ds(16, 8)],
    )
    return out_copies, first_copies, second_copies


def mlp_forward(place_ref, h, pieces, a1p_send, po_ref, p2_ref, gains_ref, slope_ref, outs, parts):
    send_ref, op_keep, act_keep = outs
    turned, wout, w1, w2, out_copies, first_copies, second_copies = parts
    send_ref[:, 0:384] = a1p_send[...]
    x = place_ref[X]
    for k, piece in enumerate(pieces):
        turned[pl.ds(group_start(x, k), GROUP), :] = piece[...]
    op = dot(turned[...], po_ref[...], 0, 0).astype(BF)
    op_keep[...] = op[:, :384]
    send_ref[:, 384:768] = op[:, 384:]
    wait_copies(out_copies)
    h1 = h + dot_two(dot(op, wout[...]), p2_ref[...])
    z, _ = normed(h1)
    a2 = (z * gains_ref[2:3] + gains_ref[3:4]).astype(BF)
    send_ref[:, 768:1536] = a2
    wait_copies(first_copies)
    total = h1
    for half in range(2):
        pre = dot(a2, w1[half])
        below = 0.5 * (1.0 + lax.erf(pre * ROOT_HALF))
        act = (pre * below).astype(BF)
        slope = below + pre * (jnp.exp(-0.5 * pre * pre) * INV_ROOT_TWO_PI)
        columns = slice(half * 1536, (half + 1) * 1536)
        if half == 0:
            act_keep[...] = act
            wait_copies(second_copies)
        else:
            send_ref[:, 1536:] = act
        slope_ref[:, columns] = slope.astype(BF)
        total = total + dot(act, w2[:, columns], 1, 1)
    return h1, total


def mlp_backward(place_ref, grad, h1, gains_ref, p2_ref, po_ref, slope_ref, outs, parts):
    send_ref, dpre_keep, norm_ref, out_refs = outs
    turned, wout, w1, w2, out_copies, first_copies, second_copies = parts
    grad_low = grad.astype(BF)
    send_ref[:, 1536:2304] = grad_low
    wait_copies(second_copies)
    grad_a2 = jnp.zeros((TOKENS, D), F32)
    for half in range(2):
        columns = slice(half * 1536, (half + 1) * 1536)
        grad_act = dot(grad_low, w2[:, columns])
        dpre = (grad_act * slope_ref[:, columns].astype(F32)).astype(BF)
        if half == 0:
            dpre_keep[...] = dpre
            wait_copies(first_copies)
        else:
            send_ref[:, 0:1536] = dpre
        grad_a2 = grad_a2 + dot(dpre, w1[half], 1, 1)
    dv, gain_grad, offset_grad = norm_back(grad_a2, h1, gains_ref[2:3])
    norm_ref[...] = two_rows(gain_grad, offset_grad)
    g1 = grad + dv
    g1b = dot(g1.astype(BF), p2_ref[...], 1, 1).astype(BF)
    send_ref[:, 2304:] = g1b
    wait_copies(out_copies)
    grad_op = dot(g1b, wout[...], 1, 1).astype(BF)
    turned[...] = dot(po_ref[...], grad_op, 1, 1).astype(BF)
    x = place_ref[X]
    for k in range(4):
        out_refs[k][...] = turned[pl.ds(group_start(x, k), GROUP), :]
    return g1


def mlp_kernel(place_ref, h_ref, u0, u1, u2, u3, a1p_send, po_ref, p2_ref, gains_ref, *refs):
    h1_ref, next_ref, slope_ref, send_ref, op_keep, act_keep = refs[8:14]
    turned, wout, w1, w2, sems = refs[14:]
    copies = mlp_copies(place_ref, refs[:8], wout, w1, w2, sems)
    h1_ref[...], next_ref[...] = mlp_forward(
        place_ref, h_ref[...], (u0, u1, u2, u3), a1p_send, po_ref, p2_ref, gains_ref, slope_ref,
        (send_ref, op_keep, act_keep), (turned, wout, w1, w2) + copies,
    )


def mlp_turn_kernel(
    place_ref, h_ref, u0, u1, u2, u3, a1p_send, po_ref, p2_ref, gains_ref, g_ref, *refs
):
    next_ref, forward_send, op_keep, act_keep, g1_ref, back_send, dpre_keep, norm_ref = refs[8:16]
    out_refs = refs[16:20]
    turned, wout, w1, w2, sems, slope_ref = refs[20:]
    copies = mlp_copies(place_ref, refs[:8], wout, w1, w2, sems)
    h1, next_ref[...] = mlp_forward(
        place_ref, h_ref[...], (u0, u1, u2, u3), a1p_send, po_ref, p2_ref, gains_ref, slope_ref,
        (forward_send, op_keep, act_keep), (turned, wout, w1, w2) + copies,
    )
    g1_ref[...] = mlp_backward(
        place_ref, g_ref[...], h1, gains_ref, p2_ref, po_ref, slope_ref,
        (back_send, dpre_keep, norm_ref, out_refs), (turned, wout, w1, w2, (), (), ()),
    )


def qkv_back_into_mlp_kernel(
    place_ref, d0, d1, d2, d3, h_ref, g1_ref, gains_ref, pa_ref, norm2_ref,
    slope_ref, h1_ref, gains0_ref, p2_ref, po_ref, *refs,
):
    dqkv_ref, next_ref, back_send, dpre_keep, below_ref = refs[12:17]
    out_refs = refs[17:21]
    turned, wout, w1, w2, sems, win, win_sems = refs[21:]
    win_copies = win_start(place_ref, refs[:4], win, win_sems)
    copies = mlp_copies(place_ref, refs[4:12], wout, w1, w2, sems)
    grad = qkv_backward(
        place_ref, (d0, d1, d2, d3), h_ref, g1_ref, gains_ref, pa_ref, norm2_ref,
        dqkv_ref, win, win_copies,
    )
    next_ref[...] = mlp_backward(
        place_ref, grad, h1_ref[...], gains0_ref, p2_ref, po_ref, slope_ref,
        (back_send, dpre_keep, below_ref, out_refs), (turned, wout, w1, w2) + copies,
    )


def both_cores(first_ref, second_ref):
    return jnp.concatenate([first_ref[...], second_ref[...]], 0)


def store_blocks(near, mine, send, columns, blocks):
    mine[0, :, columns] = blocks[0]
    send[1, :, columns] = blocks[3]

    @pl.when(near == 1)
    def _():
        mine[1, :, columns] = blocks[1]
        send[0, :, columns] = blocks[2]

    @pl.when(near == 2)
    def _():
        mine[1, :, columns] = blocks[2]
        send[0, :, columns] = blocks[1]


def mlp_grad_kernel(
    place_ref, a2_0, a2_1, act_0, act_1, dpre_0, dpre_1, gb_0, gb_1,
    first_mine, first_send, second_mine, second_send,
):
    a2 = both_cores(a2_0, a2_1)
    grad_low = both_cores(gb_0, gb_1)
    dpre = both_cores(dpre_0, dpre_1)
    for part in range(2):
        columns = slice(part * 768, part * 768 + 768)
        value = dot(a2, dpre[:, columns], 0, 0).astype(BF)
        blocks = [value[192 * k : 192 * k + 192] for k in range(4)]
        store_blocks(place_ref[NEAR_X], first_mine, first_send, columns, blocks)
    act = both_cores(act_0, act_1)
    blocks = [
        dot(grad_low, act[:, 384 * k : 384 * k + 384], 0, 0).astype(BF) for k in range(4)
    ]
    store_blocks(place_ref[NEAR_Z], second_mine, second_send, slice(0, 384), blocks)


def win_start(place_ref, refs, win, sems):
    return start_copies(
        [
            (r.at[i, :, pl.ds(0, 3 * D)], win.at[at_rows(core, spot, 96)])
            for r, i, core, spot in weight_blocks(refs, place_ref[NEAR_Y])
        ],
        sems,
    )


def qkv_backward(
    place_ref, pieces, h_ref, g1_ref, gains_ref, pa_ref, norm2_ref, dqkv_ref, win, copies
):
    x = place_ref[X]
    for k, piece in enumerate(pieces):
        for c in range(3):
            dqkv_ref[pl.ds(group_start(x, k, c * D), GROUP), :] = piece[
                c * GROUP : (c + 1) * GROUP, :
            ]
    wait_copies(copies)
    turned = dot(win[...], dqkv_ref[0 : 3 * D, :])
    grad_a1 = dot_two(turned, pa_ref[...], 0, 1)
    dv, gain_grad, offset_grad = norm_back(grad_a1, h_ref[...], gains_ref[0:1])
    norms = jnp.concatenate([gain_grad, offset_grad, norm2_ref[0:2], jnp.zeros((4, D), F32)], 0)
    high = norms.astype(BF)
    norms = jnp.concatenate([high, (norms - high.astype(F32)).astype(BF)], 0)
    for c in range(3):
        dqkv_ref[3 * D + 16 * c : 3 * D + 16 * c + 16, :] = norms[:, 256 * c : 256 * c + 256]
    return g1_ref[...] + dv


def qkv_back_kernel(
    place_ref, d0, d1, d2, d3, h_ref, g1_ref, gains_ref, pa_ref, norm2_ref, *refs
):
    next_ref, dqkv_ref, win, sems = refs[4:]
    copies = win_start(place_ref, refs[:4], win, sems)
    next_ref[...] = qkv_backward(
        place_ref, (d0, d1, d2, d3), h_ref, g1_ref, gains_ref, pa_ref, norm2_ref,
        dqkv_ref, win, copies,
    )


def attn_grad_kernel(
    place_ref, a1p_0, a1p_1, op_0, op_1, g1b_0, g1b_1, dqkv_0, dqkv_1, pa_ref, mine, send
):
    near = place_ref[NEAR_Y]
    norms = jnp.zeros((8, D), F32)
    for ref in (dqkv_0, dqkv_1):
        pair = [ref[3 * D + 16 * c : 3 * D + 16 * c + 16, :].astype(F32) for c in range(3)]
        pair = jnp.concatenate(pair, 1)
        norms = norms + pair[0:8] + pair[8:16]
    norms = dot_two(norms, pa_ref[:, 0:384])
    norms = jnp.concatenate([norms, jnp.zeros((120, 384), F32)], 0).T.astype(BF)
    a1p = both_cores(a1p_0, a1p_1)
    for c in range(5):
        columns = slice(c * D, min((c + 1) * D, ROW_A))
        if c < 3:
            dqkv = jnp.concatenate(
                [dqkv_0[c * D : (c + 1) * D, :], dqkv_1[c * D : (c + 1) * D, :]], 1
            )
            value = dot(a1p, dqkv, 0, 1).astype(BF)
        elif c == 3:
            value = dot(both_cores(op_0, op_1), both_cores(g1b_0, g1b_1), 0, 0).astype(BF)
        else:
            value = norms
        blocks = [value[96 * k : 96 * k + 96] for k in range(4)]
        store_blocks(near, mine, send, columns, blocks)


def join_kernel(*refs):
    count = (len(refs) - 1) // 3
    pairs = []
    for own, came, out in zip(refs[:count], refs[count : 2 * count], refs[2 * count : -1]):
        pairs += [(own, out.at[0]), (came, out.at[1])]
    wait_copies(start_copies(pairs, refs[-1]))


def order_kernel(spots, place_ref, *refs):
    count = len(spots)
    pairs = []
    for spot, pair, far, out in zip(
        spots, refs[:count], refs[count : 2 * count], refs[2 * count : -1]
    ):
        near = place_ref[spot]
        pairs += [
            (pair.at[0], out.at[0]),
            (pair.at[1], out.at[near]),
            (far.at[0], out.at[3 - near]),
            (far.at[1], out.at[3]),
        ]
    wait_copies(start_copies(pairs, refs[-1]))


def layer_blocks_kernel(
    layer, place_ref, b_pair, c_pair, b_far, c_far, first_ref, second_ref
):
    middle = 1 + place_ref[LOW]
    near_z = place_ref[NEAR_Z]
    straight = place_ref[NEAR_Y] == middle
    part = slice(layer * 192, layer * 192 + 192)
    b_slots = ((b_pair, 0, 0), (b_pair, 1, near_z), (b_far, 0, 3 - near_z), (b_far, 1, 3))
    for high in range(2):
        one, two = (0, middle) if high == 0 else (3, 3 - middle)
        for ref, i, spot in b_slots:
            both = [ref[i, one][:, part], ref[i, two][:, part]]
            first_ref[
                high * 96 : high * 96 + 96, pl.ds(pl.multiple_of(spot * 384, 384), 384)
            ] = jnp.concatenate(both, 1)
        for k in range(4):
            outer = c_pair[0, k] if high == 0 else c_far[1, k]
            near, other = c_pair[1, k], c_far[0, k]
            if high == 0:
                inner = jnp.where(straight, near, other)
            else:
                inner = jnp.where(straight, other, near)
            start = (2 * k + high) * 96
            second_ref[start : start + 96, :] = jnp.concatenate(
                [outer[:, part], inner[:, part]], 1
            )


def both_layers_kernel(place_ref, *refs):
    b0, b0_came, c0, c0_came, b1, b1_came, c1, c1_came = refs[:8]
    b_mine, b_send, c_mine, c_send = refs[8:]
    middle = 1 + place_ref[LOW]
    near_z, near_x = place_ref[NEAR_Z], place_ref[NEAR_X]

    def put(mine, send, near, spot, index, value):
        if isinstance(spot, int) and spot == 0:
            mine[0, index] = value
        elif isinstance(spot, int) and spot == 3:
            send[1, index] = value
        else:

            @pl.when(near == spot)
            def _():
                mine[1, index] = value

            @pl.when(near != spot)
            def _():
                send[0, index] = value

    for high in range(2):
        for k in range(4):
            rows, columns = slice(high * 96, high * 96 + 96), slice(k * 384, k * 384 + 384)
            b_parts = [
                total_of(b0[rows, columns], b0_came[rows, columns]),
                total_of(b1[rows, columns], b1_came[rows, columns]),
            ]
            rows = slice((2 * k + high) * 96, (2 * k + high) * 96 + 96)
            c_parts = [
                total_of(c0[rows, :], c0_came[rows, :]),
                total_of(c1[rows, :], c1_came[rows, :]),
            ]
            for part in range(2):
                if part == 0:
                    spot = 0 if high == 0 else 3
                else:
                    spot = middle if high == 0 else 3 - middle
                columns = slice(part * 192, part * 192 + 192)
                value = jnp.concatenate([v[:, columns] for v in b_parts], 1)
                put(b_mine, b_send, near_z, k, spot, value)
                value = jnp.concatenate([v[:, columns] for v in c_parts], 1)
                put(c_mine, c_send, near_x, k, spot, value)


def split_kernel(spots, place_ref, *refs):
    count = len(spots)
    for n, spot in enumerate(spots):
        near = place_ref[spot]
        value, mine, send = refs[n], refs[count + 2 * n], refs[count + 2 * n + 1]
        mine[0] = value[0]
        mine[1] = value[near]
        send[0] = value[3 - near]
        send[1] = value[3]


def total_of(first, second):
    return (first.astype(F32) + second.astype(F32)).astype(BF)


def halve_kernel(*refs):
    count = len(refs) // 4
    for n in range(count):
        mine, came = refs[n], refs[count + n]
        keep, send = refs[2 * count + 2 * n], refs[2 * count + 2 * n + 1]
        keep[...] = total_of(mine[0], came[0])
        send[...] = total_of(mine[1], came[1])


def total_pair_kernel(b_keep, b_came, c_keep, c_came, *out_refs):
    for k, out in enumerate(out_refs):
        out[0] = total_of(b_keep[k], b_came[k])
        out[1] = total_of(c_keep[k], c_came[k])


def total_kernel(keep, came, *out_refs):
    for k, out in enumerate(out_refs):
        out[...] = total_of(keep[k], came[k])


def nothing_kernel(*refs):
    pass


def after(values, done):
    anywhere = pl.BlockSpec(memory_space=pl.ANY)
    return pl.pallas_call(
        nothing_kernel,
        out_shape=tuple(jax.ShapeDtypeStruct(v.shape, v.dtype) for v in values),
        in_specs=[anywhere] * (len(values) + len(done)),
        out_specs=tuple(anywhere for _ in values),
        input_output_aliases={i: i for i in range(len(values))},
    )(*values, *done)


def shaped(*shape, dtype=BF):
    return jax.ShapeDtypeStruct(shape, dtype)


def like(value, *lead):
    return jax.ShapeDtypeStruct(tuple(lead) + tuple(value.shape), value.dtype)


def run_kernel(
    kernel, inputs, outs, scratch=(), flops=0, any_count=0, scalars=True, lying=False, done=()
):
    specs, arrays, moved = [], [], 0
    anywhere = pl.BlockSpec(memory_space=pl.ANY)
    for i, value in enumerate(inputs):
        if isinstance(value, tuple):
            value, width, index = value
            specs.append(pl.BlockSpec((value.shape[0], width), lambda _, n=index: (0, n)))
            moved += value.shape[0] * width * value.dtype.itemsize
        elif scalars and i == 0:
            specs.append(pl.BlockSpec(memory_space=pltpu.SMEM))
        else:
            lies = lying or i >= len(inputs) - any_count
            specs.append(anywhere if lies else pl.BlockSpec(memory_space=pltpu.VMEM))
            moved += value.size * value.dtype.itemsize
        arrays.append(value)
    moved += sum(v.size * v.dtype.itemsize for v in outs)
    count, extra = len(inputs), len(done)

    def whole(*refs):
        kernel(*refs[:count], *refs[count + extra :])

    return pl.pallas_call(
        whole,
        grid=(1,),
        out_shape=tuple(outs),
        in_specs=specs + [anywhere] * extra,
        out_specs=tuple(
            pl.BlockSpec(memory_space=pltpu.VMEM) for _ in outs
        ),
        scratch_shapes=list(scratch),
        compiler_params=pltpu.CompilerParams(vmem_limit_bytes=VMEM_LIMIT),
        cost_estimate=pl.CostEstimate(
            flops=flops, bytes_accessed=moved if flops else 0, transcendentals=0
        ),
    )(*arrays, *done)


MLP_SCRATCH = (
    pltpu.VMEM((D, TOKENS), BF),
    pltpu.VMEM((D, D), BF),
    pltpu.VMEM((2, D, 1536), BF),
    pltpu.VMEM((D, FF), BF),
    pltpu.SemaphoreType.DMA((24,)),
)
UNIT = 2 * TOKENS * D * D
ATTEND = 2 * 3 * 1024 * 1024 * HEAD_DIM * 4


NEAR = {"x": NEAR_X, "y": NEAR_Y, "z": NEAR_Z}


def swaps(values, axes, side):
    return [swap(v, axis, side) for v, axis in zip(values, axes)]


def join(values, came, done=()):
    return list(
        run_kernel(
            join_kernel,
            values + came,
            [like(v, 2) for v in values],
            (pltpu.SemaphoreType.DMA((2 * len(values),)),),
            scalars=False,
            lying=True,
            done=done,
        )
    )


def order(place, pairs, far, axes, done=()):
    return list(
        run_kernel(
            functools.partial(order_kernel, [NEAR[axis] for axis in axes]),
            [place] + pairs + far,
            [like(v[0], 4) for v in pairs],
            (pltpu.SemaphoreType.DMA((4 * len(pairs),)),),
            lying=True,
            done=done,
        )
    )


def padded(value):
    return jnp.pad(value.reshape(300, 128), ((0, 4), (0, 0)))


def weights_around(place, norm_params, attn_in, attn_out, mlp_in, mlp_out, early):
    norm_part = jnp.pad(jnp.swapaxes(norm_params, 1, 2), ((0, 0), (0, 0), (0, 124)))
    a = padded(jnp.concatenate([attn_in, attn_out, norm_part], -1))
    bc = [mlp_in.transpose(1, 0, 2).reshape(96, 384), mlp_out.transpose(2, 0, 1).reshape(96, 384)]
    for a_axis, bc_axes in (("z", "yx"), ("x", "zy")):
        bc_near = swaps(bc, bc_axes, 1)
        a_pair = join([a], [swap(a, a_axis, 1)], done=early + bc_near if early else bc)
        early = []
        bc_pair = join(bc, bc_near, done=a_pair)
        a_far = swap(a_pair[0], a_axis, -1)
        bc_far = swaps(bc_pair, bc_axes, -1)
        (a,) = order(place, a_pair, [a_far], a_axis, done=bc_pair)
        if a_axis == "z":
            bc = order(place, bc_pair, bc_far, bc_axes, done=[a])
    a = a[:, :, :300].reshape(4, 4, 2, 6, ROW_A)
    layers = []
    for layer in range(2):
        al = a[:, :, layer].transpose(1, 0, 2, 3).reshape(96, ROW_A)
        bl, cl = run_kernel(
            functools.partial(layer_blocks_kernel, layer),
            [place] + bc_pair + bc_far,
            [shaped(192, 1536), shaped(768, 384)],
            done=[al],
        )
        layers.append([al, bl, cl])
    return layers


LAST = "yxz"


def with_core(value):
    return fetch(value, "c", 1)


def halved(mine, came, done=()):
    outs = [like(v[0]) for v in mine for _ in range(2)]
    out = run_kernel(halve_kernel, list(mine) + list(came), outs, scalars=False, done=done)
    return list(out[0::2]), list(out[1::2])


def total(keep, came):
    return (keep.astype(F32) + came.astype(F32)).astype(BF)


def gradients_home(place, a_layers, b_layers, c_layers):
    parts = [v.reshape(4, 4, 6, ROW_A).transpose(1, 0, 2, 3) for v in a_layers]
    a = jnp.stack(parts, 2).reshape(4, 4, 300, 128)
    a = jnp.pad(a, ((0, 0), (0, 0), (0, 4), (0, 0)))
    a_mine, a_send = run_kernel(
        functools.partial(split_kernel, [NEAR_X]), [place, a], [like(a[0], 2)] * 2
    )
    a_came = swap(a_send, "x", -1)
    b_mine, b_send, c_mine, c_send = run_kernel(
        both_layers_kernel,
        [place] + b_layers[0] + c_layers[0] + b_layers[1] + c_layers[1],
        [shaped(2, 4, 96, 384)] * 4,
    )
    keep, send = halved([b_mine, c_mine], swaps([b_send, c_send], "zx", -1))
    came = swaps(send, "zx", 1)
    (a_keep,), (a_send,) = halved([a_mine], [a_came])
    parts = run_kernel(
        total_pair_kernel,
        [keep[0], came[0], keep[1], came[1]],
        [shaped(2, 96, 384)] * 4,
        scalars=False,
    )
    bc = parts[0].astype(F32)
    for part, step in zip(parts[1:], (-1, 1, 2)):
        bc = bc + fetch(part, "y", step).astype(F32)
    parts = run_kernel(
        total_kernel, [a_keep, swap(a_send, "x", 1)], [like(a_keep[0])] * 4, scalars=False
    )
    a = parts[0].astype(F32)
    for part, step in zip(parts[1:], (-1, 1, 2)):
        a = a + fetch(part, "z", step).astype(F32)
    a = a[:300].reshape(2, 6, ROW_A)
    bc = bc.reshape(2, 96, 2, 192)
    return (
        jnp.swapaxes(a[:, :, 4 * D : 4 * D + 4], 1, 2),
        a[:, :, : 3 * D],
        a[:, :, 3 * D : 4 * D],
        bc[0].transpose(1, 0, 2),
        bc[1].transpose(1, 2, 0),
    )


def body(inputs, lengths, norm_params, attn_in, attn_out, mlp_in, mlp_out, cotangent):
    wide = lax.axis_index("wide")
    narrow = lax.axis_index("narrow")
    core, low, z = wide % 2, (wide // 2) % 2, wide // 4
    x, high = narrow // 2, narrow % 2
    y = high * 2 + low
    length = lax.dynamic_index_in_dim(lengths[:, 0], high, 0, keepdims=False)
    near = [1 + (v + core) % 2 for v in (x, y, z)]
    place = jnp.stack([x, high, length] + near + [low]).astype(jnp.int32)

    def weights_of(pair, far):
        return [pair, far, with_core(pair), with_core(far)]

    def behind(values, done):
        return list(after(values, done))

    slot = jnp.arange(D, dtype=jnp.int32)
    step = jnp.array([0, 1, 3, 2], jnp.int32)
    own_order = ((x + step[slot // 192]) % 4) * 192 + ((high + (slot // 96) % 2) % 2) * 96 + slot % 96
    row_core = (core + slot // 384) % 2
    row_y = (y + step[(slot // 96) % 4]) % 4
    row_z = (z + step[(slot // 24) % 4]) % 4
    row_x = (x + step[(slot // 6) % 4]) % 4
    row_order = 6 * index_of(row_z, row_y, row_core, row_x) + slot % 6
    pa = (own_order[:, None] == row_order[None, :]).astype(BF)
    po = (slot[:, None] == row_order[None, :]).astype(BF)
    p2 = (slot[:, None] == own_order[None, :]).astype(BF)

    def mine_and_other(values):
        mine = lax.dynamic_index_in_dim(values[:, 0], high, 0, keepdims=False)
        return mine, lax.dynamic_index_in_dim(values[:, 0], 1 - high, 0, keepdims=False)

    def in_own_order(mine, came):
        return dot(jnp.concatenate([mine, came], 0), p2)

    mine, other = mine_and_other(inputs)
    other = fetch(other, "y", 2)
    hidden = in_own_order(mine, other)
    around = weights_around(
        place, norm_params, attn_in, attn_out, mlp_in, mlp_out, [other]
    )
    grad_mine, grad_other = mine_and_other(cotangent)
    a_around, *bc_around = around[0]
    a_pair = join([a_around], [swap(a_around, "y", 1)], [pa, po, p2, hidden] + bc_around)
    bc_pair = join(bc_around, swaps(bc_around, "xz", 1), a_pair + around[1])
    a_far = swap(a_pair[0], "y", -1)
    (a_far,) = after([a_far], bc_pair)
    a_weights = [weights_of(a_pair[0], a_far)]
    bc_far = swaps(bc_pair, "xz", -1)
    weights = [None, None]
    records = []
    for layer in range(2):
        a1p_keep, a1p_send, gains, *pieces = run_kernel(
            qkv_kernel,
            [place, hidden, pa] + a_weights[layer],
            [shaped(TOKENS, 384), shaped(TOKENS, 384), shaped(8, D, dtype=F32)]
            + [shaped(576, TOKENS)] * 4,
            (
                pltpu.VMEM((D, 3 * D), BF),
                pltpu.VMEM((D, 128), BF),
                pltpu.VMEM((3 * D, TOKENS), BF),
                pltpu.SemaphoreType.DMA((16,)),
            ),
            flops=4 * UNIT,
            any_count=4,
        )
        blocks = order(place, bc_pair, bc_far, "xz", done=[a1p_keep])
        turned = exchange_four(pieces)
        blocks = behind(blocks, turned[1:])
        cores = [with_core(v) for v in blocks]
        weights[layer] = a_weights[layer] + [blocks[0], cores[0], blocks[1], cores[1]]
        if layer == 0:
            held = behind(around[1], turned[1:])
            first = swaps(held, LAST, 1)
        else:
            (grad_other,) = after([grad_other], turned[1:])
            grad_other = fetch(grad_other, "y", 2)
        *mixed, sums = run_kernel(
            attend_kernel,
            [place] + turned,
            [shaped(GROUP, TOKENS)] * 4 + [shaped(3, 1024, dtype=F32)],
            flops=ATTEND,
        )
        if layer == 0:
            mixed = behind(mixed, first)
        mixed = behind(mixed, cores)
        back = exchange_four(mixed)
        if layer == 0:
            a_pair = join(held[:1], first[:1])
            bc_pair = behind(join(held[1:], first[1:], a_pair), back[1:])
            (a_pair,) = after(a_pair, back[1:])
            a_far = swap(a_pair, "y", -1)
            bc_far = swaps(bc_pair, "xz", -1)
        inputs = [place, hidden] + back + [a1p_send, po, p2, gains]
        whole, wide_rows = shaped(TOKENS, D, dtype=F32), shaped(TOKENS, FF)
        if layer == 0:
            h1, following, slope, forward_send, op_keep, act_keep = run_kernel(
                mlp_kernel,
                inputs + weights[layer],
                [whole, whole, wide_rows, wide_rows, shaped(TOKENS, 384), shaped(TOKENS, 1536)],
                MLP_SCRATCH,
                flops=11 * UNIT,
                any_count=8,
            )
            (a_far,) = after([a_far], [following])
            forward0 = forward_send, with_core(forward_send)
            a_weights.append(weights_of(a_pair, a_far))
        else:
            grad = in_own_order(grad_mine, grad_other)
            following, forward_send, op_keep, act_keep, g1, back_send, dpre_keep, norm2, *pieces = (
                run_kernel(
                    mlp_turn_kernel,
                    inputs + [grad] + weights[layer],
                    [whole, wide_rows, shaped(TOKENS, 384), shaped(TOKENS, 1536)]
                    + [whole, wide_rows, shaped(TOKENS, 1536), shaped(8, D, dtype=F32)]
                    + [shaped(GROUP, TOKENS)] * 4,
                    MLP_SCRATCH + (pltpu.VMEM((TOKENS, FF), BF),),
                    flops=22 * UNIT,
                    any_count=8,
                    done=[forward0[1]],
                )
            )
        records.append(
            (hidden, a1p_keep, gains, turned, mixed, sums, forward_send, op_keep, act_keep)
        )
        hidden = following

    def leave(values, ahead, dtype):
        values = jnp.dot(
            values, p2.astype(F32).T, precision=lax.Precision.HIGHEST, preferred_element_type=F32
        )
        (far,) = after([values[128:].astype(dtype)], list(ahead))
        return values[:128], fetch(far, "y", 2)

    def arrange(own, came):
        return jnp.stack(
            [jnp.where(high == 0, own, came), jnp.where(high == 0, came, own)]
        )[:, None]

    def mlp_gradients(forward, back, act_keep, dpre_keep):
        return run_kernel(
            mlp_grad_kernel,
            [
                place,
                (forward[0], 768, 1),
                (forward[1], 768, 1),
                act_keep,
                (forward[1], 1536, 1),
                dpre_keep,
                (back[1], 1536, 0),
                (back[0], 768, 2),
                (back[1], 768, 2),
            ],
            [shaped(2, 192, 1536)] * 2 + [shaped(2, 768, 384)] * 2,
            flops=8 * UNIT,
        )

    def attend_back(layer, grad_mixed, done):
        turned, mixed, sums = records[layer][3:6]
        return run_kernel(
            attend_back_kernel,
            [place] + turned + grad_mixed + mixed + [sums],
            [shaped(576, TOKENS)] * 4,
            flops=3 * ATTEND,
            done=done,
        )

    def qkv_back(layer, grad_pieces, g1, norm2, done):
        hidden, gains = records[layer][0], records[layer][2]
        return run_kernel(
            qkv_back_kernel,
            [place] + grad_pieces + [hidden, g1, gains, pa, norm2] + a_weights[layer],
            [shaped(TOKENS, D, dtype=F32), shaped(3 * D + 48, TOKENS)],
            (pltpu.VMEM((D, 3 * D), BF), pltpu.SemaphoreType.DMA((8,))),
            flops=5 * UNIT,
            any_count=4,
            done=done,
        )

    def attn_gradients(forward, back, a1p_keep, op_keep, dqkv, done=()):
        return run_kernel(
            attn_grad_kernel,
            [
                place,
                a1p_keep,
                (forward[1], 384, 0),
                op_keep,
                (forward[1], 384, 1),
                (back[0], 768, 3),
                (back[1], 768, 3),
                dqkv[0],
                dqkv[1],
                pa,
            ],
            [shaped(2, 96, ROW_A)] * 2,
            flops=4 * UNIT,
            done=done,
        )

    forward_send, op_keep, act_keep = records[1][6:]
    a1p_keep = records[1][1]
    forward = forward_send, with_core(forward_send)
    grad_mixed = exchange_four(pieces)
    back = back_send, with_core(back_send)
    b1_mine, b1_send, c1_mine, c1_send = mlp_gradients(forward, back, act_keep, dpre_keep)
    b1_send, c1_send = after([b1_send, c1_send], grad_mixed[1:])
    b1_came, c1_came = swap(b1_send, "x", -1), swap(c1_send, "z", -1)
    outputs = leave(hidden, grad_mixed[1:], F32)
    pieces = attend_back(1, grad_mixed, [b1_mine])
    pieces = after(pieces, [outputs[1], b1_came, c1_came])
    grad_pieces = exchange_four(pieces)
    (b1_keep, c1_keep), (b1_send, c1_send) = halved([b1_mine, c1_mine], [b1_came, c1_came])
    dqkv, g1, back_send0, dpre_keep0, norm2, *pieces = run_kernel(
        qkv_back_into_mlp_kernel,
        [place] + grad_pieces + [records[1][0], g1, records[1][2], pa, norm2]
        + [slope, h1, records[0][2], p2, po] + a_weights[1] + weights[0],
        [shaped(3 * D + 48, TOKENS), whole, wide_rows]
        + [shaped(TOKENS, 1536), shaped(8, D, dtype=F32)]
        + [shaped(GROUP, TOKENS)] * 4,
        MLP_SCRATCH + (pltpu.VMEM((D, 3 * D), BF), pltpu.SemaphoreType.DMA((8,))),
        flops=16 * UNIT,
        any_count=12,
        done=[b1_keep],
    )
    dqkv = dqkv, with_core(dqkv)

    _, op_keep0, act_keep0 = records[0][6:]
    a1p_keep0 = records[0][1]
    grad_mixed = exchange_four(pieces)
    a1_mine, a1_send = attn_gradients(forward, back, a1p_keep, op_keep, dqkv)
    a1_send, b1_send, c1_send = after([a1_send, b1_send, c1_send], grad_mixed[1:])
    a1_came = swap(a1_send, "y", -1)
    b1_came, c1_came = swap(b1_send, "x", 1), swap(c1_send, "z", 1)
    pieces = attend_back(0, grad_mixed, [a1_mine])
    pieces = after(pieces, [a1_came, b1_came, c1_came])
    dpre_keep0, back_send0 = after([dpre_keep0, back_send0], pieces[:1])
    back0 = back_send0, with_core(back_send0)
    grad_pieces = exchange_four(pieces)
    b0_mine, b0_send, c0_mine, c0_send = mlp_gradients(forward0, back0, act_keep0, dpre_keep0)
    (a1_keep,), (a1_send,) = halved([a1_mine], [a1_came], [b0_mine])
    a1_send, b0_send, c0_send = after([a1_send, b0_send, c0_send], grad_pieces[1:])
    a1_came = swap(a1_send, "y", 1)
    b0_came, c0_came = swap(b0_send, "x", -1), swap(c0_send, "z", -1)
    grad, dqkv = qkv_back(0, grad_pieces, g1, norm2, [b0_mine, a1_keep])
    grad, dqkv = after([grad, dqkv], [a1_came])
    dqkv = dqkv, with_core(dqkv)
    grad_own, grad_far = leave(grad, [], BF)
    a0_mine, a0_send = attn_gradients(
        forward0, back0, a1p_keep0, op_keep0, dqkv
    )
    (a0_send,) = after([a0_send], [grad_far])
    a0_came = swap(a0_send, "y", -1)
    (a0_keep,), (a0_send,) = halved([a0_mine], [a0_came])
    a0_came = swap(a0_send, "y", 1)
    (b0_keep, c0_keep), (b0_send, c0_send) = halved(
        [b0_mine, c0_mine], [b0_came, c0_came], [a0_keep]
    )
    b0_came, c0_came = swap(b0_send, "x", 1), swap(c0_send, "z", 1)
    weight_grads = gradients_home(
        place,
        [total(a0_keep, a0_came), total(a1_keep, a1_came)],
        [[b0_keep, b0_came], [b1_keep, b1_came]],
        [[c0_keep, c0_came], [c1_keep, c1_came]],
    )
    grad_inputs = grad_own, grad_far.astype(F32)
    return (arrange(*outputs), arrange(*grad_inputs)) + weight_grads


def solution(mesh):
    in_specs = (
        P(None, "wide", "narrow", None),
        P(None, "wide"),
        P(None, None, ("wide", "narrow")),
        P(None, ("wide", "narrow"), None),
        P(None, ("wide", "narrow"), None),
        P(None, "narrow", "wide"),
        P(None, "wide", "narrow"),
        P(None, "wide", "narrow", None),
    )
    out_specs = (
        P(None, "wide", "narrow", None),
        P(None, "wide", "narrow", None),
        P(None, None, ("wide", "narrow")),
        P(None, ("wide", "narrow"), None),
        P(None, ("wide", "narrow"), None),
        P(None, "narrow", "wide"),
        P(None, "wide", "narrow"),
    )
    return jax.shard_map(body, mesh=mesh, in_specs=in_specs, out_specs=out_specs, check_vma=False)
```

```python
import functools

import jax
import jax.numpy as jnp
from jax import lax
from jax.experimental import pallas as pl
from jax.experimental.pallas import tpu as pltpu
from jax.sharding import PartitionSpec as P

D = 768
FF = 3072
HEAD_DIM = 64
GROUP = 192
TOKENS = 256
SPAN = 1024
SPAN_BACK = 512
EPS = 1e-06
ROOT_HALF = 0.7071067811865476
INV_ROOT_TWO_PI = 0.3989422804014327
ROW_A = 3200
BF = jnp.bfloat16
F32 = jnp.float32
AXES = ("wide", "narrow")
VMEM_LIMIT = 56 * 1024 * 1024


def index_of(z, y, c, x):
    return ((z * 2 + y % 2) * 2 + c) * 8 + x * 2 + y // 2


def everywhere():
    for z in range(4):
        for y in range(4):
            for c in range(2):
                for x in range(4):
                    yield {"z": z, "y": y, "c": c, "x": x}


def fetch(value, axis, step):
    pairs = []
    for here in everywhere():
        there = dict(here)
        there[axis] = (here[axis] + step) % (2 if axis == "c" else 4)
        pairs.append((index_of(**there), index_of(**here)))
    return lax.ppermute(value, AXES, pairs)


def swap(value, axis, side):
    pairs = []
    for here in everywhere():
        step = side if (here[axis] + here["c"]) % 2 == 0 else -side
        there = dict(here)
        there[axis] = (here[axis] + step) % 4
        pairs.append((index_of(**here), index_of(**there)))
    return lax.ppermute(value, AXES, pairs)


def exchange_four(pieces):
    return [pieces[0]] + [fetch(pieces[4 - k], "x", k) for k in (1, 2, 3)]


def dot(left, right, over_left=1, over_right=0):
    return lax.dot_general(
        left, right, (((over_left,), (over_right,)), ((), ())), preferred_element_type=F32
    )


def dot_two(left, right, over_left=1, over_right=0):
    high = left.astype(BF)
    low = (left - high.astype(F32)).astype(BF)
    return dot(high, right, over_left, over_right) + dot(low, right, over_left, over_right)


def normed(values):
    average = jnp.mean(values, -1, keepdims=True)
    centred = values - average
    spread = jnp.mean(centred * centred, -1, keepdims=True)
    scale = lax.rsqrt(spread + EPS)
    return centred * scale, scale


def norm_back(grad, values, gain_row):
    z, scale = normed(values)
    dz = grad * gain_row
    out = (
        dz - jnp.mean(dz, -1, keepdims=True) - z * jnp.mean(dz * z, -1, keepdims=True)
    ) * scale
    gain_grad = jnp.sum(grad * z, 0, keepdims=True)
    offset_grad = jnp.sum(grad, 0, keepdims=True)
    return out, gain_grad, offset_grad


def two_rows(first, second):
    return jnp.concatenate([first, second, jnp.zeros((6, D), F32)], 0)


def group_start(x, k, base=0):
    return pl.multiple_of(base + lax.rem(x + k, 4) * GROUP, GROUP)


def start_copies(pairs, sems):
    copies = [
        pltpu.make_async_copy(source, target, sems.at[i])
        for i, (source, target) in enumerate(pairs)
    ]
    for copy in copies:
        copy.start()
    return copies


def wait_copies(copies):
    for copy in copies:
        copy.wait()


X, HIGH, LENGTH, NEAR_X, NEAR_Y, NEAR_Z, LOW = range(7)


def weight_blocks(refs, near):
    spots = [0, near, 3 - near, 3, 0, 3 - near, near, 3]
    return [(ref, n // 4, spot) for n, (ref, spot) in enumerate(zip(refs, spots))]


def at_rows(core, spot, rows):
    return pl.ds(pl.multiple_of((core * 4 + spot) * rows, rows), rows)


def qkv_kernel(place_ref, h_ref, pa_ref, *refs):
    blocks = weight_blocks(refs[:8], place_ref[NEAR_Y])
    a1p_keep, a1p_send, gains_ref = refs[8:11]
    out_refs = refs[11:15]
    win, table, turned, sems = refs[15:]
    norm_copies = start_copies(
        [
            (r.at[:, pl.ds(FF, 128)], table.at[at_rows(core, spot, 96)])
            for r, core, spot in blocks
        ],
        sems.at[pl.ds(0, 8)],
    )
    win_copies = start_copies(
        [
            (r.at[:, pl.ds(0, 3 * D)], win.at[at_rows(core, spot, 96)])
            for r, core, spot in blocks
        ],
        sems.at[pl.ds(8, 8)],
    )
    z, _ = normed(h_ref[...])
    wait_copies(norm_copies)
    gains = dot(table[...], pa_ref[...], 0, 1)[0:8]
    gains_ref[...] = gains
    a1 = (z * gains[0:1] + gains[1:2]).astype(BF)
    a1p = dot(a1, pa_ref[...]).astype(BF)
    a1p_keep[...] = a1p[:, :384]
    a1p_send[...] = a1p[:, 384:]
    wait_copies(win_copies)
    for c in range(3):
        part = dot(a1p, win[:, c * D : (c + 1) * D])
        if c == 0:
            part = part * HEAD_DIM ** (-0.5)
        turned[c * D : (c + 1) * D, :] = part.astype(BF).T
    x = place_ref[X]
    for k in range(4):
        for c in range(3):
            out_refs[k][c * GROUP : (c + 1) * GROUP, :] = turned[
                pl.ds(group_start(x, k, c * D), GROUP), :
            ]


def mask_row(place_ref):
    x, yh, length = place_ref[X], place_ref[HIGH], place_ref[LENGTH]
    rows = []
    for k in range(4):
        for half in range(2):
            start = lax.rem(x + k, 4) * 256 + lax.rem(yh + half, 2) * 128
            slot = start + lax.broadcasted_iota(jnp.int32, (1, 128), 1)
            rows.append(jnp.where(slot < length, 0.0, -1e30))
    return jnp.concatenate(rows, 1)


def side_by_side(refs, start):
    return jnp.concatenate([r[start : start + HEAD_DIM, :] for r in refs], 1)


def with_rows(block, rows):
    count, width = len(rows), block.shape[1]
    tail = jnp.concatenate(rows + [jnp.zeros((16 - count, width), F32)], 0).astype(BF)
    return jnp.concatenate([block, tail], 0)


def in_three(row):
    high = row.astype(BF).astype(F32)
    middle = (row - high).astype(BF).astype(F32)
    return [high, middle, row - high - middle]


def attend_kernel(place_ref, t0, t1, t2, t3, u0, u1, u2, u3, sums_ref):
    t_refs, u_refs = (t0, t1, t2, t3), (u0, u1, u2, u3)
    mask = mask_row(place_ref)
    count = SPAN // TOKENS
    ones = jnp.ones((1, SPAN), F32)
    for j in range(3):
        keys = with_rows(side_by_side(t_refs, GROUP + j * HEAD_DIM), [mask]).T
        values_t = side_by_side(t_refs, 2 * GROUP + j * HEAD_DIM)
        rows = slice(j * HEAD_DIM, (j + 1) * HEAD_DIM)
        for b in range(0, 4, count):
            query_t = side_by_side(t_refs[b : b + count], j * HEAD_DIM)
            scores = dot(keys, with_rows(query_t, [ones]))
            peak = jnp.max(scores, 0, keepdims=True)
            expont = jnp.exp(scores - peak)
            total = jnp.sum(expont, 0, keepdims=True)
            mixed = (dot(values_t, expont.astype(BF)) / total).astype(BF)
            for n in range(count):
                u_refs[b + n][rows, :] = mixed[:, n * TOKENS : (n + 1) * TOKENS]
            sums_ref[j : j + 1, b * TOKENS : (b + count) * TOKENS] = peak + jnp.log(total)


def attend_back_kernel(place_ref, *refs):
    t_refs, g_refs, u_refs = refs[0:4], refs[4:8], refs[8:12]
    sums_ref = refs[12]
    out_refs = refs[13:17]
    mask = mask_row(place_ref)
    count = SPAN_BACK // TOKENS
    ones = jnp.ones((1, SPAN_BACK), F32)
    one_row = jnp.ones((1, 4 * TOKENS), F32)
    for j in range(3):
        keys_t = side_by_side(t_refs, GROUP + j * HEAD_DIM)
        keys = with_rows(keys_t, [mask] + [one_row] * 3).T
        values = with_rows(side_by_side(t_refs, 2 * GROUP + j * HEAD_DIM), [one_row] * 3).T
        grad_keys = jnp.zeros((4 * TOKENS, HEAD_DIM), F32)
        grad_values = jnp.zeros((4 * TOKENS, HEAD_DIM), F32)
        rows = slice(j * HEAD_DIM, (j + 1) * HEAD_DIM)
        for b in range(0, 4, count):
            query_t = side_by_side(t_refs[b : b + count], j * HEAD_DIM)
            grad_t = side_by_side(g_refs[b : b + count], j * HEAD_DIM)
            mixed_t = side_by_side(u_refs[b : b + count], j * HEAD_DIM)
            sums = sums_ref[j : j + 1, b * TOKENS : (b + count) * TOKENS]
            delta = jnp.sum(grad_t.astype(F32) * mixed_t.astype(F32), 0, keepdims=True)
            probs = jnp.exp(dot(keys, with_rows(query_t, [ones] + in_three(-sums))))
            grad_probs = dot(values, with_rows(grad_t, in_three(-delta)))
            grad_scores = (probs * grad_probs).astype(BF)
            grad_values = grad_values + dot(probs.astype(BF), grad_t, 1, 1)
            grad_keys = grad_keys + dot(grad_scores, query_t, 1, 1)
            grad_query = (dot(keys_t, grad_scores) * HEAD_DIM ** (-0.5)).astype(BF)
            for n in range(count):
                out_refs[b + n][rows, :] = grad_query[:, n * TOKENS : (n + 1) * TOKENS]
        grad_keys = grad_keys.astype(BF).T
        grad_values = grad_values.astype(BF).T
        for b in range(4):
            columns = slice(b * TOKENS, (b + 1) * TOKENS)
            start = GROUP + j * HEAD_DIM
            out_refs[b][start : start + HEAD_DIM, :] = grad_keys[:, columns]
            start = 2 * GROUP + j * HEAD_DIM
            out_refs[b][start : start + HEAD_DIM, :] = grad_values[:, columns]


def mlp_copies(place_ref, refs, wout, w1, w2, sems):
    out_copies = start_copies(
        [
            (r.at[:, pl.ds(3 * D, D)], wout.at[at_rows(core, spot, 96)])
            for r, core, spot in weight_blocks(refs[0:8], place_ref[NEAR_Y])
        ],
        sems.at[pl.ds(0, 8)],
    )
    first_copies = start_copies(
        [
            (ref.at[k], w1.at[core, pl.ds(192 * k, 192)])
            for core, ref in enumerate(refs[8:10])
            for k in range(4)
        ],
        sems.at[pl.ds(8, 8)],
    )
    second_copies = start_copies(
        [
            (ref.at[k], w2.at[:, pl.ds((core * 4 + k) * 384, 384)])
            for core, ref in enumerate(refs[10:12])
            for k in range(4)
        ],
        sems.at[pl.ds(16, 8)],
    )
    return out_copies, first_copies, second_copies


def mlp_forward(place_ref, h, pieces, a1p_send, po_ref, p2_ref, gains_ref, slope_ref, outs, parts):
    send_ref, op_keep, act_keep = outs
    turned, wout, w1, w2, out_copies, first_copies, second_copies = parts
    send_ref[:, 0:384] = a1p_send[...]
    x = place_ref[X]
    for k, piece in enumerate(pieces):
        turned[pl.ds(group_start(x, k), GROUP), :] = piece[...]
    op = dot(turned[...], po_ref[...], 0, 0).astype(BF)
    op_keep[...] = op[:, :384]
    send_ref[:, 384:768] = op[:, 384:]
    wait_copies(out_copies)
    h1 = h + dot_two(dot(op, wout[...]), p2_ref[...])
    z, _ = normed(h1)
    a2 = (z * gains_ref[2:3] + gains_ref[3:4]).astype(BF)
    send_ref[:, 768:1536] = a2
    wait_copies(first_copies)
    total = h1
    for half in range(2):
        pre = dot(a2, w1[half])
        below = 0.5 * (1.0 + lax.erf(pre * ROOT_HALF))
        act = (pre * below).astype(BF)
        slope = below + pre * (jnp.exp(-0.5 * pre * pre) * INV_ROOT_TWO_PI)
        columns = slice(half * 1536, (half + 1) * 1536)
        if half == 0:
            act_keep[...] = act
            wait_copies(second_copies)
        else:
            send_ref[:, 1536:] = act
        slope_ref[:, columns] = slope.astype(BF)
        total = total + dot(act, w2[:, columns], 1, 1)
    return h1, total


def mlp_backward(place_ref, grad, h1, gains_ref, p2_ref, po_ref, slope_ref, outs, parts):
    send_ref, dpre_keep, norm_ref, out_refs = outs
    turned, wout, w1, w2, out_copies, first_copies, second_copies = parts
    grad_low = grad.astype(BF)
    send_ref[:, 1536:2304] = grad_low
    wait_copies(second_copies)
    grad_a2 = jnp.zeros((TOKENS, D), F32)
    for half in range(2):
        columns = slice(half * 1536, (half + 1) * 1536)
        grad_act = dot(grad_low, w2[:, columns])
        dpre = (grad_act * slope_ref[:, columns].astype(F32)).astype(BF)
        if half == 0:
            dpre_keep[...] = dpre
            wait_copies(first_copies)
        else:
            send_ref[:, 0:1536] = dpre
        grad_a2 = grad_a2 + dot(dpre, w1[half], 1, 1)
    dv, gain_grad, offset_grad = norm_back(grad_a2, h1, gains_ref[2:3])
    norm_ref[...] = two_rows(gain_grad, offset_grad)
    g1 = grad + dv
    g1b = dot(g1.astype(BF), p2_ref[...], 1, 1).astype(BF)
    send_ref[:, 2304:] = g1b
    wait_copies(out_copies)
    grad_op = dot(g1b, wout[...], 1, 1).astype(BF)
    turned[...] = dot(po_ref[...], grad_op, 1, 1).astype(BF)
    x = place_ref[X]
    for k in range(4):
        out_refs[k][...] = turned[pl.ds(group_start(x, k), GROUP), :]
    return g1


def mlp_kernel(place_ref, h_ref, u0, u1, u2, u3, a1p_send, po_ref, p2_ref, gains_ref, *refs):
    h1_ref, next_ref, slope_ref, send_ref, op_keep, act_keep = refs[12:18]
    turned, wout, w1, w2, sems = refs[18:]
    copies = mlp_copies(place_ref, refs[:12], wout, w1, w2, sems)
    h1_ref[...], next_ref[...] = mlp_forward(
        place_ref, h_ref[...], (u0, u1, u2, u3), a1p_send, po_ref, p2_ref, gains_ref, slope_ref,
        (send_ref, op_keep, act_keep), (turned, wout, w1, w2) + copies,
    )


def mlp_turn_kernel(
    place_ref, h_ref, u0, u1, u2, u3, a1p_send, po_ref, p2_ref, gains_ref, g_ref, *refs
):
    next_ref, forward_send, op_keep, act_keep, g1_ref, back_send, dpre_keep, norm_ref = refs[12:20]
    out_refs = refs[20:24]
    turned, wout, w1, w2, sems, slope_ref = refs[24:]
    copies = mlp_copies(place_ref, refs[:12], wout, w1, w2, sems)
    h1, next_ref[...] = mlp_forward(
        place_ref, h_ref[...], (u0, u1, u2, u3), a1p_send, po_ref, p2_ref, gains_ref, slope_ref,
        (forward_send, op_keep, act_keep), (turned, wout, w1, w2) + copies,
    )
    g1_ref[...] = mlp_backward(
        place_ref, g_ref[...], h1, gains_ref, p2_ref, po_ref, slope_ref,
        (back_send, dpre_keep, norm_ref, out_refs), (turned, wout, w1, w2, (), (), ()),
    )


def qkv_back_into_mlp_kernel(
    place_ref, d0, d1, d2, d3, h_ref, g1_ref, gains_ref, pa_ref, norm2_ref,
    slope_ref, h1_ref, gains0_ref, p2_ref, po_ref, *refs,
):
    dqkv_ref, next_ref, back_send, dpre_keep, below_ref = refs[20:25]
    out_refs = refs[25:29]
    turned, wout, w1, w2, sems, win, win_sems = refs[29:]
    win_copies = win_start(place_ref, refs[:8], win, win_sems)
    copies = mlp_copies(place_ref, refs[8:20], wout, w1, w2, sems)
    grad = qkv_backward(
        place_ref, (d0, d1, d2, d3), h_ref, g1_ref, gains_ref, pa_ref, norm2_ref,
        dqkv_ref, win, win_copies,
    )
    next_ref[...] = mlp_backward(
        place_ref, grad, h1_ref[...], gains0_ref, p2_ref, po_ref, slope_ref,
        (back_send, dpre_keep, below_ref, out_refs), (turned, wout, w1, w2) + copies,
    )


def both_cores(first_ref, second_ref):
    return jnp.concatenate([first_ref[...], second_ref[...]], 0)


def store_blocks(near, mine, send, columns, blocks):
    mine[0, :, columns] = blocks[0]
    send[1, :, columns] = blocks[3]

    @pl.when(near == 1)
    def _():
        mine[1, :, columns] = blocks[1]
        send[0, :, columns] = blocks[2]

    @pl.when(near == 2)
    def _():
        mine[1, :, columns] = blocks[2]
        send[0, :, columns] = blocks[1]


def mlp_grad_kernel(
    place_ref, a2_0, a2_1, act_0, act_1, dpre_0, dpre_1, gb_0, gb_1,
    first_mine, first_send, second_mine, second_send,
):
    a2 = both_cores(a2_0, a2_1)
    grad_low = both_cores(gb_0, gb_1)
    dpre = both_cores(dpre_0, dpre_1)
    for part in range(2):
        columns = slice(part * 768, part * 768 + 768)
        value = dot(a2, dpre[:, columns], 0, 0).astype(BF)
        blocks = [value[192 * k : 192 * k + 192] for k in range(4)]
        store_blocks(place_ref[NEAR_X], first_mine, first_send, columns, blocks)
    act = both_cores(act_0, act_1)
    blocks = [
        dot(grad_low, act[:, 384 * k : 384 * k + 384], 0, 0).astype(BF) for k in range(4)
    ]
    store_blocks(place_ref[NEAR_Z], second_mine, second_send, slice(0, 384), blocks)


def win_start(place_ref, refs, win, sems):
    return start_copies(
        [
            (r.at[:, pl.ds(0, 3 * D)], win.at[at_rows(core, spot, 96)])
            for r, core, spot in weight_blocks(refs, place_ref[NEAR_Y])
        ],
        sems,
    )


def qkv_backward(
    place_ref, pieces, h_ref, g1_ref, gains_ref, pa_ref, norm2_ref, dqkv_ref, win, copies
):
    x = place_ref[X]
    for k, piece in enumerate(pieces):
        for c in range(3):
            dqkv_ref[pl.ds(group_start(x, k, c * D), GROUP), :] = piece[
                c * GROUP : (c + 1) * GROUP, :
            ]
    wait_copies(copies)
    turned = dot(win[...], dqkv_ref[0 : 3 * D, :])
    grad_a1 = dot_two(turned, pa_ref[...], 0, 1)
    dv, gain_grad, offset_grad = norm_back(grad_a1, h_ref[...], gains_ref[0:1])
    norms = jnp.concatenate([gain_grad, offset_grad, norm2_ref[0:2], jnp.zeros((4, D), F32)], 0)
    high = norms.astype(BF)
    norms = jnp.concatenate([high, (norms - high.astype(F32)).astype(BF)], 0)
    for c in range(3):
        dqkv_ref[3 * D + 16 * c : 3 * D + 16 * c + 16, :] = norms[:, 256 * c : 256 * c + 256]
    return g1_ref[...] + dv


def qkv_back_kernel(
    place_ref, d0, d1, d2, d3, h_ref, g1_ref, gains_ref, pa_ref, norm2_ref, *refs
):
    next_ref, dqkv_ref, win, sems = refs[8:]
    copies = win_start(place_ref, refs[:8], win, sems)
    next_ref[...] = qkv_backward(
        place_ref, (d0, d1, d2, d3), h_ref, g1_ref, gains_ref, pa_ref, norm2_ref,
        dqkv_ref, win, copies,
    )


def attn_grad_kernel(
    place_ref, a1p_0, a1p_1, op_0, op_1, g1b_0, g1b_1, dqkv_0, dqkv_1, pa_ref, mine, send
):
    near = place_ref[NEAR_Y]
    norms = jnp.zeros((8, D), F32)
    for ref in (dqkv_0, dqkv_1):
        pair = [ref[3 * D + 16 * c : 3 * D + 16 * c + 16, :].astype(F32) for c in range(3)]
        pair = jnp.concatenate(pair, 1)
        norms = norms + pair[0:8] + pair[8:16]
    norms = dot_two(norms, pa_ref[:, 0:384])
    norms = jnp.concatenate([norms, jnp.zeros((120, 384), F32)], 0).T.astype(BF)
    a1p = both_cores(a1p_0, a1p_1)
    for c in range(5):
        columns = slice(c * D, min((c + 1) * D, ROW_A))
        if c < 3:
            dqkv = jnp.concatenate(
                [dqkv_0[c * D : (c + 1) * D, :], dqkv_1[c * D : (c + 1) * D, :]], 1
            )
            value = dot(a1p, dqkv, 0, 1).astype(BF)
        elif c == 3:
            value = dot(both_cores(op_0, op_1), both_cores(g1b_0, g1b_1), 0, 0).astype(BF)
        else:
            value = norms
        blocks = [value[96 * k : 96 * k + 96] for k in range(4)]
        store_blocks(near, mine, send, columns, blocks)


def join_kernel(*refs):
    count = (len(refs) - 1) // 3
    pairs = []
    for own, came, out in zip(refs[:count], refs[count : 2 * count], refs[2 * count : -1]):
        pairs += [(own, out.at[0]), (came, out.at[1])]
    wait_copies(start_copies(pairs, refs[-1]))


def order_kernel(spots, place_ref, *refs):
    count = len(spots)
    pairs = []
    for spot, pair, far, out in zip(
        spots, refs[:count], refs[count : 2 * count], refs[2 * count : -1]
    ):
        near = place_ref[spot]
        pairs += [
            (pair.at[0], out.at[0]),
            (pair.at[1], out.at[near]),
            (far.at[0], out.at[3 - near]),
            (far.at[1], out.at[3]),
        ]
    wait_copies(start_copies(pairs, refs[-1]))


def layer_blocks_kernel(
    layer, place_ref, b_pair, c_pair, b_far, c_far, first_ref, second_ref
):
    middle = 1 + place_ref[LOW]
    near_z = place_ref[NEAR_Z]
    straight = place_ref[NEAR_Y] == middle
    part = slice(layer * 192, layer * 192 + 192)
    b_slots = ((b_pair, 0, 0), (b_pair, 1, near_z), (b_far, 0, 3 - near_z), (b_far, 1, 3))
    for high in range(2):
        one, two = (0, middle) if high == 0 else (3, 3 - middle)
        for ref, i, spot in b_slots:
            both = [ref[i, one][:, part], ref[i, two][:, part]]
            first_ref[
                high * 96 : high * 96 + 96, pl.ds(pl.multiple_of(spot * 384, 384), 384)
            ] = jnp.concatenate(both, 1)
        for k in range(4):
            outer = c_pair[0, k] if high == 0 else c_far[1, k]
            near, other = c_pair[1, k], c_far[0, k]
            if high == 0:
                inner = jnp.where(straight, near, other)
            else:
                inner = jnp.where(straight, other, near)
            start = (2 * k + high) * 96
            second_ref[start : start + 96, :] = jnp.concatenate(
                [outer[:, part], inner[:, part]], 1
            )


def both_layers_kernel(place_ref, *refs):
    b0, b0_came, c0, c0_came, b1, b1_came, c1, c1_came = refs[:8]
    b_mine, b_send, c_mine, c_send = refs[8:]
    middle = 1 + place_ref[LOW]
    near_z, near_x = place_ref[NEAR_Z], place_ref[NEAR_X]

    def put(mine, send, near, spot, index, value):
        if isinstance(spot, int) and spot == 0:
            mine[0, index] = value
        elif isinstance(spot, int) and spot == 3:
            send[1, index] = value
        else:

            @pl.when(near == spot)
            def _():
                mine[1, index] = value

            @pl.when(near != spot)
            def _():
                send[0, index] = value

    for high in range(2):
        for k in range(4):
            rows, columns = slice(high * 96, high * 96 + 96), slice(k * 384, k * 384 + 384)
            b_parts = [
                total_of(b0[rows, columns], b0_came[rows, columns]),
                total_of(b1[rows, columns], b1_came[rows, columns]),
            ]
            rows = slice((2 * k + high) * 96, (2 * k + high) * 96 + 96)
            c_parts = [
                total_of(c0[rows, :], c0_came[rows, :]),
                total_of(c1[rows, :], c1_came[rows, :]),
            ]
            for part in range(2):
                if part == 0:
                    spot = 0 if high == 0 else 3
                else:
                    spot = middle if high == 0 else 3 - middle
                columns = slice(part * 192, part * 192 + 192)
                value = jnp.concatenate([v[:, columns] for v in b_parts], 1)
                put(b_mine, b_send, near_z, k, spot, value)
                value = jnp.concatenate([v[:, columns] for v in c_parts], 1)
                put(c_mine, c_send, near_x, k, spot, value)


def split_kernel(spots, place_ref, *refs):
    count = len(spots)
    for n, spot in enumerate(spots):
        near = place_ref[spot]
        value, mine, send = refs[n], refs[count + 2 * n], refs[count + 2 * n + 1]
        mine[0] = value[0]
        mine[1] = value[near]
        send[0] = value[3 - near]
        send[1] = value[3]


def total_of(first, second):
    return (first.astype(F32) + second.astype(F32)).astype(BF)


def halve_kernel(*refs):
    count = len(refs) // 4
    for n in range(count):
        mine, came = refs[n], refs[count + n]
        keep, send = refs[2 * count + 2 * n], refs[2 * count + 2 * n + 1]
        keep[...] = total_of(mine[0], came[0])
        send[...] = total_of(mine[1], came[1])


def total_pair_kernel(b_keep, b_came, c_keep, c_came, *out_refs):
    for k, out in enumerate(out_refs):
        out[0] = total_of(b_keep[k], b_came[k])
        out[1] = total_of(c_keep[k], c_came[k])


def total_kernel(keep, came, *out_refs):
    for k, out in enumerate(out_refs):
        out[...] = total_of(keep[k], came[k])


def nothing_kernel(*refs):
    pass


def after(values, done):
    anywhere = pl.BlockSpec(memory_space=pl.ANY)
    return pl.pallas_call(
        nothing_kernel,
        out_shape=tuple(jax.ShapeDtypeStruct(v.shape, v.dtype) for v in values),
        in_specs=[anywhere] * (len(values) + len(done)),
        out_specs=tuple(anywhere for _ in values),
        input_output_aliases={i: i for i in range(len(values))},
    )(*values, *done)


def shaped(*shape, dtype=BF):
    return jax.ShapeDtypeStruct(shape, dtype)


def like(value, *lead):
    return jax.ShapeDtypeStruct(tuple(lead) + tuple(value.shape), value.dtype)


def run_kernel(
    kernel, inputs, outs, scratch=(), flops=0, any_count=0, scalars=True, lying=False, done=()
):
    specs, arrays, moved = [], [], 0
    anywhere = pl.BlockSpec(memory_space=pl.ANY)
    for i, value in enumerate(inputs):
        if isinstance(value, tuple):
            value, width, index = value
            specs.append(pl.BlockSpec((value.shape[0], width), lambda _, n=index: (0, n)))
            moved += value.shape[0] * width * value.dtype.itemsize
        elif scalars and i == 0:
            specs.append(pl.BlockSpec(memory_space=pltpu.SMEM))
        else:
            lies = lying or i >= len(inputs) - any_count
            specs.append(anywhere if lies else pl.BlockSpec(memory_space=pltpu.VMEM))
            moved += value.size * value.dtype.itemsize
        arrays.append(value)
    moved += sum(v.size * v.dtype.itemsize for v in outs)
    count, extra = len(inputs), len(done)

    def whole(*refs):
        kernel(*refs[:count], *refs[count + extra :])

    return pl.pallas_call(
        whole,
        grid=(1,),
        out_shape=tuple(outs),
        in_specs=specs + [anywhere] * extra,
        out_specs=tuple(
            pl.BlockSpec(memory_space=pltpu.VMEM) for _ in outs
        ),
        scratch_shapes=list(scratch),
        compiler_params=pltpu.CompilerParams(vmem_limit_bytes=VMEM_LIMIT),
        cost_estimate=pl.CostEstimate(
            flops=flops, bytes_accessed=moved if flops else 0, transcendentals=0
        ),
    )(*arrays, *done)


MLP_SCRATCH = (
    pltpu.VMEM((D, TOKENS), BF),
    pltpu.VMEM((D, D), BF),
    pltpu.VMEM((2, D, 1536), BF),
    pltpu.VMEM((D, FF), BF),
    pltpu.SemaphoreType.DMA((24,)),
)
UNIT = 2 * TOKENS * D * D
ATTEND = 2 * 3 * 1024 * 1024 * HEAD_DIM * 4


NEAR = {"x": NEAR_X, "y": NEAR_Y, "z": NEAR_Z}


def swaps(values, axes, side):
    return [swap(v, axis, side) for v, axis in zip(values, axes)]


def join(values, came, done=()):
    return list(
        run_kernel(
            join_kernel,
            values + came,
            [like(v, 2) for v in values],
            (pltpu.SemaphoreType.DMA((2 * len(values),)),),
            scalars=False,
            lying=True,
            done=done,
        )
    )


def order(place, pairs, far, axes, done=()):
    return list(
        run_kernel(
            functools.partial(order_kernel, [NEAR[axis] for axis in axes]),
            [place] + pairs + far,
            [like(v[0], 4) for v in pairs],
            (pltpu.SemaphoreType.DMA((4 * len(pairs),)),),
            lying=True,
            done=done,
        )
    )


def padded(value):
    return jnp.pad(value.reshape(300, 128), ((0, 4), (0, 0)))


def weights_around(place, norm_params, attn_in, attn_out, mlp_in, mlp_out, early):
    norm_part = jnp.pad(jnp.swapaxes(norm_params, 1, 2), ((0, 0), (0, 0), (0, 124)))
    a = padded(jnp.concatenate([attn_in, attn_out, norm_part], -1))
    bc = [mlp_in.transpose(1, 0, 2).reshape(96, 384), mlp_out.transpose(2, 0, 1).reshape(96, 384)]
    for a_axis, bc_axes in (("z", "yx"), ("x", "zy")):
        bc_near = swaps(bc, bc_axes, 1)
        a_pair = join([a], [swap(a, a_axis, 1)], done=bc_near if early else bc)
        bc_pair = join(bc, bc_near, done=a_pair + early)
        early = []
        a_far = swap(a_pair[0], a_axis, -1)
        bc_far = swaps(bc_pair, bc_axes, -1)
        (a,) = order(place, a_pair, [a_far], a_axis, done=bc_pair)
        if a_axis == "z":
            bc = order(place, bc_pair, bc_far, bc_axes, done=[a])
    a = a[:, :, :300].reshape(4, 4, 2, 6, ROW_A)
    layers = []
    for layer in range(2):
        al = a[:, :, layer].transpose(1, 0, 2, 3).reshape(96, ROW_A)
        bl, cl = run_kernel(
            functools.partial(layer_blocks_kernel, layer),
            [place] + bc_pair + bc_far,
            [shaped(192, 1536), shaped(768, 384)],
            done=[al],
        )
        layers.append([al, bl, cl])
    return layers, bc_far


LAST = "yxz"


def with_core(value):
    return fetch(value, "c", 1)


def halved(mine, came, done=()):
    outs = [like(v[0]) for v in mine for _ in range(2)]
    out = run_kernel(halve_kernel, list(mine) + list(came), outs, scalars=False, done=done)
    return list(out[0::2]), list(out[1::2])


def total(keep, came):
    return (keep.astype(F32) + came.astype(F32)).astype(BF)


def gradients_home(place, a_layers, b_layers, c_layers):
    parts = [v.reshape(4, 4, 6, ROW_A).transpose(1, 0, 2, 3) for v in a_layers]
    a = jnp.stack(parts, 2).reshape(4, 4, 300, 128)
    a = jnp.pad(a, ((0, 0), (0, 0), (0, 4), (0, 0)))
    a_mine, a_send = run_kernel(
        functools.partial(split_kernel, [NEAR_X]), [place, a], [like(a[0], 2)] * 2
    )
    a_came = swap(a_send, "x", -1)
    b_mine, b_send, c_mine, c_send = run_kernel(
        both_layers_kernel,
        [place] + b_layers[0] + c_layers[0] + b_layers[1] + c_layers[1],
        [shaped(2, 4, 96, 384)] * 4,
    )
    keep, send = halved([b_mine, c_mine], swaps([b_send, c_send], "zx", -1))
    came = swaps(send, "zx", 1)
    (a_keep,), (a_send,) = halved([a_mine], [a_came])
    parts = run_kernel(
        total_pair_kernel,
        [keep[0], came[0], keep[1], came[1]],
        [shaped(2, 96, 384)] * 4,
        scalars=False,
    )
    bc = parts[0].astype(F32)
    for part, step in zip(parts[1:], (-1, 1, 2)):
        bc = bc + fetch(part, "y", step).astype(F32)
    parts = run_kernel(
        total_kernel, [a_keep, swap(a_send, "x", 1)], [like(a_keep[0])] * 4, scalars=False
    )
    a = parts[0].astype(F32)
    for part, step in zip(parts[1:], (-1, 1, 2)):
        a = a + fetch(part, "z", step).astype(F32)
    a = a[:300].reshape(2, 6, ROW_A)
    bc = bc.reshape(2, 96, 2, 192)
    return (
        jnp.swapaxes(a[:, :, 4 * D : 4 * D + 4], 1, 2),
        a[:, :, : 3 * D],
        a[:, :, 3 * D : 4 * D],
        bc[0].transpose(1, 0, 2),
        bc[1].transpose(1, 2, 0),
    )


def body(inputs, lengths, norm_params, attn_in, attn_out, mlp_in, mlp_out, cotangent):
    wide = lax.axis_index("wide")
    narrow = lax.axis_index("narrow")
    core, low, z = wide % 2, (wide // 2) % 2, wide // 4
    x, high = narrow // 2, narrow % 2
    y = high * 2 + low
    length = lax.dynamic_index_in_dim(lengths[:, 0], high, 0, keepdims=False)
    near = [1 + (v + core) % 2 for v in (x, y, z)]
    place = jnp.stack([x, high, length] + near + [low]).astype(jnp.int32)

    def weights_of(blocks):
        return blocks + [with_core(v) for v in blocks]

    def behind(values, done):
        return list(after(values, done))

    slot = jnp.arange(D, dtype=jnp.int32)
    step = jnp.array([0, 1, 3, 2], jnp.int32)
    own_order = ((x + step[slot // 192]) % 4) * 192 + ((high + (slot // 96) % 2) % 2) * 96 + slot % 96
    row_core = (core + slot // 384) % 2
    row_y = (y + step[(slot // 96) % 4]) % 4
    row_z = (z + step[(slot // 24) % 4]) % 4
    row_x = (x + step[(slot // 6) % 4]) % 4
    row_order = 6 * index_of(row_z, row_y, row_core, row_x) + slot % 6
    pa = (own_order[:, None] == row_order[None, :]).astype(BF)
    po = (slot[:, None] == row_order[None, :]).astype(BF)
    p2 = (slot[:, None] == own_order[None, :]).astype(BF)

    def mine_and_other(values):
        mine = lax.dynamic_index_in_dim(values[:, 0], high, 0, keepdims=False)
        return mine, lax.dynamic_index_in_dim(values[:, 0], 1 - high, 0, keepdims=False)

    def in_own_order(mine, came):
        return dot(jnp.concatenate([mine, came], 0), p2)

    mine, other = mine_and_other(inputs)
    other = fetch(other, "y", 2)
    hidden = in_own_order(mine, other)
    around, beside = weights_around(
        place, norm_params, attn_in, attn_out, mlp_in, mlp_out, [other]
    )
    grad_mine, grad_other = mine_and_other(cotangent)
    a_around, *bc_around = around[0]
    a_near, a_far = swap(a_around, "y", 1), swap(a_around, "y", -1)
    a_near, a_far = after([a_near, a_far], [pa, po, p2, hidden] + beside)
    bc_pair = join(bc_around, swaps(bc_around, "xz", 1), [a_near] + around[1])
    (a_last,) = after([swap(a_near, "y", -1)], bc_pair)
    a_weights = [weights_of([a_around, a_near, a_far, a_last])]
    bc_far = swaps(bc_pair, "xz", -1)
    weights = [None, None]
    records = []
    for layer in range(2):
        a1p_keep, a1p_send, gains, *pieces = run_kernel(
            qkv_kernel,
            [place, hidden, pa] + a_weights[layer],
            [shaped(TOKENS, 384), shaped(TOKENS, 384), shaped(8, D, dtype=F32)]
            + [shaped(576, TOKENS)] * 4,
            (
                pltpu.VMEM((D, 3 * D), BF),
                pltpu.VMEM((D, 128), BF),
                pltpu.VMEM((3 * D, TOKENS), BF),
                pltpu.SemaphoreType.DMA((16,)),
            ),
            flops=4 * UNIT,
            any_count=8,
        )
        blocks = order(place, bc_pair, bc_far, "xz", done=[a1p_keep])
        turned = exchange_four(pieces)
        blocks = behind(blocks, turned[1:])
        cores = [with_core(v) for v in blocks]
        weights[layer] = a_weights[layer] + [blocks[0], cores[0], blocks[1], cores[1]]
        if layer == 0:
            held = behind(around[1], turned[1:])
            first = swaps(held, LAST, 1)
        else:
            (grad_other,) = after([grad_other], turned[1:])
            grad_other = fetch(grad_other, "y", 2)
        *mixed, sums = run_kernel(
            attend_kernel,
            [place] + turned,
            [shaped(GROUP, TOKENS)] * 4 + [shaped(3, 1024, dtype=F32)],
            flops=ATTEND,
        )
        if layer == 0:
            mixed = behind(mixed, first)
        mixed = behind(mixed, cores)
        back = exchange_four(mixed)
        if layer == 0:
            bc_pair = behind(join(held[1:], first[1:]), back[1:])
            a_own, a_near = after([held[0], first[0]], back[1:])
            a_far, a_last = swap(a_own, "y", -1), swap(a_near, "y", -1)
            bc_far = swaps(bc_pair, "xz", -1)
        inputs = [place, hidden] + back + [a1p_send, po, p2, gains]
        whole, wide_rows = shaped(TOKENS, D, dtype=F32), shaped(TOKENS, FF)
        if layer == 0:
            h1, following, slope, forward_send, op_keep, act_keep = run_kernel(
                mlp_kernel,
                inputs + weights[layer],
                [whole, whole, wide_rows, wide_rows, shaped(TOKENS, 384), shaped(TOKENS, 1536)],
                MLP_SCRATCH,
                flops=11 * UNIT,
                any_count=12,
            )
            a_far, a_last = after([a_far, a_last], [following])
            forward0 = forward_send, with_core(forward_send)
            a_weights.append(weights_of([a_own, a_near, a_far, a_last]))
        else:
            grad = in_own_order(grad_mine, grad_other)
            following, forward_send, op_keep, act_keep, g1, back_send, dpre_keep, norm2, *pieces = (
                run_kernel(
                    mlp_turn_kernel,
                    inputs + [grad] + weights[layer],
                    [whole, wide_rows, shaped(TOKENS, 384), shaped(TOKENS, 1536)]
                    + [whole, wide_rows, shaped(TOKENS, 1536), shaped(8, D, dtype=F32)]
                    + [shaped(GROUP, TOKENS)] * 4,
                    MLP_SCRATCH + (pltpu.VMEM((TOKENS, FF), BF),),
                    flops=22 * UNIT,
                    any_count=12,
                    done=[forward0[1]],
                )
            )
        records.append(
            (hidden, a1p_keep, gains, turned, mixed, sums, forward_send, op_keep, act_keep)
        )
        hidden = following

    def leave(values, ahead, dtype):
        values = jnp.dot(
            values, p2.astype(F32).T, precision=lax.Precision.HIGHEST, preferred_element_type=F32
        )
        (far,) = after([values[128:].astype(dtype)], list(ahead))
        return values[:128], fetch(far, "y", 2)

    def arrange(own, came):
        return jnp.stack(
            [jnp.where(high == 0, own, came), jnp.where(high == 0, came, own)]
        )[:, None]

    def mlp_gradients(forward, back, act_keep, dpre_keep):
        return run_kernel(
            mlp_grad_kernel,
            [
                place,
                (forward[0], 768, 1),
                (forward[1], 768, 1),
                act_keep,
                (forward[1], 1536, 1),
                dpre_keep,
                (back[1], 1536, 0),
                (back[0], 768, 2),
                (back[1], 768, 2),
            ],
            [shaped(2, 192, 1536)] * 2 + [shaped(2, 768, 384)] * 2,
            flops=8 * UNIT,
        )

    def attend_back(layer, grad_mixed, done):
        turned, mixed, sums = records[layer][3:6]
        return run_kernel(
            attend_back_kernel,
            [place] + turned + grad_mixed + mixed + [sums],
            [shaped(576, TOKENS)] * 4,
            flops=3 * ATTEND,
            done=done,
        )

    def qkv_back(layer, grad_pieces, g1, norm2, done):
        hidden, gains = records[layer][0], records[layer][2]
        return run_kernel(
            qkv_back_kernel,
            [place] + grad_pieces + [hidden, g1, gains, pa, norm2] + a_weights[layer],
            [shaped(TOKENS, D, dtype=F32), shaped(3 * D + 48, TOKENS)],
            (pltpu.VMEM((D, 3 * D), BF), pltpu.SemaphoreType.DMA((8,))),
            flops=5 * UNIT,
            any_count=8,
            done=done,
        )

    def attn_gradients(forward, back, a1p_keep, op_keep, dqkv, done=()):
        return run_kernel(
            attn_grad_kernel,
            [
                place,
                a1p_keep,
                (forward[1], 384, 0),
                op_keep,
                (forward[1], 384, 1),
                (back[0], 768, 3),
                (back[1], 768, 3),
                dqkv[0],
                dqkv[1],
                pa,
            ],
            [shaped(2, 96, ROW_A)] * 2,
            flops=4 * UNIT,
            done=done,
        )

    forward_send, op_keep, act_keep = records[1][6:]
    a1p_keep = records[1][1]
    forward = forward_send, with_core(forward_send)
    grad_mixed = exchange_four(pieces)
    back = back_send, with_core(back_send)
    b1_mine, b1_send, c1_mine, c1_send = mlp_gradients(forward, back, act_keep, dpre_keep)
    b1_send, c1_send = after([b1_send, c1_send], grad_mixed[1:])
    b1_came, c1_came = swap(b1_send, "x", -1), swap(c1_send, "z", -1)
    outputs = leave(hidden, grad_mixed[1:], F32)
    pieces = attend_back(1, grad_mixed, [b1_mine])
    pieces = after(pieces, [outputs[1], b1_came, c1_came])
    grad_pieces = exchange_four(pieces)
    (b1_keep, c1_keep), (b1_send, c1_send) = halved([b1_mine, c1_mine], [b1_came, c1_came])
    dqkv, g1, back_send0, dpre_keep0, norm2, *pieces = run_kernel(
        qkv_back_into_mlp_kernel,
        [place] + grad_pieces + [records[1][0], g1, records[1][2], pa, norm2]
        + [slope, h1, records[0][2], p2, po] + a_weights[1] + weights[0],
        [shaped(3 * D + 48, TOKENS), whole, wide_rows]
        + [shaped(TOKENS, 1536), shaped(8, D, dtype=F32)]
        + [shaped(GROUP, TOKENS)] * 4,
        MLP_SCRATCH + (pltpu.VMEM((D, 3 * D), BF), pltpu.SemaphoreType.DMA((8,))),
        flops=16 * UNIT,
        any_count=20,
        done=[b1_keep],
    )
    dqkv = dqkv, with_core(dqkv)

    _, op_keep0, act_keep0 = records[0][6:]
    a1p_keep0 = records[0][1]
    grad_mixed = exchange_four(pieces)
    a1_mine, a1_send = attn_gradients(forward, back, a1p_keep, op_keep, dqkv)
    a1_send, b1_send, c1_send = after([a1_send, b1_send, c1_send], grad_mixed[1:])
    a1_came = swap(a1_send, "y", -1)
    b1_came, c1_came = swap(b1_send, "x", 1), swap(c1_send, "z", 1)
    pieces = attend_back(0, grad_mixed, [a1_mine])
    pieces = after(pieces, [a1_came, b1_came, c1_came])
    dpre_keep0, back_send0 = after([dpre_keep0, back_send0], pieces[:1])
    back0 = back_send0, with_core(back_send0)
    grad_pieces = exchange_four(pieces)
    b0_mine, b0_send, c0_mine, c0_send = mlp_gradients(forward0, back0, act_keep0, dpre_keep0)
    (a1_keep,), (a1_send,) = halved([a1_mine], [a1_came], [b0_mine])
    a1_send, b0_send, c0_send = after([a1_send, b0_send, c0_send], grad_pieces[1:])
    a1_came = swap(a1_send, "y", 1)
    b0_came, c0_came = swap(b0_send, "x", -1), swap(c0_send, "z", -1)
    grad, dqkv = qkv_back(0, grad_pieces, g1, norm2, [b0_mine, a1_keep])
    grad, dqkv = after([grad, dqkv], [a1_came])
    dqkv = dqkv, with_core(dqkv)
    grad_own, grad_far = leave(grad, [], BF)
    a0_mine, a0_send = attn_gradients(
        forward0, back0, a1p_keep0, op_keep0, dqkv
    )
    (a0_send,) = after([a0_send], [grad_far])
    a0_came = swap(a0_send, "y", -1)
    (a0_keep, b0_keep, c0_keep), (a0_send, b0_send, c0_send) = halved(
        [a0_mine, b0_mine, c0_mine], [a0_came, b0_came, c0_came]
    )
    a0_came = swap(a0_send, "y", 1)
    b0_came, c0_came = swap(b0_send, "x", 1), swap(c0_send, "z", 1)
    weight_grads = gradients_home(
        place,
        [total(a0_keep, a0_came), total(a1_keep, a1_came)],
        [[b0_keep, b0_came], [b1_keep, b1_came]],
        [[c0_keep, c0_came], [c1_keep, c1_came]],
    )
    grad_inputs = grad_own, grad_far.astype(F32)
    return (arrange(*outputs), arrange(*grad_inputs)) + weight_grads


def solution(mesh):
    in_specs = (
        P(None, "wide", "narrow", None),
        P(None, "wide"),
        P(None, None, ("wide", "narrow")),
        P(None, ("wide", "narrow"), None),
        P(None, ("wide", "narrow"), None),
        P(None, "narrow", "wide"),
        P(None, "wide", "narrow"),
        P(None, "wide", "narrow", None),
    )
    out_specs = (
        P(None, "wide", "narrow", None),
        P(None, "wide", "narrow", None),
        P(None, None, ("wide", "narrow")),
        P(None, ("wide", "narrow"), None),
        P(None, ("wide", "narrow"), None),
        P(None, "narrow", "wide"),
        P(None, "wide", "narrow"),
    )
    return jax.shard_map(body, mesh=mesh, in_specs=in_specs, out_specs=out_specs, check_vma=False)
```

```python
import functools

import jax
import jax.numpy as jnp
from jax import lax
from jax.experimental import pallas as pl
from jax.experimental.pallas import tpu as pltpu
from jax.sharding import PartitionSpec as P

D = 768
FF = 3072
HEAD_DIM = 64
GROUP = 192
TOKENS = 256
SPAN = 1024
SPAN_BACK = 512
EPS = 1e-06
ROOT_HALF = 0.7071067811865476
INV_ROOT_TWO_PI = 0.3989422804014327
ROW_A = 3200
BF = jnp.bfloat16
F32 = jnp.float32
AXES = ("wide", "narrow")
VMEM_LIMIT = 56 * 1024 * 1024


def index_of(z, y, c, x):
    return ((z * 2 + y % 2) * 2 + c) * 8 + x * 2 + y // 2


def everywhere():
    for z in range(4):
        for y in range(4):
            for c in range(2):
                for x in range(4):
                    yield {"z": z, "y": y, "c": c, "x": x}


def fetch(value, axis, step):
    pairs = []
    for here in everywhere():
        there = dict(here)
        there[axis] = (here[axis] + step) % (2 if axis == "c" else 4)
        pairs.append((index_of(**there), index_of(**here)))
    return lax.ppermute(value, AXES, pairs)


def swap(value, axis, side):
    pairs = []
    for here in everywhere():
        step = side if (here[axis] + here["c"]) % 2 == 0 else -side
        there = dict(here)
        there[axis] = (here[axis] + step) % 4
        pairs.append((index_of(**here), index_of(**there)))
    return lax.ppermute(value, AXES, pairs)


def exchange_four(pieces):
    return [pieces[0]] + [fetch(pieces[4 - k], "x", k) for k in (1, 2, 3)]


def dot(left, right, over_left=1, over_right=0):
    return lax.dot_general(
        left, right, (((over_left,), (over_right,)), ((), ())), preferred_element_type=F32
    )


def dot_two(left, right, over_left=1, over_right=0):
    high = left.astype(BF)
    low = (left - high.astype(F32)).astype(BF)
    return dot(high, right, over_left, over_right) + dot(low, right, over_left, over_right)


def normed(values):
    average = jnp.mean(values, -1, keepdims=True)
    centred = values - average
    spread = jnp.mean(centred * centred, -1, keepdims=True)
    scale = lax.rsqrt(spread + EPS)
    return centred * scale, scale


def norm_back(grad, values, gain_row):
    z, scale = normed(values)
    dz = grad * gain_row
    out = (
        dz - jnp.mean(dz, -1, keepdims=True) - z * jnp.mean(dz * z, -1, keepdims=True)
    ) * scale
    gain_grad = jnp.sum(grad * z, 0, keepdims=True)
    offset_grad = jnp.sum(grad, 0, keepdims=True)
    return out, gain_grad, offset_grad


def two_rows(first, second):
    return jnp.concatenate([first, second, jnp.zeros((6, D), F32)], 0)


def group_start(x, k, base=0):
    return pl.multiple_of(base + lax.rem(x + k, 4) * GROUP, GROUP)


def start_copies(pairs, sems):
    copies = [
        pltpu.make_async_copy(source, target, sems.at[i])
        for i, (source, target) in enumerate(pairs)
    ]
    for copy in copies:
        copy.start()
    return copies


def wait_copies(copies):
    for copy in copies:
        copy.wait()


X, HIGH, LENGTH, NEAR_X, NEAR_Y, NEAR_Z, LOW = range(7)


def weight_blocks(refs, near):
    spots = [0, near, 3 - near, 3, 0, 3 - near, near, 3]
    return [(ref, n // 4, spot) for n, (ref, spot) in enumerate(zip(refs, spots))]


def at_rows(core, spot, rows):
    return pl.ds(pl.multiple_of((core * 4 + spot) * rows, rows), rows)


def qkv_kernel(place_ref, h_ref, pa_ref, *refs):
    blocks = weight_blocks(refs[:8], place_ref[NEAR_Y])
    a1p_keep, a1p_send, gains_ref = refs[8:11]
    out_refs = refs[11:15]
    win, table, turned, sems = refs[15:]
    norm_copies = start_copies(
        [
            (r.at[:, pl.ds(FF, 128)], table.at[at_rows(core, spot, 96)])
            for r, core, spot in blocks
        ],
        sems.at[pl.ds(0, 8)],
    )
    win_copies = start_copies(
        [
            (r.at[:, pl.ds(0, 3 * D)], win.at[at_rows(core, spot, 96)])
            for r, core, spot in blocks
        ],
        sems.at[pl.ds(8, 8)],
    )
    z, _ = normed(h_ref[...])
    wait_copies(norm_copies)
    gains = dot(table[...], pa_ref[...], 0, 1)[0:8]
    gains_ref[...] = gains
    a1 = (z * gains[0:1] + gains[1:2]).astype(BF)
    a1p = dot(a1, pa_ref[...]).astype(BF)
    a1p_keep[...] = a1p[:, :384]
    a1p_send[...] = a1p[:, 384:]
    wait_copies(win_copies)
    for c in range(3):
        part = dot(a1p, win[:, c * D : (c + 1) * D])
        if c == 0:
            part = part * HEAD_DIM ** (-0.5)
        turned[c * D : (c + 1) * D, :] = part.astype(BF).T
    x = place_ref[X]
    for k in range(4):
        for c in range(3):
            out_refs[k][c * GROUP : (c + 1) * GROUP, :] = turned[
                pl.ds(group_start(x, k, c * D), GROUP), :
            ]


def mask_row(place_ref):
    x, yh, length = place_ref[X], place_ref[HIGH], place_ref[LENGTH]
    rows = []
    for k in range(4):
        for half in range(2):
            start = lax.rem(x + k, 4) * 256 + lax.rem(yh + half, 2) * 128
            slot = start + lax.broadcasted_iota(jnp.int32, (1, 128), 1)
            rows.append(jnp.where(slot < length, 0.0, -1e30))
    return jnp.concatenate(rows, 1)


def side_by_side(refs, start):
    return jnp.concatenate([r[start : start + HEAD_DIM, :] for r in refs], 1)


def with_rows(block, rows):
    count, width = len(rows), block.shape[1]
    tail = jnp.concatenate(rows + [jnp.zeros((16 - count, width), F32)], 0).astype(BF)
    return jnp.concatenate([block, tail], 0)


def in_three(row):
    high = row.astype(BF).astype(F32)
    middle = (row - high).astype(BF).astype(F32)
    return [high, middle, row - high - middle]


def attend_kernel(place_ref, t0, t1, t2, t3, u0, u1, u2, u3, sums_ref):
    t_refs, u_refs = (t0, t1, t2, t3), (u0, u1, u2, u3)
    mask = mask_row(place_ref)
    count = SPAN // TOKENS
    ones = jnp.ones((1, SPAN), F32)
    for j in range(3):
        keys = with_rows(side_by_side(t_refs, GROUP + j * HEAD_DIM), [mask]).T
        values_t = side_by_side(t_refs, 2 * GROUP + j * HEAD_DIM)
        rows = slice(j * HEAD_DIM, (j + 1) * HEAD_DIM)
        for b in range(0, 4, count):
            query_t = side_by_side(t_refs[b : b + count], j * HEAD_DIM)
            scores = dot(keys, with_rows(query_t, [ones]))
            peak = jnp.max(scores, 0, keepdims=True)
            expont = jnp.exp(scores - peak)
            total = jnp.sum(expont, 0, keepdims=True)
            mixed = (dot(values_t, expont.astype(BF)) / total).astype(BF)
            for n in range(count):
                u_refs[b + n][rows, :] = mixed[:, n * TOKENS : (n + 1) * TOKENS]
            sums_ref[j : j + 1, b * TOKENS : (b + count) * TOKENS] = peak + jnp.log(total)


def attend_back_kernel(place_ref, *refs):
    t_refs, g_refs, u_refs = refs[0:4], refs[4:8], refs[8:12]
    sums_ref = refs[12]
    out_refs = refs[13:17]
    mask = mask_row(place_ref)
    count = SPAN_BACK // TOKENS
    ones = jnp.ones((1, SPAN_BACK), F32)
    one_row = jnp.ones((1, 4 * TOKENS), F32)
    for j in range(3):
        keys_t = side_by_side(t_refs, GROUP + j * HEAD_DIM)
        keys = with_rows(keys_t, [mask] + [one_row] * 3).T
        values = with_rows(side_by_side(t_refs, 2 * GROUP + j * HEAD_DIM), [one_row] * 3).T
        grad_keys = jnp.zeros((4 * TOKENS, HEAD_DIM), F32)
        grad_values = jnp.zeros((4 * TOKENS, HEAD_DIM), F32)
        rows = slice(j * HEAD_DIM, (j + 1) * HEAD_DIM)
        for b in range(0, 4, count):
            query_t = side_by_side(t_refs[b : b + count], j * HEAD_DIM)
            grad_t = side_by_side(g_refs[b : b + count], j * HEAD_DIM)
            mixed_t = side_by_side(u_refs[b : b + count], j * HEAD_DIM)
            sums = sums_ref[j : j + 1, b * TOKENS : (b + count) * TOKENS]
            delta = jnp.sum(grad_t.astype(F32) * mixed_t.astype(F32), 0, keepdims=True)
            probs = jnp.exp(dot(keys, with_rows(query_t, [ones] + in_three(-sums))))
            grad_probs = dot(values, with_rows(grad_t, in_three(-delta)))
            grad_scores = (probs * grad_probs).astype(BF)
            grad_values = grad_values + dot(probs.astype(BF), grad_t, 1, 1)
            grad_keys = grad_keys + dot(grad_scores, query_t, 1, 1)
            grad_query = (dot(keys_t, grad_scores) * HEAD_DIM ** (-0.5)).astype(BF)
            for n in range(count):
                out_refs[b + n][rows, :] = grad_query[:, n * TOKENS : (n + 1) * TOKENS]
        grad_keys = grad_keys.astype(BF).T
        grad_values = grad_values.astype(BF).T
        for b in range(4):
            columns = slice(b * TOKENS, (b + 1) * TOKENS)
            start = GROUP + j * HEAD_DIM
            out_refs[b][start : start + HEAD_DIM, :] = grad_keys[:, columns]
            start = 2 * GROUP + j * HEAD_DIM
            out_refs[b][start : start + HEAD_DIM, :] = grad_values[:, columns]


def mlp_copies(place_ref, refs, wout, w1, w2, sems):
    out_copies = start_copies(
        [
            (r.at[:, pl.ds(3 * D, D)], wout.at[at_rows(core, spot, 96)])
            for r, core, spot in weight_blocks(refs[0:8], place_ref[NEAR_Y])
        ],
        sems.at[pl.ds(0, 8)],
    )
    first_copies = start_copies(
        [
            (ref.at[k], w1.at[core, pl.ds(192 * k, 192)])
            for core, ref in enumerate(refs[8:10])
            for k in range(4)
        ],
        sems.at[pl.ds(8, 8)],
    )
    second_copies = start_copies(
        [
            (ref.at[k], w2.at[:, pl.ds((core * 4 + k) * 384, 384)])
            for core, ref in enumerate(refs[10:12])
            for k in range(4)
        ],
        sems.at[pl.ds(16, 8)],
    )
    return out_copies, first_copies, second_copies


def mlp_forward(place_ref, h, pieces, a1p_send, po_ref, p2_ref, gains_ref, slope_ref, outs, parts):
    send_ref, op_keep, act_keep = outs
    turned, wout, w1, w2, out_copies, first_copies, second_copies = parts
    send_ref[:, 0:384] = a1p_send[...]
    x = place_ref[X]
    for k, piece in enumerate(pieces):
        turned[pl.ds(group_start(x, k), GROUP), :] = piece[...]
    op = dot(turned[...], po_ref[...], 0, 0).astype(BF)
    op_keep[...] = op[:, :384]
    send_ref[:, 384:768] = op[:, 384:]
    wait_copies(out_copies)
    h1 = h + dot_two(dot(op, wout[...]), p2_ref[...])
    z, _ = normed(h1)
    a2 = (z * gains_ref[2:3] + gains_ref[3:4]).astype(BF)
    send_ref[:, 768:1536] = a2
    wait_copies(first_copies)
    total = h1
    for half in range(2):
        pre = dot(a2, w1[half])
        below = 0.5 * (1.0 + lax.erf(pre * ROOT_HALF))
        act = (pre * below).astype(BF)
        slope = below + pre * (jnp.exp(-0.5 * pre * pre) * INV_ROOT_TWO_PI)
        columns = slice(half * 1536, (half + 1) * 1536)
        if half == 0:
            act_keep[...] = act
            wait_copies(second_copies)
        else:
            send_ref[:, 1536:] = act
        slope_ref[:, columns] = slope.astype(BF)
        total = total + dot(act, w2[:, columns], 1, 1)
    return h1, total


def mlp_backward(place_ref, grad, h1, gains_ref, p2_ref, po_ref, slope_ref, outs, parts):
    send_ref, dpre_keep, norm_ref, out_refs = outs
    turned, wout, w1, w2, out_copies, first_copies, second_copies = parts
    grad_low = grad.astype(BF)
    send_ref[:, 1536:2304] = grad_low
    wait_copies(second_copies)
    grad_a2 = jnp.zeros((TOKENS, D), F32)
    for half in range(2):
        columns = slice(half * 1536, (half + 1) * 1536)
        grad_act = dot(grad_low, w2[:, columns])
        dpre = (grad_act * slope_ref[:, columns].astype(F32)).astype(BF)
        if half == 0:
            dpre_keep[...] = dpre
            wait_copies(first_copies)
        else:
            send_ref[:, 0:1536] = dpre
        grad_a2 = grad_a2 + dot(dpre, w1[half], 1, 1)
    dv, gain_grad, offset_grad = norm_back(grad_a2, h1, gains_ref[2:3])
    norm_ref[...] = two_rows(gain_grad, offset_grad)
    g1 = grad + dv
    g1b = dot(g1.astype(BF), p2_ref[...], 1, 1).astype(BF)
    send_ref[:, 2304:] = g1b
    wait_copies(out_copies)
    grad_op = dot(g1b, wout[...], 1, 1).astype(BF)
    turned[...] = dot(po_ref[...], grad_op, 1, 1).astype(BF)
    x = place_ref[X]
    for k in range(4):
        out_refs[k][...] = turned[pl.ds(group_start(x, k), GROUP), :]
    return g1


def mlp_kernel(place_ref, h_ref, u0, u1, u2, u3, a1p_send, po_ref, p2_ref, gains_ref, *refs):
    h1_ref, next_ref, slope_ref, send_ref, op_keep, act_keep = refs[12:18]
    turned, wout, w1, w2, sems = refs[18:]
    copies = mlp_copies(place_ref, refs[:12], wout, w1, w2, sems)
    h1_ref[...], next_ref[...] = mlp_forward(
        place_ref, h_ref[...], (u0, u1, u2, u3), a1p_send, po_ref, p2_ref, gains_ref, slope_ref,
        (send_ref, op_keep, act_keep), (turned, wout, w1, w2) + copies,
    )


def mlp_turn_kernel(
    place_ref, h_ref, u0, u1, u2, u3, a1p_send, po_ref, p2_ref, gains_ref, g_ref, *refs
):
    next_ref, forward_send, op_keep, act_keep, g1_ref, back_send, dpre_keep, norm_ref = refs[12:20]
    out_refs = refs[20:24]
    turned, wout, w1, w2, sems, slope_ref = refs[24:]
    copies = mlp_copies(place_ref, refs[:12], wout, w1, w2, sems)
    h1, next_ref[...] = mlp_forward(
        place_ref, h_ref[...], (u0, u1, u2, u3), a1p_send, po_ref, p2_ref, gains_ref, slope_ref,
        (forward_send, op_keep, act_keep), (turned, wout, w1, w2) + copies,
    )
    g1_ref[...] = mlp_backward(
        place_ref, g_ref[...], h1, gains_ref, p2_ref, po_ref, slope_ref,
        (back_send, dpre_keep, norm_ref, out_refs), (turned, wout, w1, w2, (), (), ()),
    )


def qkv_back_into_mlp_kernel(
    place_ref, d0, d1, d2, d3, h_ref, g1_ref, gains_ref, pa_ref, norm2_ref,
    slope_ref, h1_ref, gains0_ref, p2_ref, po_ref, *refs,
):
    dqkv_ref, next_ref, back_send, dpre_keep, below_ref = refs[20:25]
    out_refs = refs[25:29]
    turned, wout, w1, w2, sems, win, win_sems = refs[29:]
    win_copies = win_start(place_ref, refs[:8], win, win_sems)
    copies = mlp_copies(place_ref, refs[8:20], wout, w1, w2, sems)
    grad = qkv_backward(
        place_ref, (d0, d1, d2, d3), h_ref, g1_ref, gains_ref, pa_ref, norm2_ref,
        dqkv_ref, win, win_copies,
    )
    next_ref[...] = mlp_backward(
        place_ref, grad, h1_ref[...], gains0_ref, p2_ref, po_ref, slope_ref,
        (back_send, dpre_keep, below_ref, out_refs), (turned, wout, w1, w2) + copies,
    )


def both_cores(first_ref, second_ref):
    return jnp.concatenate([first_ref[...], second_ref[...]], 0)


def store_blocks(near, mine, send, columns, blocks):
    mine[0, :, columns] = blocks[0]
    send[1, :, columns] = blocks[3]

    @pl.when(near == 1)
    def _():
        mine[1, :, columns] = blocks[1]
        send[0, :, columns] = blocks[2]

    @pl.when(near == 2)
    def _():
        mine[1, :, columns] = blocks[2]
        send[0, :, columns] = blocks[1]


def store_four(near, out_refs, columns, blocks):
    own, first, other, opposite = out_refs
    own[:, columns] = blocks[0]
    opposite[:, columns] = blocks[3]

    @pl.when(near == 1)
    def _():
        first[:, columns] = blocks[1]
        other[:, columns] = blocks[2]

    @pl.when(near == 2)
    def _():
        first[:, columns] = blocks[2]
        other[:, columns] = blocks[1]


def mlp_grad_kernel(
    place_ref, a2_0, a2_1, act_0, act_1, dpre_0, dpre_1, gb_0, gb_1,
    first_mine, first_send, second_mine, second_send,
):
    a2 = both_cores(a2_0, a2_1)
    grad_low = both_cores(gb_0, gb_1)
    dpre = both_cores(dpre_0, dpre_1)
    for part in range(2):
        columns = slice(part * 768, part * 768 + 768)
        value = dot(a2, dpre[:, columns], 0, 0).astype(BF)
        blocks = [value[192 * k : 192 * k + 192] for k in range(4)]
        store_blocks(place_ref[NEAR_X], first_mine, first_send, columns, blocks)
    act = both_cores(act_0, act_1)
    blocks = [
        dot(grad_low, act[:, 384 * k : 384 * k + 384], 0, 0).astype(BF) for k in range(4)
    ]
    store_blocks(place_ref[NEAR_Z], second_mine, second_send, slice(0, 384), blocks)


def win_start(place_ref, refs, win, sems):
    return start_copies(
        [
            (r.at[:, pl.ds(0, 3 * D)], win.at[at_rows(core, spot, 96)])
            for r, core, spot in weight_blocks(refs, place_ref[NEAR_Y])
        ],
        sems,
    )


def qkv_backward(
    place_ref, pieces, h_ref, g1_ref, gains_ref, pa_ref, norm2_ref, dqkv_ref, win, copies
):
    x = place_ref[X]
    for k, piece in enumerate(pieces):
        for c in range(3):
            dqkv_ref[pl.ds(group_start(x, k, c * D), GROUP), :] = piece[
                c * GROUP : (c + 1) * GROUP, :
            ]
    wait_copies(copies)
    turned = dot(win[...], dqkv_ref[0 : 3 * D, :])
    grad_a1 = dot_two(turned, pa_ref[...], 0, 1)
    dv, gain_grad, offset_grad = norm_back(grad_a1, h_ref[...], gains_ref[0:1])
    norms = jnp.concatenate([gain_grad, offset_grad, norm2_ref[0:2], jnp.zeros((4, D), F32)], 0)
    high = norms.astype(BF)
    norms = jnp.concatenate([high, (norms - high.astype(F32)).astype(BF)], 0)
    for c in range(3):
        dqkv_ref[3 * D + 16 * c : 3 * D + 16 * c + 16, :] = norms[:, 256 * c : 256 * c + 256]
    return g1_ref[...] + dv


def qkv_back_kernel(
    place_ref, d0, d1, d2, d3, h_ref, g1_ref, gains_ref, pa_ref, norm2_ref, *refs
):
    next_ref, dqkv_ref, win, sems = refs[8:]
    copies = win_start(place_ref, refs[:8], win, sems)
    next_ref[...] = qkv_backward(
        place_ref, (d0, d1, d2, d3), h_ref, g1_ref, gains_ref, pa_ref, norm2_ref,
        dqkv_ref, win, copies,
    )


def attn_grad_kernel(
    place_ref, a1p_0, a1p_1, op_0, op_1, g1b_0, g1b_1, dqkv_0, dqkv_1, pa_ref, *out_refs
):
    near = place_ref[NEAR_Y]
    norms = jnp.zeros((8, D), F32)
    for ref in (dqkv_0, dqkv_1):
        pair = [ref[3 * D + 16 * c : 3 * D + 16 * c + 16, :].astype(F32) for c in range(3)]
        pair = jnp.concatenate(pair, 1)
        norms = norms + pair[0:8] + pair[8:16]
    norms = dot_two(norms, pa_ref[:, 0:384])
    norms = jnp.concatenate([norms, jnp.zeros((120, 384), F32)], 0).T.astype(BF)
    a1p = both_cores(a1p_0, a1p_1)
    for c in range(5):
        columns = slice(c * D, min((c + 1) * D, ROW_A))
        if c < 3:
            dqkv = jnp.concatenate(
                [dqkv_0[c * D : (c + 1) * D, :], dqkv_1[c * D : (c + 1) * D, :]], 1
            )
            value = dot(a1p, dqkv, 0, 1).astype(BF)
        elif c == 3:
            value = dot(both_cores(op_0, op_1), both_cores(g1b_0, g1b_1), 0, 0).astype(BF)
        else:
            value = norms
        blocks = [value[96 * k : 96 * k + 96] for k in range(4)]
        store_four(near, out_refs, columns, blocks)


def join_kernel(*refs):
    count = (len(refs) - 1) // 3
    pairs = []
    for own, came, out in zip(refs[:count], refs[count : 2 * count], refs[2 * count : -1]):
        pairs += [(own, out.at[0]), (came, out.at[1])]
    wait_copies(start_copies(pairs, refs[-1]))


def order_kernel(spots, place_ref, *refs):
    count = len(spots)
    pairs = []
    for spot, pair, far, out in zip(
        spots, refs[:count], refs[count : 2 * count], refs[2 * count : -1]
    ):
        near = place_ref[spot]
        pairs += [
            (pair.at[0], out.at[0]),
            (pair.at[1], out.at[near]),
            (far.at[0], out.at[3 - near]),
            (far.at[1], out.at[3]),
        ]
    wait_copies(start_copies(pairs, refs[-1]))


def layer_blocks_kernel(
    layer, place_ref, b_pair, c_pair, b_far, c_far, first_ref, second_ref
):
    middle = 1 + place_ref[LOW]
    near_z = place_ref[NEAR_Z]
    straight = place_ref[NEAR_Y] == middle
    part = slice(layer * 192, layer * 192 + 192)
    b_slots = ((b_pair, 0, 0), (b_pair, 1, near_z), (b_far, 0, 3 - near_z), (b_far, 1, 3))
    for high in range(2):
        one, two = (0, middle) if high == 0 else (3, 3 - middle)
        for ref, i, spot in b_slots:
            both = [ref[i, one][:, part], ref[i, two][:, part]]
            first_ref[
                high * 96 : high * 96 + 96, pl.ds(pl.multiple_of(spot * 384, 384), 384)
            ] = jnp.concatenate(both, 1)
        for k in range(4):
            outer = c_pair[0, k] if high == 0 else c_far[1, k]
            near, other = c_pair[1, k], c_far[0, k]
            if high == 0:
                inner = jnp.where(straight, near, other)
            else:
                inner = jnp.where(straight, other, near)
            start = (2 * k + high) * 96
            second_ref[start : start + 96, :] = jnp.concatenate(
                [outer[:, part], inner[:, part]], 1
            )


def both_layers_kernel(place_ref, *refs):
    b0, b0_came, c0, c0_came, b1, b1_came, c1, c1_came = refs[:8]
    b_mine, b_send, c_mine, c_send = refs[8:]
    middle = 1 + place_ref[LOW]
    near_z, near_x = place_ref[NEAR_Z], place_ref[NEAR_X]

    def put(mine, send, near, spot, index, value):
        if isinstance(spot, int) and spot == 0:
            mine[0, index] = value
        elif isinstance(spot, int) and spot == 3:
            send[1, index] = value
        else:

            @pl.when(near == spot)
            def _():
                mine[1, index] = value

            @pl.when(near != spot)
            def _():
                send[0, index] = value

    for high in range(2):
        for k in range(4):
            rows, columns = slice(high * 96, high * 96 + 96), slice(k * 384, k * 384 + 384)
            b_parts = [
                total_of(b0[rows, columns], b0_came[rows, columns]),
                total_of(b1[rows, columns], b1_came[rows, columns]),
            ]
            rows = slice((2 * k + high) * 96, (2 * k + high) * 96 + 96)
            c_parts = [
                total_of(c0[rows, :], c0_came[rows, :]),
                total_of(c1[rows, :], c1_came[rows, :]),
            ]
            for part in range(2):
                if part == 0:
                    spot = 0 if high == 0 else 3
                else:
                    spot = middle if high == 0 else 3 - middle
                columns = slice(part * 192, part * 192 + 192)
                value = jnp.concatenate([v[:, columns] for v in b_parts], 1)
                put(b_mine, b_send, near_z, k, spot, value)
                value = jnp.concatenate([v[:, columns] for v in c_parts], 1)
                put(c_mine, c_send, near_x, k, spot, value)


def split_kernel(spots, place_ref, *refs):
    count = len(spots)
    for n, spot in enumerate(spots):
        near = place_ref[spot]
        value, mine, send = refs[n], refs[count + 2 * n], refs[count + 2 * n + 1]
        mine[0] = value[0]
        mine[1] = value[near]
        send[0] = value[3 - near]
        send[1] = value[3]


def total_of(first, second):
    return (first.astype(F32) + second.astype(F32)).astype(BF)


def halve_kernel(*refs):
    count = len(refs) // 4
    for n in range(count):
        mine, came = refs[n], refs[count + n]
        keep, send = refs[2 * count + 2 * n], refs[2 * count + 2 * n + 1]
        keep[...] = total_of(mine[0], came[0])
        send[...] = total_of(mine[1], came[1])


def total_pair_kernel(b_keep, b_came, c_keep, c_came, *out_refs):
    for k, out in enumerate(out_refs):
        out[0] = total_of(b_keep[k], b_came[k])
        out[1] = total_of(c_keep[k], c_came[k])


def total_kernel(keep, came, *out_refs):
    for k, out in enumerate(out_refs):
        out[...] = total_of(keep[k], came[k])


def sum_kernel(first, second, out):
    out[...] = total_of(first[...], second[...])


def nothing_kernel(*refs):
    pass


def after(values, done):
    anywhere = pl.BlockSpec(memory_space=pl.ANY)
    return pl.pallas_call(
        nothing_kernel,
        out_shape=tuple(jax.ShapeDtypeStruct(v.shape, v.dtype) for v in values),
        in_specs=[anywhere] * (len(values) + len(done)),
        out_specs=tuple(anywhere for _ in values),
        input_output_aliases={i: i for i in range(len(values))},
    )(*values, *done)


def shaped(*shape, dtype=BF):
    return jax.ShapeDtypeStruct(shape, dtype)


def like(value, *lead):
    return jax.ShapeDtypeStruct(tuple(lead) + tuple(value.shape), value.dtype)


def run_kernel(
    kernel, inputs, outs, scratch=(), flops=0, any_count=0, scalars=True, lying=False, done=()
):
    specs, arrays, moved = [], [], 0
    anywhere = pl.BlockSpec(memory_space=pl.ANY)
    for i, value in enumerate(inputs):
        if isinstance(value, tuple):
            value, width, index = value
            specs.append(pl.BlockSpec((value.shape[0], width), lambda _, n=index: (0, n)))
            moved += value.shape[0] * width * value.dtype.itemsize
        elif scalars and i == 0:
            specs.append(pl.BlockSpec(memory_space=pltpu.SMEM))
        else:
            lies = lying or i >= len(inputs) - any_count
            specs.append(anywhere if lies else pl.BlockSpec(memory_space=pltpu.VMEM))
            moved += value.size * value.dtype.itemsize
        arrays.append(value)
    moved += sum(v.size * v.dtype.itemsize for v in outs)
    count, extra = len(inputs), len(done)

    def whole(*refs):
        kernel(*refs[:count], *refs[count + extra :])

    return pl.pallas_call(
        whole,
        grid=(1,),
        out_shape=tuple(outs),
        in_specs=specs + [anywhere] * extra,
        out_specs=tuple(
            pl.BlockSpec(memory_space=pltpu.VMEM) for _ in outs
        ),
        scratch_shapes=list(scratch),
        compiler_params=pltpu.CompilerParams(vmem_limit_bytes=VMEM_LIMIT),
        cost_estimate=pl.CostEstimate(
            flops=flops, bytes_accessed=moved if flops else 0, transcendentals=0
        ),
    )(*arrays, *done)


MLP_SCRATCH = (
    pltpu.VMEM((D, TOKENS), BF),
    pltpu.VMEM((D, D), BF),
    pltpu.VMEM((2, D, 1536), BF),
    pltpu.VMEM((D, FF), BF),
    pltpu.SemaphoreType.DMA((24,)),
)
UNIT = 2 * TOKENS * D * D
ATTEND = 2 * 3 * 1024 * 1024 * HEAD_DIM * 4


NEAR = {"x": NEAR_X, "y": NEAR_Y, "z": NEAR_Z}


def swaps(values, axes, side):
    return [swap(v, axis, side) for v, axis in zip(values, axes)]


def join(values, came, done=()):
    return list(
        run_kernel(
            join_kernel,
            values + came,
            [like(v, 2) for v in values],
            (pltpu.SemaphoreType.DMA((2 * len(values),)),),
            scalars=False,
            lying=True,
            done=done,
        )
    )


def order(place, pairs, far, axes, done=()):
    return list(
        run_kernel(
            functools.partial(order_kernel, [NEAR[axis] for axis in axes]),
            [place] + pairs + far,
            [like(v[0], 4) for v in pairs],
            (pltpu.SemaphoreType.DMA((4 * len(pairs),)),),
            lying=True,
            done=done,
        )
    )


def padded(value):
    return jnp.pad(value.reshape(300, 128), ((0, 4), (0, 0)))


def weights_around(place, norm_params, attn_in, attn_out, mlp_in, mlp_out, early):
    norm_part = jnp.pad(jnp.swapaxes(norm_params, 1, 2), ((0, 0), (0, 0), (0, 124)))
    a = padded(jnp.concatenate([attn_in, attn_out, norm_part], -1))
    bc = [mlp_in.transpose(1, 0, 2).reshape(96, 384), mlp_out.transpose(2, 0, 1).reshape(96, 384)]
    for a_axis, bc_axes in (("z", "yx"), ("x", "zy")):
        bc_near = swaps(bc, bc_axes, 1)
        a_pair = join([a], [swap(a, a_axis, 1)], done=bc_near if early else bc)
        bc_pair = join(bc, bc_near, done=a_pair + early)
        early = []
        a_far = swap(a_pair[0], a_axis, -1)
        bc_far = swaps(bc_pair, bc_axes, -1)
        (a,) = order(place, a_pair, [a_far], a_axis, done=bc_pair)
        if a_axis == "z":
            bc = order(place, bc_pair, bc_far, bc_axes, done=[a])
    a = a[:, :, :300].reshape(4, 4, 2, 6, ROW_A)
    layers = []
    for layer in range(2):
        al = a[:, :, layer].transpose(1, 0, 2, 3).reshape(96, ROW_A)
        bl, cl = run_kernel(
            functools.partial(layer_blocks_kernel, layer),
            [place] + bc_pair + bc_far,
            [shaped(192, 1536), shaped(768, 384)],
            done=[al],
        )
        layers.append([al, bl, cl])
    return layers, bc_far


LAST = "yxz"


def with_core(value):
    return fetch(value, "c", 1)


def halved(mine, came, done=()):
    outs = [like(v[0]) for v in mine for _ in range(2)]
    out = run_kernel(halve_kernel, list(mine) + list(came), outs, scalars=False, done=done)
    return list(out[0::2]), list(out[1::2])


def summed(first, second, done=()):
    (out,) = run_kernel(sum_kernel, [first, second], [like(first)], scalars=False, done=done)
    return out


def total(*terms):
    return sum(v.astype(F32) for v in terms).astype(BF)


def gradients_home(place, a_layers, b_layers, c_layers):
    parts = [v.reshape(4, 4, 6, ROW_A).transpose(1, 0, 2, 3) for v in a_layers]
    a = jnp.stack(parts, 2).reshape(4, 4, 300, 128)
    a = jnp.pad(a, ((0, 0), (0, 0), (0, 4), (0, 0)))
    a_mine, a_send = run_kernel(
        functools.partial(split_kernel, [NEAR_X]), [place, a], [like(a[0], 2)] * 2
    )
    a_came = swap(a_send, "x", -1)
    b_mine, b_send, c_mine, c_send = run_kernel(
        both_layers_kernel,
        [place] + b_layers[0] + c_layers[0] + b_layers[1] + c_layers[1],
        [shaped(2, 4, 96, 384)] * 4,
    )
    keep, send = halved([b_mine, c_mine], swaps([b_send, c_send], "zx", -1))
    came = swaps(send, "zx", 1)
    (a_keep,), (a_send,) = halved([a_mine], [a_came])
    parts = run_kernel(
        total_pair_kernel,
        [keep[0], came[0], keep[1], came[1]],
        [shaped(2, 96, 384)] * 4,
        scalars=False,
    )
    bc = parts[0].astype(F32)
    for part, step in zip(parts[1:], (-1, 1, 2)):
        bc = bc + fetch(part, "y", step).astype(F32)
    parts = run_kernel(
        total_kernel, [a_keep, swap(a_send, "x", 1)], [like(a_keep[0])] * 4, scalars=False
    )
    a = parts[0].astype(F32)
    for part, step in zip(parts[1:], (-1, 1, 2)):
        a = a + fetch(part, "z", step).astype(F32)
    a = a[:300].reshape(2, 6, ROW_A)
    bc = bc.reshape(2, 96, 2, 192)
    return (
        jnp.swapaxes(a[:, :, 4 * D : 4 * D + 4], 1, 2),
        a[:, :, : 3 * D],
        a[:, :, 3 * D : 4 * D],
        bc[0].transpose(1, 0, 2),
        bc[1].transpose(1, 2, 0),
    )


def body(inputs, lengths, norm_params, attn_in, attn_out, mlp_in, mlp_out, cotangent):
    wide = lax.axis_index("wide")
    narrow = lax.axis_index("narrow")
    core, low, z = wide % 2, (wide // 2) % 2, wide // 4
    x, high = narrow // 2, narrow % 2
    y = high * 2 + low
    length = lax.dynamic_index_in_dim(lengths[:, 0], high, 0, keepdims=False)
    near = [1 + (v + core) % 2 for v in (x, y, z)]
    place = jnp.stack([x, high, length] + near + [low]).astype(jnp.int32)

    def weights_of(blocks):
        return blocks + [with_core(v) for v in blocks]

    def behind(values, done):
        return list(after(values, done))

    slot = jnp.arange(D, dtype=jnp.int32)
    step = jnp.array([0, 1, 3, 2], jnp.int32)
    own_order = ((x + step[slot // 192]) % 4) * 192 + ((high + (slot // 96) % 2) % 2) * 96 + slot % 96
    row_core = (core + slot // 384) % 2
    row_y = (y + step[(slot // 96) % 4]) % 4
    row_z = (z + step[(slot // 24) % 4]) % 4
    row_x = (x + step[(slot // 6) % 4]) % 4
    row_order = 6 * index_of(row_z, row_y, row_core, row_x) + slot % 6
    pa = (own_order[:, None] == row_order[None, :]).astype(BF)
    po = (slot[:, None] == row_order[None, :]).astype(BF)
    p2 = (slot[:, None] == own_order[None, :]).astype(BF)

    def mine_and_other(values):
        mine = lax.dynamic_index_in_dim(values[:, 0], high, 0, keepdims=False)
        return mine, lax.dynamic_index_in_dim(values[:, 0], 1 - high, 0, keepdims=False)

    def in_own_order(mine, came):
        return dot(jnp.concatenate([mine, came], 0), p2)

    mine, other = mine_and_other(inputs)
    other = fetch(other, "y", 2)
    hidden = in_own_order(mine, other)
    around, beside = weights_around(
        place, norm_params, attn_in, attn_out, mlp_in, mlp_out, [other]
    )
    grad_mine, grad_other = mine_and_other(cotangent)
    a_around, *bc_around = around[0]
    a_near, a_far = swap(a_around, "y", 1), swap(a_around, "y", -1)
    a_near, a_far = after([a_near, a_far], [pa, po, p2, hidden] + beside)
    bc_pair = join(bc_around, swaps(bc_around, "xz", 1), [a_near] + around[1])
    (a_last,) = after([swap(a_near, "y", -1)], bc_pair)
    a_weights = [weights_of([a_around, a_near, a_far, a_last])]
    bc_far = swaps(bc_pair, "xz", -1)
    weights = [None, None]
    records = []
    for layer in range(2):
        a1p_keep, a1p_send, gains, *pieces = run_kernel(
            qkv_kernel,
            [place, hidden, pa] + a_weights[layer],
            [shaped(TOKENS, 384), shaped(TOKENS, 384), shaped(8, D, dtype=F32)]
            + [shaped(576, TOKENS)] * 4,
            (
                pltpu.VMEM((D, 3 * D), BF),
                pltpu.VMEM((D, 128), BF),
                pltpu.VMEM((3 * D, TOKENS), BF),
                pltpu.SemaphoreType.DMA((16,)),
            ),
            flops=4 * UNIT,
            any_count=8,
        )
        blocks = order(place, bc_pair, bc_far, "xz", done=[a1p_keep])
        turned = exchange_four(pieces)
        blocks = behind(blocks, turned[1:])
        cores = [with_core(v) for v in blocks]
        weights[layer] = a_weights[layer] + [blocks[0], cores[0], blocks[1], cores[1]]
        if layer == 0:
            held = behind(around[1], turned[1:])
            first = swaps(held, LAST, 1)
        else:
            (grad_other,) = after([grad_other], turned[1:])
            grad_other = fetch(grad_other, "y", 2)
        *mixed, sums = run_kernel(
            attend_kernel,
            [place] + turned,
            [shaped(GROUP, TOKENS)] * 4 + [shaped(3, 1024, dtype=F32)],
            flops=ATTEND,
        )
        if layer == 0:
            mixed = behind(mixed, first)
        mixed = behind(mixed, cores)
        back = exchange_four(mixed)
        if layer == 0:
            bc_pair = behind(join(held[1:], first[1:]), back[1:])
            a_own, a_near = after([held[0], first[0]], back[1:])
            a_far, a_last = swap(a_own, "y", -1), swap(a_near, "y", -1)
            bc_far = swaps(bc_pair, "xz", -1)
        inputs = [place, hidden] + back + [a1p_send, po, p2, gains]
        whole, wide_rows = shaped(TOKENS, D, dtype=F32), shaped(TOKENS, FF)
        if layer == 0:
            h1, following, slope, forward_send, op_keep, act_keep = run_kernel(
                mlp_kernel,
                inputs + weights[layer],
                [whole, whole, wide_rows, wide_rows, shaped(TOKENS, 384), shaped(TOKENS, 1536)],
                MLP_SCRATCH,
                flops=11 * UNIT,
                any_count=12,
            )
            a_far, a_last = after([a_far, a_last], [following])
            forward0 = forward_send, with_core(forward_send)
            a_weights.append(weights_of([a_own, a_near, a_far, a_last]))
        else:
            grad = in_own_order(grad_mine, grad_other)
            following, forward_send, op_keep, act_keep, g1, back_send, dpre_keep, norm2, *pieces = (
                run_kernel(
                    mlp_turn_kernel,
                    inputs + [grad] + weights[layer],
                    [whole, wide_rows, shaped(TOKENS, 384), shaped(TOKENS, 1536)]
                    + [whole, wide_rows, shaped(TOKENS, 1536), shaped(8, D, dtype=F32)]
                    + [shaped(GROUP, TOKENS)] * 4,
                    MLP_SCRATCH + (pltpu.VMEM((TOKENS, FF), BF),),
                    flops=22 * UNIT,
                    any_count=12,
                    done=[forward0[1]],
                )
            )
        records.append(
            (hidden, a1p_keep, gains, turned, mixed, sums, forward_send, op_keep, act_keep)
        )
        hidden = following

    def leave(values, ahead, dtype):
        values = jnp.dot(
            values, p2.astype(F32).T, precision=lax.Precision.HIGHEST, preferred_element_type=F32
        )
        (far,) = after([values[128:].astype(dtype)], list(ahead))
        return values[:128], fetch(far, "y", 2)

    def arrange(own, came):
        return jnp.stack(
            [jnp.where(high == 0, own, came), jnp.where(high == 0, came, own)]
        )[:, None]

    def mlp_gradients(forward, back, act_keep, dpre_keep):
        return run_kernel(
            mlp_grad_kernel,
            [
                place,
                (forward[0], 768, 1),
                (forward[1], 768, 1),
                act_keep,
                (forward[1], 1536, 1),
                dpre_keep,
                (back[1], 1536, 0),
                (back[0], 768, 2),
                (back[1], 768, 2),
            ],
            [shaped(2, 192, 1536)] * 2 + [shaped(2, 768, 384)] * 2,
            flops=8 * UNIT,
        )

    def attend_back(layer, grad_mixed, done):
        turned, mixed, sums = records[layer][3:6]
        return run_kernel(
            attend_back_kernel,
            [place] + turned + grad_mixed + mixed + [sums],
            [shaped(576, TOKENS)] * 4,
            flops=3 * ATTEND,
            done=done,
        )

    def qkv_back(layer, grad_pieces, g1, norm2, done):
        hidden, gains = records[layer][0], records[layer][2]
        return run_kernel(
            qkv_back_kernel,
            [place] + grad_pieces + [hidden, g1, gains, pa, norm2] + a_weights[layer],
            [shaped(TOKENS, D, dtype=F32), shaped(3 * D + 48, TOKENS)],
            (pltpu.VMEM((D, 3 * D), BF), pltpu.SemaphoreType.DMA((8,))),
            flops=5 * UNIT,
            any_count=8,
            done=done,
        )

    def attn_gradients(forward, back, a1p_keep, op_keep, dqkv, done=()):
        return run_kernel(
            attn_grad_kernel,
            [
                place,
                a1p_keep,
                (forward[1], 384, 0),
                op_keep,
                (forward[1], 384, 1),
                (back[0], 768, 3),
                (back[1], 768, 3),
                dqkv[0],
                dqkv[1],
                pa,
            ],
            [shaped(96, ROW_A)] * 4,
            flops=4 * UNIT,
            done=done,
        )

    forward_send, op_keep, act_keep = records[1][6:]
    a1p_keep = records[1][1]
    forward = forward_send, with_core(forward_send)
    grad_mixed = exchange_four(pieces)
    back = back_send, with_core(back_send)
    b1_mine, b1_send, c1_mine, c1_send = mlp_gradients(forward, back, act_keep, dpre_keep)
    b1_send, c1_send = after([b1_send, c1_send], grad_mixed[1:])
    b1_came, c1_came = swap(b1_send, "x", -1), swap(c1_send, "z", -1)
    outputs = leave(hidden, grad_mixed[1:], F32)
    pieces = attend_back(1, grad_mixed, [b1_mine])
    pieces = after(pieces, [outputs[1], b1_came, c1_came])
    grad_pieces = exchange_four(pieces)
    (b1_keep, c1_keep), (b1_send, c1_send) = halved([b1_mine, c1_mine], [b1_came, c1_came])
    dqkv, g1, back_send0, dpre_keep0, norm2, *pieces = run_kernel(
        qkv_back_into_mlp_kernel,
        [place] + grad_pieces + [records[1][0], g1, records[1][2], pa, norm2]
        + [slope, h1, records[0][2], p2, po] + a_weights[1] + weights[0],
        [shaped(3 * D + 48, TOKENS), whole, wide_rows]
        + [shaped(TOKENS, 1536), shaped(8, D, dtype=F32)]
        + [shaped(GROUP, TOKENS)] * 4,
        MLP_SCRATCH + (pltpu.VMEM((D, 3 * D), BF), pltpu.SemaphoreType.DMA((8,))),
        flops=16 * UNIT,
        any_count=20,
        done=[b1_keep],
    )
    dqkv = dqkv, with_core(dqkv)

    _, op_keep0, act_keep0 = records[0][6:]
    a1p_keep0 = records[0][1]
    grad_mixed = exchange_four(pieces)
    a1_own, a1_near, a1_far, a1_last = attn_gradients(forward, back, a1p_keep, op_keep, dqkv)
    a1_far, a1_last, b1_send, c1_send = after(
        [a1_far, a1_last, b1_send, c1_send], grad_mixed[1:]
    )
    a1_far, a1_last = swap(a1_far, "y", -1), swap(a1_last, "y", -1)
    b1_came, c1_came = swap(b1_send, "x", 1), swap(c1_send, "z", 1)
    pieces = attend_back(0, grad_mixed, [a1_own])
    pieces = after(pieces, [a1_far, a1_last, b1_came, c1_came])
    dpre_keep0, back_send0 = after([dpre_keep0, back_send0], pieces[:1])
    back0 = back_send0, with_core(back_send0)
    grad_pieces = exchange_four(pieces)
    b0_mine, b0_send, c0_mine, c0_send = mlp_gradients(forward0, back0, act_keep0, dpre_keep0)
    a1_near = summed(a1_near, a1_last, [b0_mine])
    a1_near, b0_send, c0_send = after([a1_near, b0_send, c0_send], grad_pieces[1:])
    a1_came = swap(a1_near, "y", 1)
    b0_came, c0_came = swap(b0_send, "x", -1), swap(c0_send, "z", -1)
    grad, dqkv = qkv_back(0, grad_pieces, g1, norm2, [b0_mine, a1_near])
    grad, dqkv = after([grad, dqkv], [a1_came])
    dqkv = dqkv, with_core(dqkv)
    grad_own, grad_far = leave(grad, [], BF)
    a0_own, a0_near, a0_far, a0_last = attn_gradients(
        forward0, back0, a1p_keep0, op_keep0, dqkv
    )
    (a0_last,) = after([a0_last], [grad_far])
    a0_last = swap(a0_last, "y", -1)
    a0_near = summed(a0_near, a0_last)
    (a0_far,) = after([a0_far], [a0_near])
    a0_came, a0_far = swap(a0_near, "y", 1), swap(a0_far, "y", -1)
    (b0_keep, c0_keep), (b0_send, c0_send) = halved(
        [b0_mine, c0_mine], [b0_came, c0_came], [a0_near]
    )
    b0_came, c0_came = swap(b0_send, "x", 1), swap(c0_send, "z", 1)
    weight_grads = gradients_home(
        place,
        [total(a0_own, a0_far, a0_came), total(a1_own, a1_far, a1_came)],
        [[b0_keep, b0_came], [b1_keep, b1_came]],
        [[c0_keep, c0_came], [c1_keep, c1_came]],
    )
    grad_inputs = grad_own, grad_far.astype(F32)
    return (arrange(*outputs), arrange(*grad_inputs)) + weight_grads


def solution(mesh):
    in_specs = (
        P(None, "wide", "narrow", None),
        P(None, "wide"),
        P(None, None, ("wide", "narrow")),
        P(None, ("wide", "narrow"), None),
        P(None, ("wide", "narrow"), None),
        P(None, "narrow", "wide"),
        P(None, "wide", "narrow"),
        P(None, "wide", "narrow", None),
    )
    out_specs = (
        P(None, "wide", "narrow", None),
        P(None, "wide", "narrow", None),
        P(None, None, ("wide", "narrow")),
        P(None, ("wide", "narrow"), None),
        P(None, ("wide", "narrow"), None),
        P(None, "narrow", "wide"),
        P(None, "wide", "narrow"),
    )
    return jax.shard_map(body, mesh=mesh, in_specs=in_specs, out_specs=out_specs, check_vma=False)
```
